32 devices in a mesh: lat: 16 (over z, y, core), lon: 2 (over x).
Axes of the slice: x: 2, y: 2, z: 4, core: 2. Of those that a mesh axis runs over, the one named last changes fastest.
Arguments:
- inputs: bfloat16 [1024, 128, 128], P('lat', 'lon'), may hold values from -6 to 6
- w_first: bfloat16 [221184], P(('lat', 'lon')), may hold values from -0.1875 to 0.1875
- w_second: bfloat16 [331776], P(('lat', 'lon')), may hold values from -0.15625 to 0.15625
- w_third: bfloat16 [331776], P(('lat', 'lon')), may hold values from -0.15625 to 0.15625
- cotangent: bfloat16 [512, 64, 192], P('lat', 'lon'), may hold values from -6 to 6
Outputs:
- features: bfloat16 [512, 64, 192], P('lat', 'lon')
- grad_input: bfloat16 [1024, 128, 128], P('lat', 'lon')
- grad_first: float32 [221184], P(('lat', 'lon'))
- grad_second: float32 [331776], P(('lat', 'lon'))
- grad_third: float32 [331776], P(('lat', 'lon'))
The draws below stay inside these ranges and needn't reach their ends.
All inputs are finite; a program needn't handle non-finite values.
Results may differ from the reference program's by a relative error of at most 0.011.
Values may be sent and summed in bfloat16 or wider, within the bound.
No kernel may reach another device: no remote copies, remote signals or barrier semaphores. Data moves between devices by JAX's collectives and lax.ppermute only.
A program may use at most 64 MiB of HBM per device.

```python
import jax
import jax.numpy as jnp
from jax import lax

C0 = 128
C1 = 192
H = 1024
W = 128
LOSS_CELLS = 1024
WS1 = 221184
WS2 = 331776


def steps_of(rng, dims, cuts, least, largest):
    factor_of = 1.0
    for axis_at, blocks in cuts:
        heights = jax.random.uniform(jax.random.fold_in(jax.random.fold_in(rng, 6), axis_at), (blocks,), jnp.float32, least / len(cuts), largest / len(cuts))
        factor_of = factor_of * jnp.repeat(jnp.exp(heights), dims[axis_at] // blocks).reshape((-1,) + (1,) * (len(dims) - 1 - axis_at))
    return factor_of


def noise(own_key, shape, width, most, shards=(), dtype=jnp.bfloat16):
    array = width * jax.random.normal(own_key, shape, jnp.float32)
    if shards:
        array = array * steps_of(own_key, shape, shards, -0.22, 0.18)
    return jnp.clip(array, -most, most).astype(dtype)


def setup_inputs(seed: int = 0) -> dict:
    seeds = jax.random.split(jax.random.key(seed), 6)
    return {
        "inputs": noise(seeds[0], (H, W, C0), 1.0, 6.0, ((0, 16), (1, 2))),
        "w_first": noise(seeds[1], (WS1,), (9 * C0) ** -0.5, 0.1875, ((0, 32),)),
        "w_second": noise(seeds[2], (WS2,), (9 * C1) ** -0.5, 0.15625, ((0, 32),)),
        "w_third": noise(seeds[3], (WS2,), (9 * C1) ** -0.5, 0.15625, ((0, 32),)),
        "cotangent": noise(seeds[4], (H // 2, W // 2, C1), 1.0, 6.0, ((0, 16), (1, 2))),
    }


LAYOUT = ('NHWC', 'HWIO', 'NHWC')

def convolve(values, kernel, stride, padding, dilation):
    result = lax.conv_general_dilated(values[None].astype(jnp.float32), kernel.astype(jnp.float32), (stride, stride), padding, lhs_dilation=(dilation, dilation), dimension_numbers=LAYOUT, precision=lax.Precision.HIGHEST)
    return result[0]

def surround(values):
    wrapped = jnp.concatenate([values[:, -1:], values, values[:, :1]], axis=1)
    return jnp.pad(wrapped, ((1, 1), (0, 0), (0, 0)))

def flipped(kernel):
    return jnp.transpose(kernel[::-1, ::-1], (0, 1, 3, 2))

def derivative(preact):
    logistic = jax.nn.sigmoid(preact)
    return logistic * (1.0 + preact * (1.0 - logistic))

def kernel_grad(padded, deltas, stride):
    row_count, col_count = (deltas.shape[0], deltas.shape[1])
    tap_terms = []
    for row_tap in range(3):
        for col_tap in range(3):
            window = padded[row_tap:row_tap + stride * (row_count - 1) + 1:stride, col_tap:col_tap + stride * (col_count - 1) + 1:stride]
            tap_terms.append(jnp.einsum('hwc,hwo->co', window.astype(jnp.float32), deltas.astype(jnp.float32), precision=lax.Precision.HIGHEST))
    return jnp.stack(tap_terms).reshape(-1) / LOSS_CELLS

def reference(inputs, w_first, w_second, w_third, cotangent):
    kernel_one = w_first.reshape(3, 3, C0, C1)
    kernel_two = w_second.reshape(3, 3, C1, C1)
    kernel_three = w_third.reshape(3, 3, C1, C1)
    flat_pad = ((0, 0), (0, 0))
    padded_in = jnp.pad(jnp.concatenate([inputs[:, -1:], inputs], axis=1), ((1, 0), (0, 0), (0, 0)))
    h_one = convolve(padded_in, kernel_one, 2, flat_pad, 1).astype(jnp.bfloat16)
    padded_one = surround(h_one)
    pre_two = convolve(padded_one, kernel_two, 1, flat_pad, 1)
    h_two = jax.nn.silu(pre_two).astype(jnp.bfloat16)
    padded_two = surround(h_two)
    pre_three = convolve(padded_two, kernel_three, 1, flat_pad, 1)
    features = jax.nn.silu(pre_three).astype(jnp.bfloat16)
    delta_three = (cotangent.astype(jnp.float32) * derivative(pre_three)).astype(jnp.bfloat16)
    grad_third = kernel_grad(padded_two, delta_three, 1)
    back_two = convolve(surround(delta_three), flipped(kernel_three), 1, flat_pad, 1)
    delta_two = (back_two * derivative(pre_two)).astype(jnp.bfloat16)
    grad_second = kernel_grad(padded_one, delta_two, 1)
    back_one = convolve(surround(delta_two), flipped(kernel_two), 1, flat_pad, 1).astype(jnp.bfloat16)
    grad_first = kernel_grad(padded_in, back_one, 2)
    extended = jnp.concatenate([back_one, back_one[:, :1]], axis=1)
    extended = jnp.pad(extended, ((0, 1), (0, 0), (0, 0)))
    grad_input = convolve(extended, flipped(kernel_one), 1, ((1, 0), (1, 0)), 2).astype(jnp.bfloat16)
    return (features, grad_input, grad_first, grad_second, grad_third)
```

```python
import jax
import jax.numpy as jnp
from jax import lax
from jax.sharding import PartitionSpec as P

LOSS_CELLS = 1024
LAYOUT = ("NHWC", "HWIO", "NHWC")
BOTH = ("lat", "lon")
F32 = jnp.float32
BF16 = jnp.bfloat16


class Slice:
    def __init__(self):
        lat, lon = lax.axis_size("lat"), lax.axis_size("lon")
        core = 2 if lat % 2 == 0 else 1
        near = 2 if (lat // core) % 2 == 0 else 1
        self.sizes = (lat // core // near, near, core, lon)
        self.count = lat * lon

    def coords(self, index):
        out = []
        for size in reversed(self.sizes):
            out.append(index % size)
            index = index // size
        return tuple(reversed(out))

    def index(self, coords):
        total = 0
        for at, size in zip(coords, self.sizes):
            total = total * size + at
        return total

    def moved(self, coords, steps, sign=1):
        return tuple((at + sign * by) % size for at, by, size in zip(coords, steps, self.sizes))

    def send(self, value, steps):
        pairs = []
        for source in range(self.count):
            pairs.append((source, self.index(self.moved(self.coords(source), steps))))
        return lax.ppermute(value, BOTH, pairs)


def gathered(devices, shard):
    far, near, core, lon = devices.sizes
    line = jnp.stack([shard] + [devices.send(shard, (f, 0, 0, 0)) for f in range(1, far)])
    plane = []
    for n in range(near):
        for o in range(lon):
            plane.append(line if n == o == 0 else devices.send(line, (0, n, 0, o)))
    plane = jnp.stack(plane)
    both = [plane] + [devices.send(plane, (0, 0, c, 0)) for c in range(1, core)]
    return jnp.stack(both)


def summed(devices, chunks):
    far, near, core, lon = devices.sizes

    def add(terms):
        total = terms[0].astype(F32)
        for term in terms[1:]:
            total = total + term.astype(F32)
        return total

    half = add([chunks[0]] + [devices.send(chunks[c], (0, 0, c, 0)) for c in range(1, core)])
    half = half.astype(BF16)
    terms = []
    for n in range(near):
        for o in range(lon):
            part = half[n * lon + o]
            terms.append(part if n == o == 0 else devices.send(part, (0, n, 0, o)))
    line = add(terms).astype(BF16)
    return add([line[0]] + [devices.send(line[f], (f, 0, 0, 0)) for f in range(1, far)])


def order(devices, sign):
    far, near, core, lon = devices.sizes
    me = lax.axis_index("lat") * lon + lax.axis_index("lon")
    mine = devices.coords(me)
    places = []
    for c in range(core):
        for n in range(near):
            for o in range(lon):
                for f in range(far):
                    places.append(devices.index(devices.moved(mine, (f, n, c, o), sign)))
    return jnp.stack(places)


def widened(block, low, high):
    count = lax.axis_size("lon")
    east = [(i, (i + 1) % count) for i in range(count)]
    west = [(i, (i - 1) % count) for i in range(count)]
    before = lax.ppermute(block[:, -low:], "lon", east)
    after = lax.ppermute(block[:, :high], "lon", west)
    block = jnp.concatenate([before, block, after], axis=1)
    count = lax.axis_size("lat")
    south = [(i, i + 1) for i in range(count - 1)]
    north = [(i + 1, i) for i in range(count - 1)]
    before = lax.ppermute(block[-low:], "lat", south)
    after = lax.ppermute(block[:high], "lat", north)
    return jnp.concatenate([before, block, after], axis=0)


def convolve(values, kernel, stride=1):
    return lax.conv_general_dilated(
        values[None],
        kernel,
        (stride, stride),
        ((0, 0), (0, 0)),
        dimension_numbers=LAYOUT,
        preferred_element_type=F32,
    )[0]


def flipped(kernel):
    return jnp.transpose(kernel[::-1, ::-1], (0, 1, 3, 2))


def derivative(preact):
    logistic = jax.nn.sigmoid(preact)
    return logistic * (1.0 + preact * (1.0 - logistic))


def inner(block, rows, cols, low):
    return block[low : low + rows, low : low + cols]


def kernel_grad(windows, deltas, factor):
    cells = deltas.shape[0] * deltas.shape[1]
    columns = jnp.concatenate(windows, axis=2).reshape(cells, -1)
    product = lax.dot_general(
        columns,
        deltas.reshape(cells, -1),
        (((0,), (0,)), ((), ())),
        preferred_element_type=F32,
    )
    return (product * factor).astype(BF16).reshape(-1)


def tap_term(values, kernel, row_tap, col_tap):
    return lax.dot_general(
        values,
        kernel[row_tap, col_tap],
        (((2,), (1,)), ((), ())),
        preferred_element_type=F32,
    )


def phase_spread(source, kernel, row_count, col_count):
    here = source[:row_count, :col_count]
    right = source[:row_count, 1 : col_count + 1]
    below = source[1 : row_count + 1, :col_count]
    corner = source[1 : row_count + 1, 1 : col_count + 1]
    even_even = tap_term(here, kernel, 1, 1)
    even_odd = tap_term(right, kernel, 1, 0) + tap_term(here, kernel, 1, 2)
    odd_even = tap_term(below, kernel, 0, 1) + tap_term(here, kernel, 2, 1)
    odd_odd = (
        tap_term(corner, kernel, 0, 0)
        + tap_term(below, kernel, 0, 2)
        + tap_term(right, kernel, 2, 0)
        + tap_term(here, kernel, 2, 2)
    )
    chans = even_even.shape[2]
    even_rows = jnp.stack([even_even, even_odd], axis=2).reshape(row_count, 2 * col_count, chans)
    odd_rows = jnp.stack([odd_even, odd_odd], axis=2).reshape(row_count, 2 * col_count, chans)
    return jnp.stack([even_rows, odd_rows], axis=1).reshape(2 * row_count, 2 * col_count, chans)


def local(inputs, w_first, w_second, w_third, cotangent):
    devices = Slice()
    rows, cols, mid = cotangent.shape
    chan_in = inputs.shape[2]
    factor = 1.0 / LOSS_CELLS
    shard = jnp.concatenate([w_first, w_second, w_third])
    sizes = (w_first.shape[0], w_second.shape[0], w_third.shape[0])
    chunks = gathered(devices, shard.reshape(-1, 128))
    chunks = chunks.reshape(devices.count, -1)
    places = jnp.argsort(order(devices, -1))
    chunks = jnp.take(chunks, places, axis=0)
    one, two, three = jnp.split(chunks, (sizes[0], sizes[0] + sizes[1]), axis=1)
    kernel_one = one.reshape(3, 3, chan_in, mid)
    kernel_two = two.reshape(3, 3, mid, mid)
    kernel_three = three.reshape(3, 3, mid, mid)

    wide_in = widened(inputs, 9, 10)
    wide_cot = widened(cotangent, 2, 3)
    first_row = lax.axis_index("lat") * rows
    all_rows = lax.axis_size("lat") * rows

    def masked(block, low):
        row = lax.broadcasted_iota(jnp.int32, (block.shape[0], 1, 1), 0) - low + first_row
        return jnp.where((row >= 0) & (row < all_rows), block, 0)

    h_one = masked(convolve(wide_in, kernel_one, 2), 4).astype(BF16)
    pre_two = convolve(h_one, kernel_two)
    h_two = masked(jax.nn.silu(pre_two), 3).astype(BF16)
    pre_three = convolve(h_two, kernel_three)
    features = jax.nn.silu(inner(pre_three, rows, cols, 2)).astype(BF16)
    delta_three = (wide_cot.astype(F32) * derivative(pre_three)).astype(BF16)

    def windows(block, low):
        return [
            block[low - 1 + a : low - 1 + a + rows, low - 1 + b : low - 1 + b + cols]
            for a in range(3)
            for b in range(3)
        ]

    term_three = kernel_grad(windows(h_two, 3), inner(delta_three, rows, cols, 2), factor)
    back_two = convolve(delta_three, flipped(kernel_three))
    slope = derivative(pre_two[2:-2, 2:-2])
    delta_two = masked(back_two * slope, 1).astype(BF16)
    term_two = kernel_grad(windows(h_one, 4), inner(delta_two, rows, cols, 1), factor)
    back_one = masked(convolve(delta_two, flipped(kernel_two)), 0).astype(BF16)
    near_in = wide_in[7:, 7:][: 2 * rows + 4, : 2 * cols + 4]
    phases = near_in.reshape(rows + 2, 2, cols + 2, 2, chan_in)
    taps = []
    for a in range(3):
        for b in range(3):
            r, c = a + 1, b + 1
            taps.append(phases[r // 2 : r // 2 + rows, r % 2, c // 2 : c // 2 + cols, c % 2])
    term_one = kernel_grad(taps, inner(back_one, rows, cols, 0), factor)
    terms = jnp.concatenate(
        [t.reshape(devices.count, -1) for t in (term_one, term_two, term_three)], axis=1
    )
    terms = jnp.take(terms, order(devices, 1), axis=0)
    far, near, core, lon = devices.sizes
    terms = terms.reshape(core, near * lon, far, -1, 128)
    total = summed(devices, terms).reshape(-1)
    grad_first, grad_second, grad_third = jnp.split(total, (sizes[0], sizes[0] + sizes[1]))
    grad_input = phase_spread(back_one, kernel_one, rows, cols).astype(BF16)
    return (features, grad_input, grad_first, grad_second, grad_third)


def solution(mesh):
    tile = P("lat", "lon", None)
    flat = P(("lat", "lon"))
    return jax.shard_map(
        local,
        mesh=mesh,
        in_specs=(tile, flat, flat, flat, tile),
        out_specs=(tile, tile, flat, flat, flat),
        check_vma=False,
    )
```

```python
import functools

import jax
import jax.numpy as jnp
from jax import lax
from jax.experimental import pallas as pl
from jax.experimental.pallas import tpu as pltpu
from jax.sharding import PartitionSpec as P

LOSS_CELLS = 1024
BOTH = ("lat", "lon")
F32 = jnp.float32
BF16 = jnp.bfloat16


class Slice:
    def __init__(self):
        lat, lon = lax.axis_size("lat"), lax.axis_size("lon")
        core = 2 if lat % 2 == 0 else 1
        near = 2 if (lat // core) % 2 == 0 else 1
        self.sizes = (lat // core // near, near, core, lon)
        self.count = lat * lon

    def coords(self, index):
        out = []
        for size in reversed(self.sizes):
            if isinstance(index, int):
                out.append(index % size)
                index = index // size
            else:
                out.append(lax.rem(index, size))
                index = lax.div(index, size)
        return tuple(reversed(out))

    def index(self, coords):
        total = 0
        for at, size in zip(coords, self.sizes):
            total = total * size + at
        return total

    def moved(self, coords, steps, sign=1):
        out = []
        for at, by, size in zip(coords, steps, self.sizes):
            to = at + sign * by + size
            out.append(to % size if isinstance(to, int) else lax.rem(to, size))
        return tuple(out)

    def send(self, value, steps):
        pairs = []
        for source in range(self.count):
            pairs.append((source, self.index(self.moved(self.coords(source), steps))))
        return lax.ppermute(value, BOTH, pairs)


def gathered(devices, shard):
    far, near, core, lon = devices.sizes
    line = jnp.stack([shard] + [devices.send(shard, (f, 0, 0, 0)) for f in range(1, far)])
    planes, parts = [], []
    for c in range(core):
        for n in range(near):
            for o in range(lon):
                if c:
                    plane = devices.send(planes[n * lon + o], (0, 0, c, 0))
                else:
                    plane = line if n == o == 0 else devices.send(line, (0, n, 0, o))
                planes.append(plane)
                parts.append((c, n, o))
    return planes, parts


def summed(devices, chunks):
    far, near, core, lon = devices.sizes

    def add(terms):
        total = terms[0].astype(F32)
        for term in terms[1:]:
            total = total + term.astype(F32)
        return total

    half = add([chunks[0]] + [devices.send(chunks[c], (0, 0, c, 0)) for c in range(1, core)])
    half = half.astype(BF16)
    terms = []
    for n in range(near):
        for o in range(lon):
            part = half[n * lon + o]
            terms.append(part if n == o == 0 else devices.send(part, (0, n, 0, o)))
    line = add(terms).astype(BF16)
    return add([line[0]] + [devices.send(line[f], (f, 0, 0, 0)) for f in range(1, far)])


def order(devices, sign):
    far, near, core, lon = devices.sizes
    me = lax.axis_index("lat") * lon + lax.axis_index("lon")
    mine = devices.coords(me)
    places = []
    for c in range(core):
        for n in range(near):
            for o in range(lon):
                for f in range(far):
                    places.append(devices.index(devices.moved(mine, (f, n, c, o), sign)))
    return jnp.stack(places)


def widened(block, low, high):
    count = lax.axis_size("lon")
    east = [(i, (i + 1) % count) for i in range(count)]
    west = [(i, (i - 1) % count) for i in range(count)]
    before = lax.ppermute(block[:, -low:], "lon", east)
    after = lax.ppermute(block[:, :high], "lon", west)
    block = jnp.concatenate([before, block, after], axis=1)
    count = lax.axis_size("lat")
    south = [(i, i + 1) for i in range(count - 1)]
    north = [(i + 1, i) for i in range(count - 1)]
    before = lax.ppermute(block[-low:], "lat", south)
    after = lax.ppermute(block[:high], "lat", north)
    return jnp.concatenate([before, block, after], axis=0)


LEFT = 16
ABOVE = 5
BELOW = 7
GUARD = 8
HALF = 64

FRINGE = (((0, 0, 0),), ((0, 1, 0),), ((0, 2, 0),), ((0, 0, 1), (0, 1, 1)), ((0, 2, 1), (1, 2, 1)))
MIDDLE = (((1, 0, 0),), ((1, 1, 0),), ((1, 2, 0),), ((1, 0, 1), (1, 1, 1)))
LAST = (((2, 0, 0),), ((2, 1, 0),), ((2, 2, 0),), ((2, 0, 1), (2, 1, 1)), ((2, 2, 1), None))
BLOCKS = FRINGE + MIDDLE + LAST


def low_lanes(rows):
    return lax.broadcasted_iota(jnp.int32, (rows, 128), 1) < HALF


def swapped(value):
    return pltpu.roll(value, HALF, 1)


def prepare(rows, cols, x_ref, c_ref, windows_ref, cot_ref, wide, cot_a, cot_b):
    pitch = cols + LEFT
    height = rows + ABOVE + BELOW
    span = wide.shape[0] // (2 * height + 4)
    wide[...] = jnp.zeros_like(wide)
    cot_a[...] = jnp.zeros_like(cot_a)
    cot_b[...] = jnp.zeros_like(cot_b)
    high, across = x_ref.shape[0], x_ref.shape[1]

    def spread(i, _):
        start = pl.multiple_of((i + 4) * span + 16, 8)
        wide[pl.ds(start, across), :] = x_ref[i].astype(F32)
        return 0

    lax.fori_loop(0, high, spread, 0)

    def window(k, _):
        for parity in range(2):
            row = 2 * (k - ABOVE) + 13 + parity
            for tap in range(3):
                base = row * span + 24 + tap
                mid = wide[pl.ds(base, cols, stride=2), :]
                before = wide[pl.ds(base - 16, 8, stride=2), :]
                after = wide[pl.ds(base - 2 * span + 2 * cols, 8, stride=2), :]
                lane = (3 * parity + tap) * 128
                cells = jnp.concatenate([after, before, mid], axis=0).astype(BF16)
                windows_ref[pl.ds(pl.multiple_of(k * pitch, 16), pitch), lane : lane + 128] = cells
        return 0

    lax.fori_loop(0, height, window, 0)
    for i in range(c_ref.shape[0]):
        value = c_ref[i].astype(F32)
        start = GUARD + (i - 2 + ABOVE) * pitch + LEFT - 2
        cot_a[start : start + value.shape[0], :] = value[:, :128]
        cot_b[start : start + value.shape[0], 0:HALF] = value[:, 128:]
    size = height * pitch
    cot_ref[:, :128] = cot_a[GUARD : GUARD + size, :].astype(BF16)
    part = cot_b[GUARD : GUARD + size, :]
    cot_ref[:, 128:] = jnp.where(low_lanes(size), part, swapped(part)).astype(BF16)


def level(
    shape,
    devices,
    parts,
    x_ref,
    c_ref,
    *refs,
):
    rows, cols, chan_in, mid, factor, whole = shape
    planes = refs[: len(parts)]
    (
        features_ref,
        input_ref,
        terms_ref,
        chunks,
        outgoing,
        in_sems,
        out_sems,
        flat,
        k_a,
        k_b,
        w_one,
        w_two,
        w_three,
        t_two,
        t_three,
        t_one,
        f_a,
        f_b,
        slope,
        win_one,
        win_two,
        win_delta,
        spread,
        image,
    ) = refs[len(parts) :]
    pitch = cols + LEFT
    height = rows + ABOVE + BELOW
    size = height * pitch
    far, near, core, lon = devices.sizes
    sections = ((0, chan_in), (1, mid), (2, mid))
    count = chunks.shape[0]
    share = [9 * c * mid // 128 // count for _, c in sections]
    begin = [0, share[0], share[0] + share[1]]

    lat_at = lax.axis_index("lat")
    mine = devices.coords(lat_at * lon + lax.axis_index("lon"))

    copies = []
    for place, (steps_at, plane) in enumerate(zip(parts, planes)):
        for f in range(plane.shape[0]):
            if whole:
                owner = 0
            else:
                c, n, o = steps_at
                owner = devices.index(devices.moved(mine, (f, n, c, o), -1))
            copy = pltpu.make_async_copy(
                plane.at[f], chunks.at[owner], in_sems.at[len(copies)]
            )
            copy.start()
            copies.append(copy)
    f_a[...] = jnp.zeros_like(f_a)
    f_b[...] = jnp.zeros_like(f_b)
    slope[...] = jnp.zeros_like(slope)
    for copy in copies:
        copy.wait()

    def unpack(which, channels):
        n = share[which]
        for k in range(count):
            flat[k * n : (k + 1) * n, :] = chunks[
                k, begin[which] // 16 * 16 : -(-(begin[which] + n) // 16) * 16, :
            ].astype(F32)[begin[which] % 16 : begin[which] % 16 + n]
        pairs = 9 * channels // 2
        step = 96

        def one(i, _):
            at = i * step
            first = flat[pl.ds(3 * at, step, stride=3), :]
            second = flat[pl.ds(3 * at + 1, step, stride=3), :]
            third = flat[pl.ds(3 * at + 2, step, stride=3), :]
            low = low_lanes(step)
            second_r, third_r = swapped(second), swapped(third)
            k_a[pl.ds(2 * at, step, stride=2), :] = first
            k_b[pl.ds(2 * at, step, stride=2), :] = jnp.where(low, second, second_r)
            k_a[pl.ds(2 * at + 1, step, stride=2), :] = jnp.where(low, second_r, third_r)
            k_b[pl.ds(2 * at + 1, step, stride=2), :] = jnp.where(low, third_r, third)
            return 0

        lax.fori_loop(0, pairs // step, one, 0)

    def tap_rows(tap, part):
        start = (3 * tap[0] + tap[1]) * mid + 128 * part
        return start, start + (HALF if part else 128)

    def forward(target):
        at = 0
        for block in BLOCKS:
            for tap in block:
                if tap is None:
                    target[at : at + HALF, :] = jnp.zeros((HALF, 256), BF16)
                    at += HALF
                    continue
                lo, hi = tap_rows(tap, tap[2])
                target[at : at + hi - lo, 0:128] = k_a[lo:hi, :].astype(BF16)
                target[at : at + hi - lo, 128:256] = k_b[lo:hi, :].astype(BF16)
                at += hi - lo

    def backward(target):
        low = low_lanes(mid)
        for i, block in enumerate(BLOCKS):
            values = []
            for tap in block:
                if tap is None:
                    values.append(jnp.zeros((mid, 128), F32))
                    continue
                lo = (3 * (2 - tap[0]) + 2 - tap[1]) * mid
                source = k_b if tap[2] else k_a
                values.append(source[lo : lo + mid, :])
            value = values[0] if len(values) == 1 else jnp.where(low, values[0], values[1])
            value = value.astype(BF16)
            target[0:mid, 128 * i : 128 * i + 128] = value
            target[mid:256, 128 * i : 128 * i + 128] = value[128:mid]

    unpack(0, chan_in)
    w_one[:, 0:128] = k_a[0 : 9 * chan_in, :].astype(BF16)
    w_one[:, 128:256] = k_b[0 : 9 * chan_in, :].astype(BF16)
    empty = jnp.zeros((chan_in, 128), F32)
    low_in = low_lanes(chan_in)
    phases = (
        ((1, 1), None, None, None),
        ((1, 2), (1, 0), None, None),
        ((2, 1), None, (0, 1), None),
        ((2, 2), (2, 0), (0, 2), (0, 0)),
    )
    for i, taps in enumerate(phases):
        a, b = [], []
        for tap in taps:
            if tap is None:
                a.append(empty)
                b.append(empty)
            else:
                lo = (3 * tap[0] + tap[1]) * chan_in
                a.append(k_a[lo : lo + chan_in, :])
                b.append(k_b[lo : lo + chan_in, :])
        blocks = (
            a[0],
            a[1],
            jnp.where(low_in, b[0], b[1]),
            a[2],
            a[3],
            jnp.where(low_in, b[2], b[3]),
        )
        for j, block in enumerate(blocks):
            t_one[chan_in * i : chan_in * (i + 1), 128 * j : 128 * j + 128] = block.astype(BF16)
    unpack(1, mid)
    forward(w_two)
    backward(t_two)
    unpack(2, mid)
    forward(w_three)
    backward(t_three)

    first_row = lat_at * rows
    bottom = lax.axis_size("lat") * rows - first_row
    low_cell = (jnp.maximum(-first_row, -ABOVE) + ABOVE) * pitch + 8
    high_cell = (jnp.minimum(bottom, rows + BELOW) + ABOVE) * pitch + 8

    def inside(start, n):
        cell = start + lax.broadcasted_iota(jnp.int32, (n, 128), 0)
        return (cell >= low_cell) & (cell < high_cell)

    def store(start, n, left, right, mask):
        if mask:
            keep = inside(start, n)
            left = jnp.where(keep, left, 0.0)
            right = jnp.where(keep, right, 0.0)
        at = pl.multiple_of(start + GUARD, 8)
        f_a[pl.ds(at, n), :] = left
        f_b[pl.ds(at, n), :] = right

    def windows(target, top, under):
        def one(i, _):
            cell = i * pitch
            q = cell + GUARD
            low = low_lanes(pitch)
            b_0, b_1, b_2 = (f_b[pl.ds(q + s, pitch), :] for s in (-1, 0, 1))
            b_3 = f_b[pl.ds(q + 1 + pitch, pitch), :]
            out = [f_a[pl.ds(q + s, pitch), :] for s in (-1, 0, 1)]
            out += [jnp.where(low, b_0, b_1), jnp.where(low, b_2, b_3)]
            at = pl.multiple_of(cell, 16)
            for j, value in enumerate(out):
                target[pl.ds(at, pitch), 128 * j : 128 * j + 128] = value.astype(BF16)
            return 0

        lax.fori_loop(top + ABOVE, under + ABOVE, one, 0)

    def convolve(source, weights, turned, halo, steps, finish):
        start = (ABOVE - halo) * pitch
        total = (rows + 1 + 2 * halo) * pitch + LEFT
        n = -(-total // steps // 16) * 16
        contract = (((1,), (1,)), ((), ())) if turned else (((1,), (0,)), ((), ()))

        def one(i, _):
            p = pl.multiple_of(start + i * n, 16)
            above = source[pl.ds(pl.multiple_of(p - pitch, 16), n), :]
            here = source[pl.ds(p, n), 0:512]
            below = source[pl.ds(pl.multiple_of(p + pitch, 16), n), :]
            value = lax.dot_general(
                jnp.concatenate([above, here, below], axis=1),
                weights[...],
                contract,
                preferred_element_type=F32,
            )
            finish(p, n, value)
            return 0

        lax.fori_loop(0, steps, one, 0)

    def own(ref, lanes, row_step=0, shift=0, offset=0):
        pieces = []
        for r in range(rows):
            at = offset + (ABOVE + r + row_step) * pitch + LEFT + shift
            pieces.append(ref[at : at + cols, lanes])
        return jnp.concatenate(pieces, axis=0)

    ALL = slice(0, 128)

    def turned_deltas():
        left = own(f_a, ALL, offset=GUARD)
        right = own(f_b, ALL, offset=GUARD)
        return jnp.concatenate([left.T, right.T], axis=0).astype(BF16)

    def pack(which, channels):
        step = 96

        def one(i, _):
            at = i * step
            even_a = k_a[pl.ds(2 * at, step, stride=2), :]
            even_b = k_b[pl.ds(2 * at, step, stride=2), :]
            odd_a = swapped(k_a[pl.ds(2 * at + 1, step, stride=2), :])
            odd_b = k_b[pl.ds(2 * at + 1, step, stride=2), :]
            low = low_lanes(step)
            flat[pl.ds(3 * at, step, stride=3), :] = even_a
            flat[pl.ds(3 * at + 1, step, stride=3), :] = jnp.where(low, even_b, odd_a)
            flat[pl.ds(3 * at + 2, step, stride=3), :] = jnp.where(low, odd_a, odd_b)
            return 0

        lax.fori_loop(0, 9 * channels // 2 // step, one, 0)
        n = share[which]
        for k in range(count):
            outgoing[k, begin[which] : begin[which] + n, :] = flat[k * n : (k + 1) * n, :]

    def field_grad(which, source):
        turned = turned_deltas()
        for a, blocks in enumerate((FRINGE, MIDDLE, LAST)):
            lanes = slice(0, 128 * len(blocks))
            product = lax.dot_general(
                turned,
                own(source, lanes, a - 1),
                (((1,), (0,)), ((), ())),
                preferred_element_type=F32,
            )
            product = product * factor
            for j, block in enumerate(blocks):
                left = product[0:128, 128 * j : 128 * j + 128].T
                right = product[128:256, 128 * j : 128 * j + 128].T
                at = 0
                for tap in block:
                    if tap is None:
                        continue
                    lo, hi = tap_rows(tap, tap[2])
                    k_a[lo:hi, :] = left[at : at + hi - lo]
                    k_b[lo:hi, :] = right[at : at + hi - lo]
                    at += hi - lo
        pack(which, mid)

    def convolve_first():
        halo, steps = 4, 4
        start = (ABOVE - halo) * pitch
        total = (rows + 1 + 2 * halo) * pitch + LEFT
        n = -(-total // steps // 16) * 16

        def one(i, _):
            p = pl.multiple_of(start + i * n, 16)
            above = x_ref[pl.ds(pl.multiple_of(p - pitch, 16), n), 384:768]
            here = x_ref[pl.ds(p, n), :]
            value = lax.dot_general(
                jnp.concatenate([above, here], axis=1),
                w_one[...],
                (((1,), (0,)), ((), ())),
                preferred_element_type=F32,
            )
            store(p, n, value[:, :128], value[:, 128:], True)
            return 0

        lax.fori_loop(0, steps, one, 0)

    convolve_first()
    windows(win_one, -4, rows + 6)

    def finish_two(p, n, value):
        s = jax.nn.sigmoid(value)
        active = value * s
        slope[pl.ds(p, n), :] = s + active * (1.0 - s)
        store(p, n, active[:, :128], active[:, 128:], True)

    convolve(win_one, w_two, False, 3, 4, finish_two)
    windows(win_two, -3, rows + 5)

    def finish_three(p, n, value):
        s = jax.nn.sigmoid(value)
        active = value * s
        delta = c_ref[pl.ds(p, n), :].astype(F32) * (s + active * (1.0 - s))
        store(p, n, delta[:, :128], delta[:, 128:], False)
        spread[pl.ds(p, n), :] = active

    convolve(win_two, w_three, False, 2, 4, finish_three)
    for r in range(rows):
        at = (ABOVE + r) * pitch + LEFT
        features_ref[r] = spread[at : at + cols, 0:mid].astype(BF16)
    field_grad(2, win_two)
    windows(win_delta, -2, rows + 4)

    def finish_delta(p, n, value):
        value = value * slope[pl.ds(p, n), :]
        store(p, n, value[:, :128], value[:, 128:], True)

    convolve(win_delta, t_three, True, 1, 4, finish_delta)
    field_grad(1, win_one)
    windows(win_delta, -1, rows + 3)

    def finish_back(p, n, value):
        store(p, n, value[:, :128], value[:, 128:], True)

    convolve(win_delta, t_two, True, 0, 4, finish_back)
    turned = turned_deltas()
    for a, (step, lanes) in enumerate(((-1, slice(384, 768)), (0, slice(0, 384)), (0, slice(384, 768)))):
        product = lax.dot_general(
            turned,
            own(x_ref, lanes, step),
            (((1,), (0,)), ((), ())),
            preferred_element_type=F32,
        )
        product = product * factor
        lo = 3 * a * chan_in
        k_a[lo : lo + 3 * chan_in, :] = product[0:128].T
        k_b[lo : lo + 3 * chan_in, :] = product[128:256].T
    pack(0, chan_in)

    sends = []
    for k in range(count):
        chunks[k] = outgoing[k].astype(BF16)
        place = 0
        if not whole:
            distance = tuple(
                lax.rem(to - at + by, by)
                for to, at, by in zip(devices.coords(k), mine, devices.sizes)
            )
            f, n, c, o = distance
            place = ((c * near + n) * lon + o) * far + f
        copy = pltpu.make_async_copy(chunks.at[k], terms_ref.at[place], out_sems.at[k])
        copy.start()
        sends.append(copy)

    low = low_lanes(rows * cols)

    def four(ref):
        return [own(ref, ALL, r, c, GUARD) for r, c in ((0, 0), (0, 1), (1, 0), (1, 1))]

    a, b = four(f_a), four(f_b)
    around = (a[0], a[1], jnp.where(low, b[0], b[1]), a[2], a[3], jnp.where(low, b[2], b[3]))
    around = jnp.concatenate([value.astype(BF16) for value in around], axis=1)
    for r in range(2):
        wide = 384 * (r + 1)
        product = lax.dot_general(
            around[:, :wide],
            t_one[2 * chan_in * r : 2 * chan_in * (r + 1), :wide],
            (((1,), (1,)), ((), ())),
            preferred_element_type=F32,
        )
        for i in range(rows):
            at = i * cols
            base = (2 * i + r) * 2 * cols
            for c in range(2):
                spread_in = product[at : at + cols, chan_in * c : chan_in * (c + 1)]
                image[pl.ds(base + c, cols, stride=2), :] = spread_in
    for i in range(2 * rows):
        input_ref[i] = image[2 * cols * i : 2 * cols * (i + 1), :].astype(BF16)
    for copy in sends:
        copy.wait()


VMEM = pl.BlockSpec(memory_space=pltpu.VMEM)
ANY = pl.BlockSpec(memory_space=pl.ANY)


def local(inputs, w_first, w_second, w_third, cotangent):
    devices = Slice()
    rows, cols, mid = cotangent.shape
    chan_in = inputs.shape[2]
    factor = 1.0 / LOSS_CELLS
    far, near, core, lon = devices.sizes
    held = (w_first.shape[0], w_second.shape[0], w_third.shape[0])
    shard = jnp.concatenate([w_first, w_second, w_third]).reshape(-1, 128)
    whole = any(n % 128 for n in held)
    if not whole:
        shard = jnp.pad(shard, ((0, -shard.shape[0] % 16), (0, 0)))
    planes, parts = gathered(devices, shard)
    if whole:
        chunks = jnp.stack(planes).reshape(devices.count, -1)
        chunks = jnp.take(chunks, jnp.argsort(order(devices, -1)), axis=0)
        pieces = jnp.split(chunks, (held[0], held[0] + held[1]), axis=1)
        chunks = jnp.concatenate([piece.reshape(-1) for piece in pieces])
        planes, parts = [chunks.reshape(1, -1, 128)], [(0, 0, 0)]
    count = 1 if whole else devices.count
    depth = planes[0].shape[1]

    wide_in = widened(inputs, 9, 10)
    wide_cot = widened(cotangent, 2, 3)
    size = (rows + ABOVE + BELOW) * (cols + LEFT)
    field = pltpu.VMEM((size + 2 * GUARD, 128), F32)
    tall = 2 * (rows + ABOVE + BELOW) + 4
    across = -(-(wide_in.shape[1] + 29) // 16) * 16
    padded, cot = pl.pallas_call(
        functools.partial(prepare, rows, cols),
        out_shape=(
            jax.ShapeDtypeStruct((size, 6 * chan_in), BF16),
            jax.ShapeDtypeStruct((size, 256), BF16),
        ),
        in_specs=[VMEM] * 2,
        out_specs=(VMEM, VMEM),
        scratch_shapes=[pltpu.VMEM((tall * across, 128), F32), field, field],
        compiler_params=pltpu.CompilerParams(vmem_limit_bytes=40 * 2**20),
        cost_estimate=pl.CostEstimate(flops=0, bytes_accessed=12 * 2**20, transcendentals=0),
    )(wide_in, wide_cot)

    cells = pltpu.VMEM((size, 640), BF16)
    shape = (rows, cols, chan_in, mid, factor, whole)
    features, grad_input, terms = pl.pallas_call(
        functools.partial(level, shape, devices, parts),
        out_shape=(
            jax.ShapeDtypeStruct((rows, cols, mid), BF16),
            jax.ShapeDtypeStruct((2 * rows, 2 * cols, chan_in), BF16),
            jax.ShapeDtypeStruct((count, depth, 128), BF16),
        ),
        in_specs=[VMEM] * 2 + [ANY] * len(planes),
        out_specs=(VMEM, VMEM, ANY),
        scratch_shapes=[
            pltpu.VMEM((count, depth, 128), BF16),
            pltpu.VMEM((count, depth, 128), F32),
            pltpu.SemaphoreType.DMA((count,)),
            pltpu.SemaphoreType.DMA((count,)),
            pltpu.VMEM((9 * mid * mid // 128, 128), F32),
            pltpu.VMEM((9 * mid, 128), F32),
            pltpu.VMEM((9 * mid, 128), F32),
            pltpu.VMEM((9 * chan_in, 256), BF16),
            pltpu.VMEM((128 * len(BLOCKS), 256), BF16),
            pltpu.VMEM((128 * len(BLOCKS), 256), BF16),
            pltpu.VMEM((256, 128 * len(BLOCKS)), BF16),
            pltpu.VMEM((256, 128 * len(BLOCKS)), BF16),
            pltpu.VMEM((4 * chan_in, 768), BF16),
            field,
            field,
            pltpu.VMEM((size, 256), F32),
            cells,
            cells,
            cells,
            pltpu.VMEM((size, 256), F32),
            pltpu.VMEM((4 * rows * cols, 128), F32),
        ],
        compiler_params=pltpu.CompilerParams(vmem_limit_bytes=60 * 2**20),
        cost_estimate=pl.CostEstimate(
            flops=6 * 10**9, bytes_accessed=16 * 2**20, transcendentals=10**6
        ),
    )(padded, cot, *planes)
    if whole:
        cuts = (held[0] * devices.count, (held[0] + held[1]) * devices.count)
        pieces = jnp.split(terms.reshape(-1), cuts)
        terms = [piece.reshape(devices.count, -1) for piece in pieces]
        terms = jnp.take(jnp.concatenate(terms, axis=1), order(devices, 1), axis=0)
    terms = terms.reshape(core, near * lon, far, -1, 128)
    total = summed(devices, terms).reshape(-1)[: sum(held)]
    grad_first, grad_second, grad_third = jnp.split(total, (held[0], held[0] + held[1]))
    return (features, grad_input, grad_first, grad_second, grad_third)


def solution(mesh):
    tile = P("lat", "lon", None)
    flat = P(("lat", "lon"))
    return jax.shard_map(
        local,
        mesh=mesh,
        in_specs=(tile, flat, flat, flat, tile),
        out_specs=(tile, tile, flat, flat, flat),
        check_vma=False,
    )
```

```python
import functools

import jax
import jax.numpy as jnp
from jax import lax
from jax.experimental import pallas as pl
from jax.experimental.pallas import tpu as pltpu
from jax.sharding import PartitionSpec as P

LOSS_CELLS = 1024
LAT = ("chip", "core")
BOTH = ("chip", "core", "lon")
F32 = jnp.float32
BF16 = jnp.bfloat16


class Slice:
    def __init__(self):
        chip, core, lon = (lax.axis_size(axis) for axis in BOTH)
        near = 2 if chip % 2 == 0 else 1
        self.sizes = (chip // near, near, core, lon)
        self.count = chip * core * lon

    def place(self):
        lat = lax.axis_index("chip") * self.sizes[2] + lax.axis_index("core")
        return lat, self.coords(lat * self.sizes[3] + lax.axis_index("lon"))

    def coords(self, index):
        out = []
        for size in reversed(self.sizes):
            if isinstance(index, int):
                out.append(index % size)
                index = index // size
            else:
                out.append(lax.rem(index, size))
                index = lax.div(index, size)
        return tuple(reversed(out))

    def index(self, coords):
        total = 0
        for at, size in zip(coords, self.sizes):
            total = total * size + at
        return total

    def moved(self, coords, steps, sign=1):
        out = []
        for at, by, size in zip(coords, steps, self.sizes):
            to = at + sign * by + size
            out.append(to % size if isinstance(to, int) else lax.rem(to, size))
        return tuple(out)

    def send(self, value, steps):
        pairs = []
        for source in range(self.count):
            pairs.append((source, self.index(self.moved(self.coords(source), steps))))
        return lax.ppermute(value, BOTH, pairs)


def gathered(devices, shard):
    far, near, core, lon = devices.sizes
    line = jnp.stack([shard] + [devices.send(shard, (f, 0, 0, 0)) for f in range(1, far)])
    planes, parts = [], []
    for c in range(core):
        for n in range(near):
            for o in range(lon):
                if c:
                    plane = devices.send(planes[n * lon + o], (0, 0, c, 0))
                else:
                    plane = line if n == o == 0 else devices.send(line, (0, n, 0, o))
                planes.append(plane)
                parts.append((c, n, o))
    return planes, parts


def halved(devices, chunks):
    half = chunks[0].astype(F32)
    for c in range(1, chunks.shape[0]):
        half = half + devices.send(chunks[c], (0, 0, c, 0)).astype(F32)
    return half.astype(BF16)


def summed(half, size):
    half = lax.all_to_all(half, ("chip", "lon"), 0, 0, tiled=True)
    return jnp.sum(half.astype(F32), axis=0).reshape(-1)[:size]


def order(devices, sign):
    far, near, core, lon = devices.sizes
    mine = devices.place()[1]
    places = []
    for c in range(core):
        for n in range(near):
            for o in range(lon):
                for f in range(far):
                    places.append(devices.index(devices.moved(mine, (f, n, c, o), sign)))
    return jnp.stack(places)


def owners(devices):
    far, near, core, lon = devices.sizes
    at = devices.place()[1][2]
    places = []
    for c in range(core):
        for f in range(far):
            for n in range(near):
                for o in range(lon):
                    places.append(devices.index((f, n, lax.rem(at + c, core), o)))
    return jnp.stack(places)


def passed(devices, half):
    far, near, core, lon = devices.sizes

    def add(terms):
        total = terms[0].astype(F32)
        for term in terms[1:]:
            total = total + term.astype(F32)
        return total

    half = half.reshape(near * lon, far, *half.shape[1:])
    terms = []
    for n in range(near):
        for o in range(lon):
            part = half[n * lon + o]
            terms.append(part if n == o == 0 else devices.send(part, (0, n, 0, o)))
    line = add(terms).astype(BF16)
    return add([line[0]] + [devices.send(line[f], (f, 0, 0, 0)) for f in range(1, far)])


WEST, EAST = 9, 10
BEFORE, AFTER = 2, 3
CORNER = 16


def strips(rows, cols):
    side, at = [], 0
    for inputs, cots in ((WEST, BEFORE), (EAST, AFTER)):
        columns = [at + 2 * rows * j for j in range(inputs)]
        at += 2 * rows * inputs
        parts = [[at + rows * (cots * part + j) for j in range(cots)] for part in range(2)]
        at += 2 * rows * cots
        side.append((columns, parts))
    return side, at


def edges(rows, cols, inputs, cots):
    places = [0, 2 * cols * inputs]
    places.append(places[-1] + CORNER * (WEST + EAST))
    places.append(places[-1] + 2 * cots * cols)
    places.append(places[-1] + 2 * CORNER * (BEFORE + AFTER))
    return places


def halves(value):
    return value[..., :128], jnp.concatenate([value[..., 128:], value[..., 128:]], axis=-1)


def pack_sides(rows, cols, x_ref, c_ref, side_ref, parts_ref, strip):
    west, east = strips(rows, cols)[0]

    def columns(value, wanted, places):
        high = value.shape[0]
        strip[: high * CORNER, :] = value.astype(F32).reshape(high * CORNER, 128)
        for j, place in zip(wanted, places):
            side_ref[place : place + high, :] = strip[pl.ds(j, high, stride=CORNER), :].astype(BF16)

    columns(x_ref[:, 2 * cols - CORNER :, :], range(CORNER - WEST, CORNER), west[0])
    columns(x_ref[:, :CORNER, :], range(EAST), east[0])
    parts = halves(c_ref[...])
    for part in range(2):
        parts_ref[part] = parts[part]
        columns(parts[part][:, cols - CORNER :], range(CORNER - BEFORE, CORNER), west[1][part])
        columns(parts[part][:, :CORNER], range(AFTER), east[1][part])


def pack_edges(rows, cols, x_ref, parts_ref, side_ref, south_ref, north_ref):
    side = strips(rows, cols)[0]
    for ref, inputs, cots, last in (
        (south_ref, WEST, BEFORE, True),
        (north_ref, EAST, AFTER, False),
    ):
        at = edges(rows, cols, inputs, cots)
        first = 2 * rows - inputs if last else 0
        for i in range(inputs):
            ref[at[0] + 2 * cols * i : at[0] + 2 * cols * (i + 1), :] = x_ref[first + i]
        first = 2 * rows - CORNER if last else 0
        to = at[1]
        for columns, _ in side:
            for place in columns:
                ref[to : to + CORNER, :] = side_ref[place + first : place + first + CORNER, :]
                to += CORNER
        first = rows - cots if last else 0
        to = at[2]
        for part in range(2):
            for i in range(cots):
                ref[to : to + cols, :] = parts_ref[part, first + i]
                to += cols
        first = rows - CORNER if last else 0
        for part in range(2):
            for _, parts in side:
                for place in parts[part]:
                    ref[to : to + CORNER, :] = side_ref[place + first : place + first + CORNER, :]
                    to += CORNER


def sideways(rows, cols, packed):
    count = lax.axis_size("lon")
    east = [(i, (i + 1) % count) for i in range(count)]
    west = [(i, (i - 1) % count) for i in range(count)]
    if count == 2:
        return lax.ppermute(packed, "lon", east)
    cut = strips(rows, cols)[0][1][0][0]
    before = lax.ppermute(packed[:cut], "lon", east)
    after = lax.ppermute(packed[cut:], "lon", west)
    return jnp.concatenate([before, after], axis=0)


def lengthways(south, north):
    count = lax.axis_size("chip") * lax.axis_size("core")
    down = [(i, i + 1) for i in range(count - 1)]
    up = [(i + 1, i) for i in range(count - 1)]
    return lax.ppermute(south, LAT, down), lax.ppermute(north, LAT, up)


LEFT = 16
ABOVE = 5
BELOW = 7
GUARD = 8
HALF = 64

FRINGE = (((0, 0, 0),), ((0, 1, 0),), ((0, 2, 0),), ((0, 0, 1), (0, 1, 1)), ((0, 2, 1), (1, 2, 1)))
MIDDLE = (((1, 0, 0),), ((1, 1, 0),), ((1, 2, 0),), ((1, 0, 1), (1, 1, 1)))
LAST = (((2, 0, 0),), ((2, 1, 0),), ((2, 2, 0),), ((2, 0, 1), (2, 1, 1)), ((2, 2, 1), None))
BLOCKS = FRINGE + MIDDLE + LAST


def low_lanes(rows):
    return lax.broadcasted_iota(jnp.int32, (rows, 128), 1) < HALF


def swapped(value):
    return pltpu.roll(value, HALF, 1)


def prepare(
    rows, cols, x_ref, parts_ref, side_ref, south_ref, north_ref, windows_ref, cot_ref, wide, cots
):
    pitch = cols + LEFT
    height = rows + ABOVE + BELOW
    size = height * pitch
    span = 2 * cols + 48
    base_row, base_col = 20, 24
    wide[...] = jnp.zeros_like(wide)
    cots[...] = jnp.zeros_like(cots)
    side = strips(rows, cols)[0]
    columns = [*range(-WEST, 0), *range(2 * cols, 2 * cols + EAST)]

    def at(i, j):
        return (i + base_row) * span + base_col + j

    def own(i, _):
        wide[pl.ds(pl.multiple_of(at(i, 0), 8), 2 * cols), :] = x_ref[i].astype(F32)
        return 0

    lax.fori_loop(0, 2 * rows, own, 0)
    for j, place in zip(columns, side[0][0] + side[1][0]):
        strip = side_ref[place : place + 2 * rows, :].astype(F32)
        wide[pl.ds(at(0, j), 2 * rows, stride=span), :] = strip
    for ref, inputs, cotangents, top, above in (
        (south_ref, WEST, BEFORE, -WEST, True),
        (north_ref, EAST, AFTER, 2 * rows, False),
    ):
        places = edges(rows, cols, inputs, cotangents)
        for i in range(inputs):
            edge = ref[2 * cols * i : 2 * cols * (i + 1), :].astype(F32)
            wide[at(top + i, 0) : at(top + i, 0) + 2 * cols, :] = edge
        first = -CORNER if above else 2 * rows
        for k, j in enumerate(columns):
            place = places[1] + CORNER * k
            corner = ref[place : place + CORNER, :].astype(F32)
            wide[pl.ds(at(first, j), CORNER, stride=span), :] = corner

    def window(k, _):
        for parity in range(2):
            row = 2 * (k - ABOVE) + parity + base_row
            for tap in range(3):
                base = row * span + base_col - 1 + tap
                mid = wide[pl.ds(base, cols, stride=2), :]
                before = wide[pl.ds(base - 16, 8, stride=2), :]
                after = wide[pl.ds(base - 2 * span + 2 * cols, 8, stride=2), :]
                lane = (3 * parity + tap) * 128
                cells = jnp.concatenate([after, before, mid], axis=0).astype(BF16)
                windows_ref[pl.ds(pl.multiple_of(k * pitch, 16), pitch), lane : lane + 128] = cells
        return 0

    lax.fori_loop(0, height, window, 0)

    def cell(i, j):
        return GUARD + (i + ABOVE) * pitch + LEFT + j

    columns = [*range(-BEFORE, 0), *range(cols, cols + AFTER)]
    for part in range(2):
        for i in range(rows):
            cots[cell(i, 0) : cell(i, cols), :] = parts_ref[part, i].astype(F32)
        for j, place in zip(columns, side[0][1][part] + side[1][1][part]):
            strip = side_ref[place : place + rows, :].astype(F32)
            cots[pl.ds(cell(0, j), rows, stride=pitch), :] = strip
        for ref, inputs, cotangents, above in (
            (south_ref, WEST, BEFORE, True),
            (north_ref, EAST, AFTER, False),
        ):
            places = edges(rows, cols, inputs, cotangents)
            for i in range(cotangents):
                place = places[2] + cols * (cotangents * part + i)
                to = cell(i - cotangents if above else rows + i, 0)
                cots[to : to + cols, :] = ref[place : place + cols, :].astype(F32)
            for k, j in enumerate(columns):
                place = places[3] + CORNER * (len(columns) * part + k)
                corner = ref[place : place + CORNER, :].astype(F32)
                if above:
                    corner = corner[CORNER - 8 :]
                else:
                    corner = corner[:8]
                for i in range(cotangents):
                    to = cell(i - cotangents if above else rows + i, j)
                    line = 8 - cotangents + i if above else i
                    cots[to : to + 1, :] = corner[line : line + 1]
        cot_ref[:, 128 * part : 128 * part + 128] = cots[GUARD : GUARD + size, :].astype(BF16)


def level(shape, devices, parts, second, names, *refs):
    rows, cols, chan_in, mid, factor, whole = shape
    refs = dict(zip(names, refs))
    x_ref, terms_ref = refs["x"], refs["terms"]
    flat, k_a, k_b, f_a, f_b = (refs[name] for name in ("flat", "k_a", "k_b", "f_a", "f_b"))
    win_delta, t_one, t_two = (refs[name] for name in ("win_delta", "t_one", "t_two"))
    pitch = cols + LEFT
    height = rows + ABOVE + BELOW
    size = height * pitch
    far, near, core, lon = devices.sizes
    count = 1 if whole else devices.count
    share = [9 * c * mid // 128 // count for c in (chan_in, mid, mid)]
    begin = [0, share[0], share[0] + share[1]]
    lat_at, mine = devices.place()
    f_a[...] = jnp.zeros_like(f_a)
    f_b[...] = jnp.zeros_like(f_b)

    def unpack(which, channels):
        n = share[which]
        for i, (c, m, o) in enumerate(parts):
            plane = refs["plane", i]
            for f in range(plane.shape[0]):
                owner = 0 if whole else devices.index(devices.moved(mine, (f, m, c, o), -1))
                lo = begin[which] // 16 * 16
                hi = -(-(begin[which] + n) // 16) * 16
                value = plane[f, lo:hi, :].astype(F32)
                flat[pl.ds(owner * n, n), :] = value[begin[which] - lo : begin[which] - lo + n]
        pairs = 9 * channels // 2
        step = 96

        def one(i, _):
            at = i * step
            first = flat[pl.ds(3 * at, step, stride=3), :]
            second = flat[pl.ds(3 * at + 1, step, stride=3), :]
            third = flat[pl.ds(3 * at + 2, step, stride=3), :]
            low = low_lanes(step)
            second_r, third_r = swapped(second), swapped(third)
            k_a[pl.ds(2 * at, step, stride=2), :] = first
            k_b[pl.ds(2 * at, step, stride=2), :] = jnp.where(low, second, second_r)
            k_a[pl.ds(2 * at + 1, step, stride=2), :] = jnp.where(low, second_r, third_r)
            k_b[pl.ds(2 * at + 1, step, stride=2), :] = jnp.where(low, third_r, third)
            return 0

        lax.fori_loop(0, pairs // step, one, 0)

    def tap_rows(tap, part):
        start = (3 * tap[0] + tap[1]) * mid + 128 * part
        return start, start + (HALF if part else 128)

    def forward(target):
        at = 0
        for block in BLOCKS:
            for tap in block:
                if tap is None:
                    target[at : at + HALF, :] = jnp.zeros((HALF, 256), BF16)
                    at += HALF
                    continue
                lo, hi = tap_rows(tap, tap[2])
                target[at : at + hi - lo, 0:128] = k_a[lo:hi, :].astype(BF16)
                target[at : at + hi - lo, 128:256] = k_b[lo:hi, :].astype(BF16)
                at += hi - lo

    def backward(target):
        low = low_lanes(mid)
        for i, block in enumerate(BLOCKS):
            values = []
            for tap in block:
                if tap is None:
                    values.append(jnp.zeros((mid, 128), F32))
                    continue
                lo = (3 * (2 - tap[0]) + 2 - tap[1]) * mid
                source = k_b if tap[2] else k_a
                values.append(source[lo : lo + mid, :])
            value = values[0] if len(values) == 1 else jnp.where(low, values[0], values[1])
            value = value.astype(BF16)
            target[0:mid, 128 * i : 128 * i + 128] = value
            target[mid:256, 128 * i : 128 * i + 128] = value[128:mid]

    def load_kernels():
        unpack(0, chan_in)
        refs["w_one"][:, 0:128] = k_a[0 : 9 * chan_in, :].astype(BF16)
        refs["w_one"][:, 128:256] = k_b[0 : 9 * chan_in, :].astype(BF16)
        empty = jnp.zeros((chan_in, 128), F32)
        low_in = low_lanes(chan_in)
        phases = (
            ((1, 1), None, None, None),
            ((1, 2), (1, 0), None, None),
            ((2, 1), None, (0, 1), None),
            ((2, 2), (2, 0), (0, 2), (0, 0)),
        )
        for i, taps in enumerate(phases):
            a, b = [], []
            for tap in taps:
                if tap is None:
                    a.append(empty)
                    b.append(empty)
                else:
                    lo = (3 * tap[0] + tap[1]) * chan_in
                    a.append(k_a[lo : lo + chan_in, :])
                    b.append(k_b[lo : lo + chan_in, :])
            blocks = (
                a[0],
                a[1],
                jnp.where(low_in, b[0], b[1]),
                a[2],
                a[3],
                jnp.where(low_in, b[2], b[3]),
            )
            for j, block in enumerate(blocks):
                t_one[chan_in * i : chan_in * (i + 1), 128 * j : 128 * j + 128] = block.astype(BF16)
        unpack(1, mid)
        forward(refs["w_two"])
        backward(t_two)
        unpack(2, mid)
        forward(refs["w_three"])
        backward(refs["t_three"])

    first_row = lat_at * rows
    bottom = lax.axis_size("chip") * core * rows - first_row
    low_cell = (jnp.maximum(-first_row, -ABOVE) + ABOVE) * pitch + 8
    high_cell = (jnp.minimum(bottom, rows + BELOW) + ABOVE) * pitch + 8

    def inside(start, n):
        cell = start + lax.broadcasted_iota(jnp.int32, (n, 128), 0)
        return (cell >= low_cell) & (cell < high_cell)

    def store(start, n, left, right, mask):
        if mask:
            keep = inside(start, n)
            left = jnp.where(keep, left, 0.0)
            right = jnp.where(keep, right, 0.0)
        at = pl.multiple_of(start + GUARD, 8)
        f_a[pl.ds(at, n), :] = left
        f_b[pl.ds(at, n), :] = right

    def windows(target, top, under):
        def one(i, _):
            cell = i * pitch
            q = cell + GUARD
            low = low_lanes(pitch)
            b_0, b_1, b_2 = (f_b[pl.ds(q + s, pitch), :] for s in (-1, 0, 1))
            b_3 = f_b[pl.ds(q + 1 + pitch, pitch), :]
            out = [f_a[pl.ds(q + s, pitch), :] for s in (-1, 0, 1)]
            out += [jnp.where(low, b_0, b_1), jnp.where(low, b_2, b_3)]
            at = pl.multiple_of(cell, 16)
            for j, value in enumerate(out):
                target[pl.ds(at, pitch), 128 * j : 128 * j + 128] = value.astype(BF16)
            return 0

        lax.fori_loop(top + ABOVE, under + ABOVE, one, 0)

    def convolve(source, weights, turned, halo, steps, finish):
        start = (ABOVE - halo) * pitch
        total = (rows + 1 + 2 * halo) * pitch + LEFT
        n = -(-total // steps // 16) * 16
        contract = (((1,), (1,)), ((), ())) if turned else (((1,), (0,)), ((), ()))

        def one(i, _):
            p = pl.multiple_of(start + i * n, 16)
            above = source[pl.ds(pl.multiple_of(p - pitch, 16), n), :]
            here = source[pl.ds(p, n), 0:512]
            below = source[pl.ds(pl.multiple_of(p + pitch, 16), n), :]
            value = lax.dot_general(
                jnp.concatenate([above, here, below], axis=1),
                weights[...],
                contract,
                preferred_element_type=F32,
            )
            finish(p, n, value)
            return 0

        lax.fori_loop(0, steps, one, 0)

    def own(ref, lanes, row_step=0, shift=0, offset=0):
        pieces = []
        for r in range(rows):
            at = offset + (ABOVE + r + row_step) * pitch + LEFT + shift
            pieces.append(ref[at : at + cols, lanes])
        return jnp.concatenate(pieces, axis=0)

    ALL = slice(0, 128)

    def turned_deltas():
        left = own(f_a, ALL, offset=GUARD)
        right = own(f_b, ALL, offset=GUARD)
        return jnp.concatenate([left.T, right.T], axis=0).astype(BF16)

    def pack(which, channels, first=0):
        step = 96

        def one(i, _):
            at = i * step
            even_a = k_a[pl.ds(2 * at, step, stride=2), :]
            even_b = k_b[pl.ds(2 * at, step, stride=2), :]
            odd_a = swapped(k_a[pl.ds(2 * at + 1, step, stride=2), :])
            odd_b = k_b[pl.ds(2 * at + 1, step, stride=2), :]
            low = low_lanes(step)
            flat[pl.ds(3 * at, step, stride=3), :] = even_a
            flat[pl.ds(3 * at + 1, step, stride=3), :] = jnp.where(low, even_b, odd_a)
            flat[pl.ds(3 * at + 2, step, stride=3), :] = jnp.where(low, odd_a, odd_b)
            return 0

        lax.fori_loop(0, 9 * channels // 2 // step, one, 0)
        n = share[which]
        for k in range(count):
            refs["chunk"][k, first : first + n, :] = flat[k * n : (k + 1) * n, :]

    def hand_over():
        for k in range(count):
            f, m, c, o = devices.coords(k)
            place, side = 0, 0
            if not whole:
                side = lax.rem(c - mine[2] + core, core)
                place = (f * near + m) * lon + o
                if not second:
                    away = zip(devices.coords(k), mine, devices.sizes)
                    f, m, c, o = (lax.rem(to - at + by, by) for to, at, by in away)
                    place = (m * lon + o) * far + f
            terms_ref[side, place] = refs["chunk"][k].astype(BF16)

    def field_grad(which, source, first):
        turned = turned_deltas()
        for a, blocks in enumerate((FRINGE, MIDDLE, LAST)):
            lanes = slice(0, 128 * len(blocks))
            product = lax.dot_general(
                turned,
                own(source, lanes, a - 1),
                (((1,), (0,)), ((), ())),
                preferred_element_type=F32,
            )
            product = product * factor
            for j, block in enumerate(blocks):
                left = product[0:128, 128 * j : 128 * j + 128].T
                right = product[128:256, 128 * j : 128 * j + 128].T
                at = 0
                for tap in block:
                    if tap is None:
                        continue
                    lo, hi = tap_rows(tap, tap[2])
                    k_a[lo:hi, :] = left[at : at + hi - lo]
                    k_b[lo:hi, :] = right[at : at + hi - lo]
                    at += hi - lo
        pack(which, mid, first)

    def forward_pass():
        load_kernels()
        win_one, win_two, slope, spread, c_ref = (
            refs[name] for name in ("win_one", "win_two", "slope", "spread", "c")
        )
        slope[...] = jnp.zeros_like(slope)

        def convolve_first():
            halo, steps = 4, 4
            start = (ABOVE - halo) * pitch
            total = (rows + 1 + 2 * halo) * pitch + LEFT
            n = -(-total // steps // 16) * 16

            def one(i, _):
                p = pl.multiple_of(start + i * n, 16)
                above = x_ref[pl.ds(pl.multiple_of(p - pitch, 16), n), 384:768]
                here = x_ref[pl.ds(p, n), :]
                value = lax.dot_general(
                    jnp.concatenate([above, here], axis=1),
                    refs["w_one"][...],
                    (((1,), (0,)), ((), ())),
                    preferred_element_type=F32,
                )
                store(p, n, value[:, :128], value[:, 128:], True)
                return 0

            lax.fori_loop(0, steps, one, 0)

        convolve_first()
        windows(win_one, -4, rows + 6)

        def finish_two(p, n, value):
            s = jax.nn.sigmoid(value)
            active = value * s
            slope[pl.ds(p, n), :] = s + active * (1.0 - s)
            store(p, n, active[:, :128], active[:, 128:], True)

        convolve(win_one, refs["w_two"], False, 3, 4, finish_two)
        windows(win_two, -3, rows + 5)

        def finish_three(p, n, value):
            s = jax.nn.sigmoid(value)
            active = value * s
            delta = c_ref[pl.ds(p, n), :].astype(F32) * (s + active * (1.0 - s))
            store(p, n, delta[:, :128], delta[:, 128:], False)
            spread[pl.ds(p, n), :] = active

        convolve(win_two, refs["w_three"], False, 2, 4, finish_three)
        for r in range(rows):
            at = (ABOVE + r) * pitch + LEFT
            refs["features"][r] = spread[at : at + cols, 0:mid].astype(BF16)
        field_grad(2, win_two, share[1])
        windows(win_delta, -2, rows + 4)

        def finish_delta(p, n, value):
            value = value * slope[pl.ds(p, n), :]
            store(p, n, value[:, :128], value[:, 128:], True)

        convolve(win_delta, refs["t_three"], True, 1, 4, finish_delta)
        field_grad(1, win_one, 0)
        hand_over()
        windows(win_delta, -1, rows + 3)

    def backward_pass():
        def finish_back(p, n, value):
            store(p, n, value[:, :128], value[:, 128:], True)

        convolve(win_delta, t_two, True, 0, 4, finish_back)
        turned = turned_deltas()
        for a, (step, lanes) in enumerate(((-1, slice(384, 768)), (0, slice(0, 384)), (0, slice(384, 768)))):
            product = lax.dot_general(
                turned,
                own(x_ref, lanes, step),
                (((1,), (0,)), ((), ())),
                preferred_element_type=F32,
            )
            product = product * factor
            lo = 3 * a * chan_in
            k_a[lo : lo + 3 * chan_in, :] = product[0:128].T
            k_b[lo : lo + 3 * chan_in, :] = product[128:256].T
        pack(0, chan_in)
        hand_over()

        low = low_lanes(rows * cols)

        def four(ref):
            return [own(ref, ALL, r, c, GUARD) for r, c in ((0, 0), (0, 1), (1, 0), (1, 1))]

        a, b = four(f_a), four(f_b)
        around = (a[0], a[1], jnp.where(low, b[0], b[1]), a[2], a[3], jnp.where(low, b[2], b[3]))
        around = jnp.concatenate([value.astype(BF16) for value in around], axis=1)
        for r in range(2):
            wide = 384 * (r + 1)
            product = lax.dot_general(
                around[:, :wide],
                t_one[2 * chan_in * r : 2 * chan_in * (r + 1), :wide],
                (((1,), (1,)), ((), ())),
                preferred_element_type=F32,
            )
            for i in range(rows):
                at = i * cols
                base = (2 * i + r) * 2 * cols
                for c in range(2):
                    spread_in = product[at : at + cols, chan_in * c : chan_in * (c + 1)]
                    refs["image"][pl.ds(base + c, cols, stride=2), :] = spread_in
        for i in range(2 * rows):
            refs["grad_input"][i] = refs["image"][2 * cols * i : 2 * cols * (i + 1), :].astype(BF16)

    if second:
        backward_pass()
    else:
        forward_pass()


VMEM = pl.BlockSpec(memory_space=pltpu.VMEM)
ANY = pl.BlockSpec(memory_space=pl.ANY)


def local(inputs, w_first, w_second, w_third, cotangent):
    devices = Slice()
    rows, cols, mid = cotangent.shape
    chan_in = inputs.shape[2]
    factor = 1.0 / LOSS_CELLS
    far, near, core, lon = devices.sizes
    held = (w_first.shape[0], w_second.shape[0], w_third.shape[0])
    shard = jnp.concatenate([w_first, w_second, w_third]).reshape(-1, 128)
    whole = any(n % 128 for n in held)
    if not whole:
        shard = jnp.pad(shard, ((0, -shard.shape[0] % 16), (0, 0)))
    planes, parts = gathered(devices, shard)
    if whole:
        chunks = jnp.stack(planes).reshape(devices.count, -1)
        chunks = jnp.take(chunks, jnp.argsort(order(devices, -1)), axis=0)
        pieces = jnp.split(chunks, (held[0], held[0] + held[1]), axis=1)
        chunks = jnp.concatenate([piece.reshape(-1) for piece in pieces])
        planes, parts = [chunks.reshape(1, -1, 128)], [(0, 0, 0)]
    count = 1 if whole else devices.count
    depth = planes[0].shape[1]

    packed_rows = strips(rows, cols)[1]
    packed, split_cot = pl.pallas_call(
        functools.partial(pack_sides, rows, cols),
        out_shape=(
            jax.ShapeDtypeStruct((packed_rows, 128), BF16),
            jax.ShapeDtypeStruct((2, rows, cols, 128), BF16),
        ),
        in_specs=[VMEM] * 2,
        out_specs=(VMEM, VMEM),
        scratch_shapes=[pltpu.VMEM((2 * rows * CORNER, 128), F32)],
        compiler_params=pltpu.CompilerParams(vmem_limit_bytes=16 * 2**20),
        cost_estimate=pl.CostEstimate(flops=0, bytes_accessed=3 * 2**20, transcendentals=0),
    )(inputs, cotangent)
    side = sideways(rows, cols, packed)
    south, north = pl.pallas_call(
        functools.partial(pack_edges, rows, cols),
        out_shape=(
            jax.ShapeDtypeStruct((edges(rows, cols, WEST, BEFORE)[-1], 128), BF16),
            jax.ShapeDtypeStruct((edges(rows, cols, EAST, AFTER)[-1], 128), BF16),
        ),
        in_specs=[VMEM] * 3,
        out_specs=(VMEM, VMEM),
        compiler_params=pltpu.CompilerParams(vmem_limit_bytes=16 * 2**20),
        cost_estimate=pl.CostEstimate(flops=0, bytes_accessed=3 * 2**20, transcendentals=0),
    )(inputs, split_cot, side)
    south, north = lengthways(south, north)
    size = (rows + ABOVE + BELOW) * (cols + LEFT)
    padded, cot = pl.pallas_call(
        functools.partial(prepare, rows, cols),
        out_shape=(
            jax.ShapeDtypeStruct((size, 6 * chan_in), BF16),
            jax.ShapeDtypeStruct((size, 256), BF16),
        ),
        in_specs=[VMEM] * 5,
        out_specs=(VMEM, VMEM),
        scratch_shapes=[
            pltpu.VMEM(((2 * rows + 40) * (2 * cols + 48), 128), F32),
            pltpu.VMEM((size + 2 * GUARD, 128), F32),
        ],
        compiler_params=pltpu.CompilerParams(vmem_limit_bytes=40 * 2**20),
        cost_estimate=pl.CostEstimate(flops=0, bytes_accessed=12 * 2**20, transcendentals=0),
    )(inputs, split_cot, side, south, north)

    deep = -(-(2 * held[1]) // 2048) * 16, -(-held[0] // 2048) * 16
    if whole:
        deep = 2 * held[1] * devices.count // 128, held[0] * devices.count // 128
    sides = 1 if whole else core
    field_shape = (size + 2 * GUARD, 128)
    shape = (rows, cols, chan_in, mid, factor, whole)
    wide = 128 * len(BLOCKS)
    shared = {
        "flat": ((9 * mid * mid // 128, 128), F32),
        "k_a": ((9 * mid, 128), F32),
        "k_b": ((9 * mid, 128), F32),
        "f_a": (field_shape, F32),
        "f_b": (field_shape, F32),
    }

    def call(second, ins, outs, scratch):
        scratch = {**scratch, **shared}
        names = list(ins) + list(outs) + list(scratch)
        results = pl.pallas_call(
            functools.partial(level, shape, devices, () if second else parts, second, names),
            out_shape=[jax.ShapeDtypeStruct(*out) for out in outs.values()],
            in_specs=[VMEM] * len(ins),
            out_specs=[VMEM] * len(outs),
            scratch_shapes=[pltpu.VMEM(*kind) for kind in scratch.values()],
            compiler_params=pltpu.CompilerParams(vmem_limit_bytes=40 * 2**20),
            cost_estimate=pl.CostEstimate(
                flops=2 * 10**9 if second else 5 * 10**9,
                bytes_accessed=12 * 2**20,
                transcendentals=10**6,
            ),
        )(*ins.values())
        return dict(zip(outs, results))

    ins = {"x": padded, "c": cot}
    for i, plane in enumerate(planes):
        ins["plane", i] = plane
    done = call(
        False,
        ins,
        {
            "features": ((rows, cols, mid), BF16),
            "terms": ((sides, count // sides, deep[0], 128), BF16),
            "win_delta": ((size, 640), BF16),
            "t_one": ((4 * chan_in, 768), BF16),
            "t_two": ((256, wide), BF16),
        },
        {
            "chunk": ((count, deep[0], 128), F32),
            "w_one": ((9 * chan_in, 256), BF16),
            "w_two": ((wide, 256), BF16),
            "w_three": ((wide, 256), BF16),
            "t_three": ((256, wide), BF16),
            "slope": ((size, 256), F32),
            "spread": ((size, 256), F32),
            "win_one": ((size, 640), BF16),
            "win_two": ((size, 640), BF16),
        },
    )
    features = done["features"]

    def reduced(terms, places, *sizes):
        if whole:
            cuts = [sum(sizes[:i]) * devices.count for i in range(1, len(sizes))]
            pieces = jnp.split(terms.reshape(-1), cuts)
            terms = [piece.reshape(devices.count, -1) for piece in pieces]
            terms = jnp.take(jnp.concatenate(terms, axis=1), places, axis=0)
            terms = terms.reshape(core, devices.count // core, 1, -1)
        return halved(devices, terms)

    upper = reduced(done["terms"], order(devices, 1), held[1], held[2])
    upper, win_delta = lax.optimization_barrier((upper, done["win_delta"]))
    done["win_delta"] = win_delta
    upper = passed(devices, upper).reshape(-1)
    grad_second, grad_third = upper[: held[1]], upper[held[1] : held[1] + held[2]]
    done = call(
        True,
        {"x": padded, **{name: done[name] for name in ("win_delta", "t_one", "t_two")}},
        {
            "grad_input": ((2 * rows, 2 * cols, chan_in), BF16),
            "terms": ((sides, count // sides, deep[1], 128), BF16),
        },
        {
            "chunk": ((count, deep[1], 128), F32),
            "image": ((4 * rows * cols, 128), F32),
        },
    )
    lower = reduced(done["terms"], owners(devices), held[0])
    grad_first = summed(lower, held[0])
    return (features, done["grad_input"], grad_first, grad_second, grad_third)


def solution(mesh):
    lat, lon = mesh.shape["lat"], mesh.shape["lon"]
    core = 2 if lat % 2 == 0 else 1
    chips = jax.sharding.Mesh(mesh.devices.reshape(lat // core, core, lon), BOTH)
    tile = P(LAT, "lon", None)
    flat = P(BOTH)
    return jax.shard_map(
        local,
        mesh=chips,
        in_specs=(tile, flat, flat, flat, tile),
        out_specs=(tile, tile, flat, flat, flat),
        check_vma=False,
    )
```

```python
import functools

import jax
import jax.numpy as jnp
from jax import lax
from jax.experimental import pallas as pl
from jax.experimental.pallas import tpu as pltpu
from jax.sharding import PartitionSpec as P

LOSS_CELLS = 1024
LAT = ("chip", "core")
BOTH = ("chip", "core", "lon")
F32 = jnp.float32
BF16 = jnp.bfloat16


class Slice:
    def __init__(self):
        chip, core, lon = (lax.axis_size(axis) for axis in BOTH)
        near = 2 if chip % 2 == 0 else 1
        self.sizes = (chip // near, near, core, lon)
        self.count = chip * core * lon

    def place(self):
        lat = lax.axis_index("chip") * self.sizes[2] + lax.axis_index("core")
        return lat, self.coords(lat * self.sizes[3] + lax.axis_index("lon"))

    def coords(self, index):
        out = []
        for size in reversed(self.sizes):
            if isinstance(index, int):
                out.append(index % size)
                index = index // size
            else:
                out.append(lax.rem(index, size))
                index = lax.div(index, size)
        return tuple(reversed(out))

    def index(self, coords):
        total = 0
        for at, size in zip(coords, self.sizes):
            total = total * size + at
        return total

    def moved(self, coords, steps, sign=1):
        out = []
        for at, by, size in zip(coords, steps, self.sizes):
            if size & (size - 1) == 0:
                out.append(at ^ by)
            else:
                to = at + sign * by + size
                out.append(to % size if isinstance(to, int) else lax.rem(to, size))
        return tuple(out)

    def apart(self, coords, origin):
        out = []
        for to, at, size in zip(coords, origin, self.sizes):
            out.append(at ^ to if size & (size - 1) == 0 else lax.rem(to - at + size, size))
        return tuple(out)

    def send(self, value, steps):
        pairs = []
        for source in range(self.count):
            pairs.append((source, self.index(self.moved(self.coords(source), steps))))
        return lax.ppermute(value, BOTH, pairs)


def lined(devices, shard):
    far = devices.sizes[0]
    return jnp.stack([shard] + [devices.send(shard, (f, 0, 0, 0)) for f in range(1, far)])


def spread(devices, line):
    far, near, core, lon = devices.sizes
    planes = []
    for n in range(near):
        for o in range(lon):
            planes.append(line if n == o == 0 else devices.send(line, (0, n, 0, o)))
    return planes


def shared_out(devices, planes):
    far, near, core, lon = devices.sizes
    out, parts = [], []
    for c in range(core):
        for n in range(near):
            for o in range(lon):
                plane = planes[n * lon + o]
                out.append(devices.send(plane, (0, 0, c, 0)) if c else plane)
                parts.append((c, n, o))
    return out, parts


def halved(devices, chunks):
    half = chunks[0].astype(F32)
    for c in range(1, chunks.shape[0]):
        half = half + devices.send(chunks[c], (0, 0, c, 0)).astype(F32)
    return half.astype(BF16)


def order(devices, sign):
    far, near, core, lon = devices.sizes
    mine = devices.place()[1]
    places = []
    for c in range(core):
        for n in range(near):
            for o in range(lon):
                for f in range(far):
                    places.append(devices.index(devices.moved(mine, (f, n, c, o), sign)))
    return jnp.stack(places)


def total_of(terms):
    total = terms[0].astype(F32)
    for term in terms[1:]:
        total = total + term.astype(F32)
    return total


def planar(devices, half):
    far, near, core, lon = devices.sizes
    half = half.reshape(near * lon, far, *half.shape[1:])
    terms = []
    for n in range(near):
        for o in range(lon):
            part = half[n * lon + o]
            terms.append(part if n == o == 0 else devices.send(part, (0, n, 0, o)))
    return total_of(terms).astype(BF16)


def linear(devices, line):
    far = devices.sizes[0]
    return total_of([line[0]] + [devices.send(line[f], (f, 0, 0, 0)) for f in range(1, far)])


WEST, EAST = 9, 10
BEFORE, AFTER = 2, 3
CORNER = 16


def strips(inputs_high, cots_high):
    side, at = [], 0
    for inputs, cots in ((WEST, BEFORE), (EAST, AFTER)):
        columns = [at + inputs_high * j for j in range(inputs)]
        at += inputs_high * inputs
        parts = [[at + cots_high * (cots * part + j) for j in range(cots)] for part in range(2)]
        at += 2 * cots_high * cots
        side.append((columns, parts))
    return side, at


def halves(value):
    return value[..., :128], jnp.concatenate([value[..., 128:], value[..., 128:]], axis=-1)


def pack_sides(rows, cols, x_ref, c_ref, side_ref, south_ref, north_ref, strip):
    west, east = strips(2 * rows, rows)[0]

    def columns(value, wanted, places):
        high = value.shape[0]
        strip[: high * CORNER, :] = value.astype(F32).reshape(high * CORNER, 128)
        for j, place in zip(wanted, places):
            side_ref[place : place + high, :] = strip[pl.ds(j, high, stride=CORNER), :].astype(BF16)

    columns(x_ref[:, 2 * cols - CORNER :, :], range(CORNER - WEST, CORNER), west[0])
    columns(x_ref[:, :CORNER, :], range(EAST), east[0])
    parts = halves(c_ref[...])
    for part in range(2):
        columns(parts[part][:, cols - CORNER :], range(CORNER - BEFORE, CORNER), west[1][part])
        columns(parts[part][:, :CORNER], range(AFTER), east[1][part])
    for ref, inputs, cots, x_row, c_row in (
        (south_ref, WEST, BEFORE, 2 * rows - WEST, rows - BEFORE),
        (north_ref, EAST, AFTER, 0, 0),
    ):
        for i in range(inputs):
            ref[2 * cols * i : 2 * cols * (i + 1), :] = x_ref[x_row + i]
        at = 2 * cols * inputs
        for part in range(2):
            for i in range(cots):
                ref[at : at + cols, :] = parts[part][c_row + i]
                at += cols


def pack_corners(rows, side_ref, lower_ref, upper_ref):
    for side, corner in zip(strips(2 * rows, rows)[0], strips(CORNER, CORNER)[0]):
        strip = [(2 * rows, *pair) for pair in zip(side[0], corner[0])]
        for part in range(2):
            strip += [(rows, *pair) for pair in zip(side[1][part], corner[1][part])]
        for high, place, to in strip:
            end = place + high
            lower_ref[to : to + CORNER, :] = side_ref[end - CORNER : end, :]
            upper_ref[to : to + CORNER, :] = side_ref[place : place + CORNER, :]


def sideways(packed, cut):
    count = lax.axis_size("lon")
    east = [(i, (i + 1) % count) for i in range(count)]
    west = [(i, (i - 1) % count) for i in range(count)]
    if count == 2:
        return lax.ppermute(packed, "lon", east)
    before = lax.ppermute(packed[:cut], "lon", east)
    after = lax.ppermute(packed[cut:], "lon", west)
    return jnp.concatenate([before, after], axis=0)


def lengthways(south, north):
    count = lax.axis_size("chip") * lax.axis_size("core")
    down = [(i, i + 1) for i in range(count - 1)]
    up = [(i + 1, i) for i in range(count - 1)]
    return lax.ppermute(south, LAT, down), lax.ppermute(north, LAT, up)


LEFT = 16
ABOVE = 5
BELOW = 7
GUARD = 8
HALF = 64

FRINGE = (((0, 0, 0),), ((0, 1, 0),), ((0, 2, 0),), ((0, 0, 1), (0, 1, 1)), ((0, 2, 1), (1, 2, 1)))
MIDDLE = (((1, 0, 0),), ((1, 1, 0),), ((1, 2, 0),), ((1, 0, 1), (1, 1, 1)))
LAST = (((2, 0, 0),), ((2, 1, 0),), ((2, 2, 0),), ((2, 0, 1), (2, 1, 1)), ((2, 2, 1), None))
BLOCKS = FRINGE + MIDDLE + LAST


def low_lanes(rows):
    return lax.broadcasted_iota(jnp.int32, (rows, 128), 1) < HALF


def swapped(value):
    return pltpu.roll(value, HALF, 1)


def prepare(
    rows, cols, x_ref, c_ref, side_ref, south_ref, north_ref, lower_ref, upper_ref,
    windows_ref, cot_ref, wide, cots,
):
    pitch = cols + LEFT
    height = rows + ABOVE + BELOW
    size = height * pitch
    span = 2 * cols + 48
    base_row, base_col = 20, 24
    wide[...] = jnp.zeros_like(wide)
    cots[...] = jnp.zeros_like(cots)
    side = strips(2 * rows, rows)[0]
    corners = strips(CORNER, CORNER)[0]
    columns = [*range(-WEST, 0), *range(2 * cols, 2 * cols + EAST)]

    def at(i, j):
        return (i + base_row) * span + base_col + j

    def own(i, _):
        wide[pl.ds(pl.multiple_of(at(i, 0), 8), 2 * cols), :] = x_ref[i].astype(F32)
        return 0

    lax.fori_loop(0, 2 * rows, own, 0)
    for j, place in zip(columns, side[0][0] + side[1][0]):
        strip = side_ref[place : place + 2 * rows, :].astype(F32)
        wide[pl.ds(at(0, j), 2 * rows, stride=span), :] = strip
    for ref, corner_ref, inputs, top, first in (
        (south_ref, lower_ref, WEST, -WEST, -CORNER),
        (north_ref, upper_ref, EAST, 2 * rows, 2 * rows),
    ):
        for i in range(inputs):
            edge = ref[2 * cols * i : 2 * cols * (i + 1), :].astype(F32)
            wide[at(top + i, 0) : at(top + i, 0) + 2 * cols, :] = edge
        for place, j in zip(corners[0][0] + corners[1][0], columns):
            corner = corner_ref[place : place + CORNER, :].astype(F32)
            wide[pl.ds(at(first, j), CORNER, stride=span), :] = corner

    def window(k, _):
        for parity in range(2):
            row = 2 * (k - ABOVE) + parity + base_row
            for tap in range(3):
                base = row * span + base_col - 1 + tap
                mid = wide[pl.ds(base, cols, stride=2), :]
                before = wide[pl.ds(base - 16, 8, stride=2), :]
                after = wide[pl.ds(base - 2 * span + 2 * cols, 8, stride=2), :]
                lane = (3 * parity + tap) * 128
                cells = jnp.concatenate([after, before, mid], axis=0).astype(BF16)
                windows_ref[pl.ds(pl.multiple_of(k * pitch, 16), pitch), lane : lane + 128] = cells
        return 0

    lax.fori_loop(0, height, window, 0)

    def cell(i, j):
        return GUARD + (i + ABOVE) * pitch + LEFT + j

    columns = [*range(-BEFORE, 0), *range(cols, cols + AFTER)]
    parts = halves(c_ref[...])
    for part in range(2):
        for i in range(rows):
            cots[cell(i, 0) : cell(i, cols), :] = parts[part][i].astype(F32)
        for j, place in zip(columns, side[0][1][part] + side[1][1][part]):
            strip = side_ref[place : place + rows, :].astype(F32)
            cots[pl.ds(cell(0, j), rows, stride=pitch), :] = strip
        for ref, corner_ref, inputs, count, above in (
            (south_ref, lower_ref, WEST, BEFORE, True),
            (north_ref, upper_ref, EAST, AFTER, False),
        ):
            first = -count if above else rows
            for i in range(count):
                place = 2 * cols * inputs + cols * (count * part + i)
                to = cell(first + i, 0)
                cots[to : to + cols, :] = ref[place : place + cols, :].astype(F32)
            for place, j in zip(corners[0][1][part] + corners[1][1][part], columns):
                corner = corner_ref[place : place + CORNER, :].astype(F32)
                corner = corner[CORNER - 8 :] if above else corner[:8]
                for i in range(count):
                    line = 8 - count + i if above else i
                    cots[cell(first + i, j) : cell(first + i, j) + 1, :] = corner[line : line + 1]
        cot_ref[:, 128 * part : 128 * part + 128] = cots[GUARD : GUARD + size, :].astype(BF16)


def level(shape, devices, parts, second, names, *refs):
    rows, cols, chan_in, mid, factor, whole = shape
    refs = dict(zip(names, refs))
    x_ref, terms_ref = refs["x"], refs["terms"]
    flat, k_a, k_b, f_a, f_b = (refs[name] for name in ("flat", "k_a", "k_b", "f_a", "f_b"))
    win_delta, t_one, t_two = (refs[name] for name in ("win_delta", "t_one", "t_two"))
    pitch = cols + LEFT
    height = rows + ABOVE + BELOW
    size = height * pitch
    far, near, core, lon = devices.sizes
    count = 1 if whole else devices.count
    share = [9 * c * mid // 128 // count for c in (chan_in, mid, mid)]
    begin = [0, share[0], share[0] + share[1]]
    lat_at, mine = devices.place()
    f_a[...] = jnp.zeros_like(f_a)
    f_b[...] = jnp.zeros_like(f_b)

    def unpack(which, channels):
        n = share[which]
        for i, (c, m, o) in enumerate(parts):
            plane = refs["plane", i]
            for f in range(plane.shape[0]):
                owner = 0 if whole else devices.index(devices.moved(mine, (f, m, c, o), -1))
                lo = begin[which] // 16 * 16
                hi = -(-(begin[which] + n) // 16) * 16
                value = plane[f, lo:hi, :].astype(F32)
                flat[pl.ds(owner * n, n), :] = value[begin[which] - lo : begin[which] - lo + n]
        pairs = 9 * channels // 2
        step = 288

        def one(i, _):
            at = i * step
            first = flat[pl.ds(3 * at, step, stride=3), :]
            second = flat[pl.ds(3 * at + 1, step, stride=3), :]
            third = flat[pl.ds(3 * at + 2, step, stride=3), :]
            low = low_lanes(step)
            second_r, third_r = swapped(second), swapped(third)
            k_a[pl.ds(2 * at, step, stride=2), :] = first
            k_b[pl.ds(2 * at, step, stride=2), :] = jnp.where(low, second, second_r)
            k_a[pl.ds(2 * at + 1, step, stride=2), :] = jnp.where(low, second_r, third_r)
            k_b[pl.ds(2 * at + 1, step, stride=2), :] = jnp.where(low, third_r, third)
            return 0

        lax.fori_loop(0, pairs // step, one, 0)

    def tap_rows(tap, part):
        start = (3 * tap[0] + tap[1]) * mid + 128 * part
        return start, start + (HALF if part else 128)

    def forward(target):
        at = 0
        for block in BLOCKS:
            for tap in block:
                if tap is None:
                    target[at : at + HALF, :] = jnp.zeros((HALF, 256), BF16)
                    at += HALF
                    continue
                lo, hi = tap_rows(tap, tap[2])
                target[at : at + hi - lo, 0:128] = k_a[lo:hi, :].astype(BF16)
                target[at : at + hi - lo, 128:256] = k_b[lo:hi, :].astype(BF16)
                at += hi - lo

    def backward(target):
        low = low_lanes(mid)
        for i, block in enumerate(BLOCKS):
            values = []
            for tap in block:
                if tap is None:
                    values.append(jnp.zeros((mid, 128), F32))
                    continue
                lo = (3 * (2 - tap[0]) + 2 - tap[1]) * mid
                source = k_b if tap[2] else k_a
                values.append(source[lo : lo + mid, :])
            value = values[0] if len(values) == 1 else jnp.where(low, values[0], values[1])
            value = value.astype(BF16)
            target[0:mid, 128 * i : 128 * i + 128] = value
            target[mid:256, 128 * i : 128 * i + 128] = value[128:mid]

    def load_kernels():
        unpack(0, chan_in)
        refs["w_one"][:, 0:128] = k_a[0 : 9 * chan_in, :].astype(BF16)
        refs["w_one"][:, 128:256] = k_b[0 : 9 * chan_in, :].astype(BF16)
        empty = jnp.zeros((chan_in, 128), F32)
        low_in = low_lanes(chan_in)
        phases = (
            ((1, 1), None, None, None),
            ((1, 2), (1, 0), None, None),
            ((2, 1), None, (0, 1), None),
            ((2, 2), (2, 0), (0, 2), (0, 0)),
        )
        for i, taps in enumerate(phases):
            a, b = [], []
            for tap in taps:
                if tap is None:
                    a.append(empty)
                    b.append(empty)
                else:
                    lo = (3 * tap[0] + tap[1]) * chan_in
                    a.append(k_a[lo : lo + chan_in, :])
                    b.append(k_b[lo : lo + chan_in, :])
            blocks = (
                a[0],
                a[1],
                jnp.where(low_in, b[0], b[1]),
                a[2],
                a[3],
                jnp.where(low_in, b[2], b[3]),
            )
            for j, block in enumerate(blocks):
                t_one[chan_in * i : chan_in * (i + 1), 128 * j : 128 * j + 128] = block.astype(BF16)
        unpack(1, mid)
        forward(refs["w_two"])
        backward(t_two)
        unpack(2, mid)
        forward(refs["w_three"])
        backward(refs["t_three"])

    first_row = lat_at * rows
    bottom = lax.axis_size("chip") * core * rows - first_row
    low_cell = (jnp.maximum(-first_row, -ABOVE) + ABOVE) * pitch + 8
    high_cell = (jnp.minimum(bottom, rows + BELOW) + ABOVE) * pitch + 8

    def inside(start, n):
        cell = start + lax.broadcasted_iota(jnp.int32, (n, 128), 0)
        return (cell >= low_cell) & (cell < high_cell)

    def store(start, n, left, right, mask):
        if mask:
            keep = inside(start, n)
            left = jnp.where(keep, left, 0.0)
            right = jnp.where(keep, right, 0.0)
        at = pl.multiple_of(start + GUARD, 8)
        f_a[pl.ds(at, n), :] = left
        f_b[pl.ds(at, n), :] = right

    def windows(target, top, under):
        wide = -(-(under - top) * pitch // 6 // 16) * 16

        def one(i, _):
            cell = (top + ABOVE) * pitch + i * wide
            q = cell + GUARD
            low = low_lanes(wide)
            b_0, b_1, b_2 = (f_b[pl.ds(q + s, wide), :] for s in (-1, 0, 1))
            b_3 = f_b[pl.ds(q + 1 + pitch, wide), :]
            out = [f_a[pl.ds(q + s, wide), :] for s in (-1, 0, 1)]
            out += [jnp.where(low, b_0, b_1), jnp.where(low, b_2, b_3)]
            at = pl.multiple_of(cell, 16)
            for j, value in enumerate(out):
                target[pl.ds(at, wide), 128 * j : 128 * j + 128] = value.astype(BF16)
            return 0

        lax.fori_loop(0, 6, one, 0)

    def convolve(source, weights, turned, halo, steps, finish):
        start = (ABOVE - halo) * pitch
        total = (rows + 1 + 2 * halo) * pitch + LEFT
        n = -(-total // steps // 16) * 16
        contract = (((1,), (1,)), ((), ())) if turned else (((1,), (0,)), ((), ()))

        def one(i, _):
            p = pl.multiple_of(start + i * n, 16)
            above = source[pl.ds(pl.multiple_of(p - pitch, 16), n), :]
            here = source[pl.ds(p, n), 0:512]
            below = source[pl.ds(pl.multiple_of(p + pitch, 16), n), :]
            value = lax.dot_general(
                jnp.concatenate([above, here, below], axis=1),
                weights[...],
                contract,
                preferred_element_type=F32,
            )
            finish(p, n, value)
            return 0

        lax.fori_loop(0, steps, one, 0)

    def own(ref, lanes, row_step=0, shift=0, offset=0):
        pieces = []
        for r in range(rows):
            at = offset + (ABOVE + r + row_step) * pitch + LEFT + shift
            pieces.append(ref[at : at + cols, lanes])
        return jnp.concatenate(pieces, axis=0)

    ALL = slice(0, 128)

    def turned_deltas():
        left = own(f_a, ALL, offset=GUARD)
        right = own(f_b, ALL, offset=GUARD)
        return jnp.concatenate([left.T, right.T], axis=0).astype(BF16)

    def pack(which, channels, first=0):
        step = 288

        def one(i, _):
            at = i * step
            even_a = k_a[pl.ds(2 * at, step, stride=2), :]
            even_b = k_b[pl.ds(2 * at, step, stride=2), :]
            odd_a = swapped(k_a[pl.ds(2 * at + 1, step, stride=2), :])
            odd_b = k_b[pl.ds(2 * at + 1, step, stride=2), :]
            low = low_lanes(step)
            flat[pl.ds(3 * at, step, stride=3), :] = even_a
            flat[pl.ds(3 * at + 1, step, stride=3), :] = jnp.where(low, even_b, odd_a)
            flat[pl.ds(3 * at + 2, step, stride=3), :] = jnp.where(low, odd_a, odd_b)
            return 0

        lax.fori_loop(0, 9 * channels // 2 // step, one, 0)
        n = share[which]
        for k in range(count):
            refs["chunk"][k, first : first + n, :] = flat[k * n : (k + 1) * n, :]

    def hand_over():
        for k in range(count):
            f, m, c, o = devices.coords(k)
            place, side = 0, 0
            if not whole:
                f, m, side, o = devices.apart(devices.coords(k), mine)
                place = (m * lon + o) * far + f
            terms_ref[side, place] = refs["chunk"][k].astype(BF16)

    def field_grad(which, source, first):
        turned = turned_deltas()
        for a, blocks in enumerate((FRINGE, MIDDLE, LAST)):
            lanes = slice(0, 128 * len(blocks))
            product = lax.dot_general(
                turned,
                own(source, lanes, a - 1),
                (((1,), (0,)), ((), ())),
                preferred_element_type=F32,
            )
            product = product * factor
            for j, block in enumerate(blocks):
                left = product[0:128, 128 * j : 128 * j + 128].T
                right = product[128:256, 128 * j : 128 * j + 128].T
                at = 0
                for tap in block:
                    if tap is None:
                        continue
                    lo, hi = tap_rows(tap, tap[2])
                    k_a[lo:hi, :] = left[at : at + hi - lo]
                    k_b[lo:hi, :] = right[at : at + hi - lo]
                    at += hi - lo
        pack(which, mid, first)

    def forward_pass():
        load_kernels()
        win_one, win_two, slope, spread, c_ref = (
            refs[name] for name in ("win_one", "win_two", "slope", "spread", "c")
        )
        slope[...] = jnp.zeros_like(slope)

        def convolve_first():
            halo, steps = 4, 2
            start = (ABOVE - halo) * pitch
            total = (rows + 1 + 2 * halo) * pitch + LEFT
            n = -(-total // steps // 16) * 16

            def one(i, _):
                p = pl.multiple_of(start + i * n, 16)
                above = x_ref[pl.ds(pl.multiple_of(p - pitch, 16), n), 384:768]
                here = x_ref[pl.ds(p, n), :]
                value = lax.dot_general(
                    jnp.concatenate([above, here], axis=1),
                    refs["w_one"][...],
                    (((1,), (0,)), ((), ())),
                    preferred_element_type=F32,
                )
                store(p, n, value[:, :128], value[:, 128:], True)
                return 0

            lax.fori_loop(0, steps, one, 0)

        convolve_first()
        windows(win_one, -4, rows + 6)

        def finish_two(p, n, value):
            s = jax.nn.sigmoid(value)
            active = value * s
            slope[pl.ds(p, n), :] = s + active * (1.0 - s)
            store(p, n, active[:, :128], active[:, 128:], True)

        convolve(win_one, refs["w_two"], False, 3, 2, finish_two)
        windows(win_two, -3, rows + 5)

        def finish_three(p, n, value):
            s = jax.nn.sigmoid(value)
            active = value * s
            delta = c_ref[pl.ds(p, n), :].astype(F32) * (s + active * (1.0 - s))
            store(p, n, delta[:, :128], delta[:, 128:], False)
            spread[pl.ds(p, n), :] = active

        convolve(win_two, refs["w_three"], False, 2, 2, finish_three)
        for r in range(rows):
            at = (ABOVE + r) * pitch + LEFT
            refs["features"][r] = spread[at : at + cols, 0:mid].astype(BF16)
        field_grad(2, win_two, share[1])
        windows(win_delta, -2, rows + 4)

        def finish_delta(p, n, value):
            value = value * slope[pl.ds(p, n), :]
            store(p, n, value[:, :128], value[:, 128:], True)

        convolve(win_delta, refs["t_three"], True, 1, 2, finish_delta)
        field_grad(1, win_one, 0)
        hand_over()
        windows(win_delta, -1, rows + 3)

    def backward_pass():
        def finish_back(p, n, value):
            store(p, n, value[:, :128], value[:, 128:], True)

        convolve(win_delta, t_two, True, 0, 2, finish_back)
        turned = turned_deltas()
        for a, (step, lanes) in enumerate(((-1, slice(384, 768)), (0, slice(0, 384)), (0, slice(384, 768)))):
            product = lax.dot_general(
                turned,
                own(x_ref, lanes, step),
                (((1,), (0,)), ((), ())),
                preferred_element_type=F32,
            )
            product = product * factor
            lo = 3 * a * chan_in
            k_a[lo : lo + 3 * chan_in, :] = product[0:128].T
            k_b[lo : lo + 3 * chan_in, :] = product[128:256].T
        pack(0, chan_in)
        hand_over()

        low = low_lanes(rows * cols)

        def four(ref):
            return [own(ref, ALL, r, c, GUARD) for r, c in ((0, 0), (0, 1), (1, 0), (1, 1))]

        a, b = four(f_a), four(f_b)
        around = (a[0], a[1], jnp.where(low, b[0], b[1]), a[2], a[3], jnp.where(low, b[2], b[3]))
        around = jnp.concatenate([value.astype(BF16) for value in around], axis=1)
        for r in range(2):
            wide = 384 * (r + 1)
            product = lax.dot_general(
                around[:, :wide],
                t_one[2 * chan_in * r : 2 * chan_in * (r + 1), :wide],
                (((1,), (1,)), ((), ())),
                preferred_element_type=F32,
            )
            for i in range(rows):
                at = i * cols
                base = (2 * i + r) * 2 * cols
                for c in range(2):
                    spread_in = product[at : at + cols, chan_in * c : chan_in * (c + 1)]
                    refs["image"][pl.ds(base + c, cols, stride=2), :] = spread_in
        for i in range(2 * rows):
            refs["grad_input"][i] = refs["image"][2 * cols * i : 2 * cols * (i + 1), :].astype(BF16)

    if second:
        backward_pass()
    else:
        forward_pass()


VMEM = pl.BlockSpec(memory_space=pltpu.VMEM)
ANY = pl.BlockSpec(memory_space=pl.ANY)


def local(inputs, w_first, w_second, w_third, cotangent):
    devices = Slice()
    rows, cols, mid = cotangent.shape
    chan_in = inputs.shape[2]
    factor = 1.0 / LOSS_CELLS
    far, near, core, lon = devices.sizes
    held = (w_first.shape[0], w_second.shape[0], w_third.shape[0])
    shard = jnp.concatenate([w_first, w_second, w_third]).reshape(-1, 128)
    whole = any(n % 128 for n in held)
    if not whole:
        shard = jnp.pad(shard, ((0, -shard.shape[0] % 16), (0, 0)))
    count = 1 if whole else devices.count

    side_rows, corner_rows = strips(2 * rows, rows)[1], strips(CORNER, CORNER)[1]
    south_rows = 2 * cols * (WEST + BEFORE)
    north_rows = 2 * cols * (EAST + AFTER)
    cost = pl.CostEstimate(flops=0, bytes_accessed=3 * 2**20, transcendentals=0)
    params = pltpu.CompilerParams(vmem_limit_bytes=16 * 2**20)

    def buffers(*sizes):
        return [jax.ShapeDtypeStruct((n, 128), BF16) for n in sizes]

    side, south, north = pl.pallas_call(
        functools.partial(pack_sides, rows, cols),
        out_shape=buffers(side_rows, south_rows, north_rows),
        in_specs=[VMEM] * 2,
        out_specs=[VMEM] * 3,
        scratch_shapes=[pltpu.VMEM((2 * rows * CORNER, 128), F32)],
        compiler_params=params,
        cost_estimate=cost,
    )(inputs, cotangent)
    line = lined(devices, shard)
    south, north = lengthways(south, north)
    side = sideways(side, strips(2 * rows, rows)[0][1][0][0])
    lower, upper = pl.pallas_call(
        functools.partial(pack_corners, rows),
        out_shape=buffers(corner_rows, corner_rows),
        in_specs=[VMEM],
        out_specs=[VMEM] * 2,
        compiler_params=params,
        cost_estimate=cost,
    )(side)
    lower, upper = lengthways(lower, upper)
    line, south, north, side = lax.optimization_barrier((line, south, north, side))
    planes = spread(devices, line)
    size = (rows + ABOVE + BELOW) * (cols + LEFT)
    padded, cot = pl.pallas_call(
        functools.partial(prepare, rows, cols),
        out_shape=(
            jax.ShapeDtypeStruct((size, 6 * chan_in), BF16),
            jax.ShapeDtypeStruct((size, 256), BF16),
        ),
        in_specs=[VMEM] * 7,
        out_specs=(VMEM, VMEM),
        scratch_shapes=[
            pltpu.VMEM(((2 * rows + 40) * (2 * cols + 48), 128), F32),
            pltpu.VMEM((size + 2 * GUARD, 128), F32),
        ],
        compiler_params=pltpu.CompilerParams(vmem_limit_bytes=40 * 2**20),
        cost_estimate=pl.CostEstimate(flops=0, bytes_accessed=12 * 2**20, transcendentals=0),
    )(inputs, cotangent, side, south, north, lower, upper)

    planes[1:], padded, cot = lax.optimization_barrier((planes[1:], padded, cot))
    planes, parts = shared_out(devices, planes)
    if whole:
        chunks = jnp.stack(planes).reshape(devices.count, -1)
        chunks = jnp.take(chunks, jnp.argsort(order(devices, -1)), axis=0)
        pieces = jnp.split(chunks, (held[0], held[0] + held[1]), axis=1)
        chunks = jnp.concatenate([piece.reshape(-1) for piece in pieces])
        planes, parts = [chunks.reshape(1, -1, 128)], [(0, 0, 0)]
    deep = -(-(2 * held[1]) // 2048) * 16, -(-held[0] // 2048) * 16
    if whole:
        deep = 2 * held[1] * devices.count // 128, held[0] * devices.count // 128
    sides = 1 if whole else core
    field_shape = (size + 2 * GUARD, 128)
    shape = (rows, cols, chan_in, mid, factor, whole)
    wide = 128 * len(BLOCKS)
    shared = {
        "flat": ((9 * mid * mid // 128, 128), F32),
        "k_a": ((9 * mid, 128), F32),
        "k_b": ((9 * mid, 128), F32),
        "f_a": (field_shape, F32),
        "f_b": (field_shape, F32),
    }

    def call(second, ins, outs, scratch):
        scratch = {**scratch, **shared}
        names = list(ins) + list(outs) + list(scratch)
        results = pl.pallas_call(
            functools.partial(level, shape, devices, () if second else parts, second, names),
            out_shape=[jax.ShapeDtypeStruct(*out) for out in outs.values()],
            in_specs=[VMEM] * len(ins),
            out_specs=[VMEM] * len(outs),
            scratch_shapes=[pltpu.VMEM(*kind) for kind in scratch.values()],
            compiler_params=pltpu.CompilerParams(vmem_limit_bytes=40 * 2**20),
            cost_estimate=pl.CostEstimate(
                flops=2 * 10**9 if second else 5 * 10**9,
                bytes_accessed=12 * 2**20,
                transcendentals=10**6,
            ),
        )(*ins.values())
        return dict(zip(outs, results))

    ins = {"x": padded, "c": cot}
    for i, plane in enumerate(planes):
        ins["plane", i] = plane
    done = call(
        False,
        ins,
        {
            "features": ((rows, cols, mid), BF16),
            "terms": ((sides, count // sides, deep[0], 128), BF16),
            "win_delta": ((size, 640), BF16),
            "t_one": ((4 * chan_in, 768), BF16),
            "t_two": ((256, wide), BF16),
        },
        {
            "chunk": ((count, deep[0], 128), F32),
            "w_one": ((9 * chan_in, 256), BF16),
            "w_two": ((wide, 256), BF16),
            "w_three": ((wide, 256), BF16),
            "t_three": ((256, wide), BF16),
            "slope": ((size, 256), F32),
            "spread": ((size, 256), F32),
            "win_one": ((size, 640), BF16),
            "win_two": ((size, 640), BF16),
        },
    )
    features = done["features"]

    def reduced(terms, *sizes):
        if whole:
            cuts = [sum(sizes[:i]) * devices.count for i in range(1, len(sizes))]
            pieces = jnp.split(terms.reshape(-1), cuts)
            terms = [piece.reshape(devices.count, -1) for piece in pieces]
            terms = jnp.take(jnp.concatenate(terms, axis=1), order(devices, 1), axis=0)
            terms = terms.reshape(core, devices.count // core, 1, -1)
        return halved(devices, terms)

    upper = reduced(done["terms"], held[1], held[2])
    upper, win_delta = lax.optimization_barrier((upper, done["win_delta"]))
    done["win_delta"] = win_delta
    upper = planar(devices, upper)
    done = call(
        True,
        {"x": padded, **{name: done[name] for name in ("win_delta", "t_one", "t_two")}},
        {
            "grad_input": ((2 * rows, 2 * cols, chan_in), BF16),
            "terms": ((sides, count // sides, deep[1], 128), BF16),
        },
        {
            "chunk": ((count, deep[1], 128), F32),
            "image": ((4 * rows * cols, 128), F32),
        },
    )
    upper, lower = lax.optimization_barrier((upper, reduced(done["terms"], held[0])))
    lower = planar(devices, lower)
    cut = upper.shape[-2] if not whole else 0
    total = linear(devices, jnp.concatenate([upper, lower], axis=-1 if whole else -2))
    if whole:
        grad_second, grad_third, grad_first = jnp.split(
            total.reshape(-1), (held[1], held[1] + held[2])
        )
    else:
        grad_first = total[cut:].reshape(-1)[: held[0]]
        total = total[:cut].reshape(-1)
        grad_second, grad_third = total[: held[1]], total[held[1] : held[1] + held[2]]
    return (features, done["grad_input"], grad_first, grad_second, grad_third)


def solution(mesh):
    lat, lon = mesh.shape["lat"], mesh.shape["lon"]
    core = 2 if lat % 2 == 0 else 1
    chips = jax.sharding.Mesh(mesh.devices.reshape(lat // core, core, lon), BOTH)
    tile = P(LAT, "lon", None)
    flat = P(BOTH)
    return jax.shard_map(
        local,
        mesh=chips,
        in_specs=(tile, flat, flat, flat, tile),
        out_specs=(tile, tile, flat, flat, flat),
        check_vma=False,
    )
```

```python
import functools

import jax
import jax.numpy as jnp
from jax import lax
from jax.experimental import pallas as pl
from jax.experimental.pallas import tpu as pltpu
from jax.sharding import PartitionSpec as P

LOSS_CELLS = 1024
LAT = ("chip", "core")
BOTH = ("chip", "core", "lon")
F32 = jnp.float32
BF16 = jnp.bfloat16


class Slice:
    def __init__(self):
        chip, core, lon = (lax.axis_size(axis) for axis in BOTH)
        near = 2 if chip % 2 == 0 else 1
        self.sizes = (chip // near, near, core, lon)
        self.count = chip * core * lon

    def place(self):
        lat = lax.axis_index("chip") * self.sizes[2] + lax.axis_index("core")
        return lat, self.coords(lat * self.sizes[3] + lax.axis_index("lon"))

    def coords(self, index):
        out = []
        for size in reversed(self.sizes):
            if isinstance(index, int):
                out.append(index % size)
                index = index // size
            else:
                out.append(lax.rem(index, size))
                index = lax.div(index, size)
        return tuple(reversed(out))

    def index(self, coords):
        total = 0
        for at, size in zip(coords, self.sizes):
            total = total * size + at
        return total

    def moved(self, coords, steps, sign=1):
        out = []
        for at, by, size in zip(coords, steps, self.sizes):
            if size & (size - 1) == 0:
                out.append(at ^ by)
            else:
                to = at + sign * by + size
                out.append(to % size if isinstance(to, int) else lax.rem(to, size))
        return tuple(out)

    def apart(self, coords, origin):
        out = []
        for to, at, size in zip(coords, origin, self.sizes):
            out.append(at ^ to if size & (size - 1) == 0 else lax.rem(to - at + size, size))
        return tuple(out)

    def send(self, value, steps):
        pairs = []
        for source in range(self.count):
            pairs.append((source, self.index(self.moved(self.coords(source), steps))))
        return lax.ppermute(value, BOTH, pairs)


def lined(devices, shard):
    far = devices.sizes[0]
    return jnp.stack([shard] + [devices.send(shard, (f, 0, 0, 0)) for f in range(1, far)])


def spread(devices, line):
    far, near, core, lon = devices.sizes
    planes = []
    for n in range(near):
        for o in range(lon):
            planes.append(line if n == o == 0 else devices.send(line, (0, n, 0, o)))
    return planes


def shared_out(devices, planes):
    far, near, core, lon = devices.sizes
    out, parts = [], []
    for c in range(core):
        for n in range(near):
            for o in range(lon):
                plane = planes[n * lon + o]
                out.append(devices.send(plane, (0, 0, c, 0)) if c else plane)
                parts.append((c, n, o))
    return out, parts


def halved(devices, chunks):
    half = chunks[0].astype(F32)
    for c in range(1, chunks.shape[0]):
        half = half + devices.send(chunks[c], (0, 0, c, 0)).astype(F32)
    return half.astype(BF16)


def order(devices, sign):
    far, near, core, lon = devices.sizes
    mine = devices.place()[1]
    places = []
    for c in range(core):
        for n in range(near):
            for o in range(lon):
                for f in range(far):
                    places.append(devices.index(devices.moved(mine, (f, n, c, o), sign)))
    return jnp.stack(places)


def total_of(terms):
    total = terms[0].astype(F32)
    for term in terms[1:]:
        total = total + term.astype(F32)
    return total


def planar(devices, half):
    far, near, core, lon = devices.sizes
    half = half.reshape(near * lon, far, *half.shape[1:])
    terms = []
    for n in range(near):
        for o in range(lon):
            part = half[n * lon + o]
            terms.append(part if n == o == 0 else devices.send(part, (0, n, 0, o)))
    return total_of(terms).astype(BF16)


def linear(devices, line):
    far = devices.sizes[0]
    return [line[0]] + [devices.send(line[f], (f, 0, 0, 0)) for f in range(1, far)]


WEST, EAST = 9, 10
BEFORE, AFTER = 2, 3
CORNER = 16


def strips(inputs_high, cots_high):
    side, at = [], 0
    for inputs, cots in ((WEST, BEFORE), (EAST, AFTER)):
        columns = [at + inputs_high * j for j in range(inputs)]
        at += inputs_high * inputs
        parts = [[at + cots_high * (cots * part + j) for j in range(cots)] for part in range(2)]
        at += 2 * cots_high * cots
        side.append((columns, parts))
    return side, at


def halves(value):
    return value[..., :128], jnp.concatenate([value[..., 128:], value[..., 128:]], axis=-1)


def pack_sides(rows, cols, x_ref, c_ref, side_ref, south_ref, north_ref, strip):
    west, east = strips(2 * rows, rows)[0]

    def columns(value, wanted, places):
        high = value.shape[0]
        strip[: high * CORNER, :] = value.astype(F32).reshape(high * CORNER, 128)
        for j, place in zip(wanted, places):
            side_ref[place : place + high, :] = strip[pl.ds(j, high, stride=CORNER), :].astype(BF16)

    columns(x_ref[:, 2 * cols - CORNER :, :], range(CORNER - WEST, CORNER), west[0])
    columns(x_ref[:, :CORNER, :], range(EAST), east[0])
    parts = halves(c_ref[...])
    for part in range(2):
        columns(parts[part][:, cols - CORNER :], range(CORNER - BEFORE, CORNER), west[1][part])
        columns(parts[part][:, :CORNER], range(AFTER), east[1][part])
    for ref, inputs, cots, x_row, c_row in (
        (south_ref, WEST, BEFORE, 2 * rows - WEST, rows - BEFORE),
        (north_ref, EAST, AFTER, 0, 0),
    ):
        for i in range(inputs):
            ref[2 * cols * i : 2 * cols * (i + 1), :] = x_ref[x_row + i]
        at = 2 * cols * inputs
        for part in range(2):
            for i in range(cots):
                ref[at : at + cols, :] = parts[part][c_row + i]
                at += cols


def pack_corners(rows, side_ref, lower_ref, upper_ref):
    for side, corner in zip(strips(2 * rows, rows)[0], strips(CORNER, CORNER)[0]):
        strip = [(2 * rows, *pair) for pair in zip(side[0], corner[0])]
        for part in range(2):
            strip += [(rows, *pair) for pair in zip(side[1][part], corner[1][part])]
        for high, place, to in strip:
            end = place + high
            lower_ref[to : to + CORNER, :] = side_ref[end - CORNER : end, :]
            upper_ref[to : to + CORNER, :] = side_ref[place : place + CORNER, :]


def sideways(packed, cut):
    count = lax.axis_size("lon")
    east = [(i, (i + 1) % count) for i in range(count)]
    west = [(i, (i - 1) % count) for i in range(count)]
    if count == 2:
        return lax.ppermute(packed, "lon", east)
    before = lax.ppermute(packed[:cut], "lon", east)
    after = lax.ppermute(packed[cut:], "lon", west)
    return jnp.concatenate([before, after], axis=0)


def lengthways(south, north):
    count = lax.axis_size("chip") * lax.axis_size("core")
    down = [(i, i + 1) for i in range(count - 1)]
    up = [(i + 1, i) for i in range(count - 1)]
    return lax.ppermute(south, LAT, down), lax.ppermute(north, LAT, up)


LEFT = 16
ABOVE = 5
BELOW = 7
GUARD = 8
HALF = 64

FRINGE = (((0, 0, 0),), ((0, 1, 0),), ((0, 2, 0),), ((0, 0, 1), (0, 1, 1)), ((0, 2, 1), (1, 2, 1)))
MIDDLE = (((1, 0, 0),), ((1, 1, 0),), ((1, 2, 0),), ((1, 0, 1), (1, 1, 1)))
LAST = (((2, 0, 0),), ((2, 1, 0),), ((2, 2, 0),), ((2, 0, 1), (2, 1, 1)), ((2, 2, 1), None))
BLOCKS = FRINGE + MIDDLE + LAST


def low_lanes(rows):
    return lax.broadcasted_iota(jnp.int32, (rows, 128), 1) < HALF


def swapped(value):
    return pltpu.roll(value, HALF, 1)


def prepare(
    rows, cols, x_ref, c_ref, side_ref, south_ref, north_ref, lower_ref, upper_ref,
    windows_ref, cot_ref, wide, cots,
):
    pitch = cols + LEFT
    height = rows + ABOVE + BELOW
    size = height * pitch
    span = 2 * cols + 48
    base_row, base_col = 20, 24
    wide[...] = jnp.zeros_like(wide)
    cots[...] = jnp.zeros_like(cots)
    side = strips(2 * rows, rows)[0]
    corners = strips(CORNER, CORNER)[0]
    columns = [*range(-WEST, 0), *range(2 * cols, 2 * cols + EAST)]

    def at(i, j):
        return (i + base_row) * span + base_col + j

    def own(i, _):
        wide[pl.ds(pl.multiple_of(at(i, 0), 8), 2 * cols), :] = x_ref[i].astype(F32)
        return 0

    lax.fori_loop(0, 2 * rows, own, 0)
    for j, place in zip(columns, side[0][0] + side[1][0]):
        strip = side_ref[place : place + 2 * rows, :].astype(F32)
        wide[pl.ds(at(0, j), 2 * rows, stride=span), :] = strip
    for ref, corner_ref, inputs, top, first in (
        (south_ref, lower_ref, WEST, -WEST, -CORNER),
        (north_ref, upper_ref, EAST, 2 * rows, 2 * rows),
    ):
        for i in range(inputs):
            edge = ref[2 * cols * i : 2 * cols * (i + 1), :].astype(F32)
            wide[at(top + i, 0) : at(top + i, 0) + 2 * cols, :] = edge
        for place, j in zip(corners[0][0] + corners[1][0], columns):
            corner = corner_ref[place : place + CORNER, :].astype(F32)
            wide[pl.ds(at(first, j), CORNER, stride=span), :] = corner

    def window(k, _):
        for parity in range(2):
            row = 2 * (k - ABOVE) + parity + base_row
            for tap in range(3):
                base = row * span + base_col - 1 + tap
                mid = wide[pl.ds(base, cols, stride=2), :]
                before = wide[pl.ds(base - 16, 8, stride=2), :]
                after = wide[pl.ds(base - 2 * span + 2 * cols, 8, stride=2), :]
                lane = (3 * parity + tap) * 128
                cells = jnp.concatenate([after, before, mid], axis=0).astype(BF16)
                windows_ref[pl.ds(pl.multiple_of(k * pitch, 16), pitch), lane : lane + 128] = cells
        return 0

    lax.fori_loop(0, height, window, 0)

    def cell(i, j):
        return GUARD + (i + ABOVE) * pitch + LEFT + j

    columns = [*range(-BEFORE, 0), *range(cols, cols + AFTER)]
    parts = halves(c_ref[...])
    for part in range(2):
        for i in range(rows):
            cots[cell(i, 0) : cell(i, cols), :] = parts[part][i].astype(F32)
        for j, place in zip(columns, side[0][1][part] + side[1][1][part]):
            strip = side_ref[place : place + rows, :].astype(F32)
            cots[pl.ds(cell(0, j), rows, stride=pitch), :] = strip
        for ref, corner_ref, inputs, count, above in (
            (south_ref, lower_ref, WEST, BEFORE, True),
            (north_ref, upper_ref, EAST, AFTER, False),
        ):
            first = -count if above else rows
            for i in range(count):
                place = 2 * cols * inputs + cols * (count * part + i)
                to = cell(first + i, 0)
                cots[to : to + cols, :] = ref[place : place + cols, :].astype(F32)
            for place, j in zip(corners[0][1][part] + corners[1][1][part], columns):
                corner = corner_ref[place : place + CORNER, :].astype(F32)
                corner = corner[CORNER - 8 :] if above else corner[:8]
                for i in range(count):
                    line = 8 - count + i if above else i
                    cots[cell(first + i, j) : cell(first + i, j) + 1, :] = corner[line : line + 1]
        cot_ref[:, 128 * part : 128 * part + 128] = cots[GUARD : GUARD + size, :].astype(BF16)


def unfold(sections, count, *refs):
    terms, outs = refs[:count], refs[count : count + len(sections)]
    total, k_a, k_b = refs[count + len(sections) :]
    value = terms[0][...].astype(F32)
    for term in terms[1:]:
        value = value + term[...].astype(F32)
    total[...] = value
    for (first, n), out in zip(sections, outs):
        half = n // 3
        low = low_lanes(half)
        pair = total[first + 2 * half : first + n, :]
        turned = swapped(pair)
        k_a[0 : 2 * half, :] = total[first : first + 2 * half, :]
        k_b[0:half, :] = jnp.where(low, pair, turned)
        k_b[half : 2 * half, :] = jnp.where(low, turned, pair)
        even_a = k_a[pl.ds(0, half, stride=2), :]
        even_b = k_b[pl.ds(0, half, stride=2), :]
        odd_a = swapped(k_a[pl.ds(1, half, stride=2), :])
        odd_b = k_b[pl.ds(1, half, stride=2), :]
        out[pl.ds(0, half, stride=3), :] = even_a
        out[pl.ds(1, half, stride=3), :] = jnp.where(low, even_b, odd_a)
        out[pl.ds(2, half, stride=3), :] = jnp.where(low, odd_a, odd_b)


def level(shape, devices, parts, second, names, *refs):
    rows, cols, chan_in, mid, factor, whole = shape
    refs = dict(zip(names, refs))
    x_ref, terms_ref = refs["x"], refs["terms"]
    flat, k_a, k_b, f_a, f_b = (refs[name] for name in ("flat", "k_a", "k_b", "f_a", "f_b"))
    win_delta = refs["win_delta"]
    if second:
        t_one, t_two = refs["t_one"], refs["t_two"]
    pitch = cols + LEFT
    height = rows + ABOVE + BELOW
    size = height * pitch
    far, near, core, lon = devices.sizes
    count = 1 if whole else devices.count
    share = [9 * c * mid // 128 // count for c in (chan_in, mid, mid)]
    begin = [0, share[0], share[0] + share[1]]
    lat_at, mine = devices.place()

    def clear():
        head, tail = GUARD + pitch, GUARD + (ABOVE + rows + 5) * pitch
        for field in (f_a, f_b):
            field[0:head, :] = jnp.zeros((head, 128), F32)
            field[tail:, :] = jnp.zeros((field.shape[0] - tail, 128), F32)

    def unpack(which, channels):
        n = share[which]
        for i, (c, m, o) in enumerate(parts):
            plane = refs["plane", i]
            for f in range(plane.shape[0]):
                owner = 0 if whole else devices.index(devices.moved(mine, (f, m, c, o), -1))
                lo = begin[which] // 16 * 16
                hi = -(-(begin[which] + n) // 16) * 16
                value = plane[f, lo:hi, :].astype(F32)
                flat[pl.ds(owner * n, n), :] = value[begin[which] - lo : begin[which] - lo + n]
        pairs = 9 * channels // 2
        step = 288

        def one(i, _):
            at = i * step
            first = flat[pl.ds(3 * at, step, stride=3), :]
            second = flat[pl.ds(3 * at + 1, step, stride=3), :]
            third = flat[pl.ds(3 * at + 2, step, stride=3), :]
            low = low_lanes(step)
            second_r, third_r = swapped(second), swapped(third)
            k_a[pl.ds(2 * at, step, stride=2), :] = first
            k_b[pl.ds(2 * at, step, stride=2), :] = jnp.where(low, second, second_r)
            k_a[pl.ds(2 * at + 1, step, stride=2), :] = jnp.where(low, second_r, third_r)
            k_b[pl.ds(2 * at + 1, step, stride=2), :] = jnp.where(low, third_r, third)
            return 0

        lax.fori_loop(0, pairs // step, one, 0)

    def tap_rows(tap, part):
        start = (3 * tap[0] + tap[1]) * mid + 128 * part
        return start, start + (HALF if part else 128)

    def forward(target):
        at = 0
        for block in BLOCKS:
            for tap in block:
                if tap is None:
                    target[at : at + HALF, :] = jnp.zeros((HALF, 256), BF16)
                    at += HALF
                    continue
                lo, hi = tap_rows(tap, tap[2])
                target[at : at + hi - lo, 0:128] = k_a[lo:hi, :].astype(BF16)
                target[at : at + hi - lo, 128:256] = k_b[lo:hi, :].astype(BF16)
                at += hi - lo

    def backward(target):
        low = low_lanes(mid)
        for i, block in enumerate(BLOCKS):
            values = []
            for tap in block:
                if tap is None:
                    values.append(jnp.zeros((mid, 128), F32))
                    continue
                lo = (3 * (2 - tap[0]) + 2 - tap[1]) * mid
                source = k_b if tap[2] else k_a
                values.append(source[lo : lo + mid, :])
            value = values[0] if len(values) == 1 else jnp.where(low, values[0], values[1])
            value = value.astype(BF16)
            target[0:mid, 128 * i : 128 * i + 128] = value
            target[mid:256, 128 * i : 128 * i + 128] = value[128:mid]

    def load_kernels():
        unpack(0, chan_in)
        refs["w_one"][:, 0:128] = k_a[0 : 9 * chan_in, :].astype(BF16)
        refs["w_one"][:, 128:256] = k_b[0 : 9 * chan_in, :].astype(BF16)
        unpack(1, mid)
        forward(refs["w_two"])
        unpack(2, mid)
        forward(refs["w_three"])
        backward(refs["t_three"])

    def load_turned():
        unpack(0, chan_in)
        empty = jnp.zeros((chan_in, 128), F32)
        low_in = low_lanes(chan_in)
        phases = (
            ((1, 1), None, None, None),
            ((1, 2), (1, 0), None, None),
            ((2, 1), None, (0, 1), None),
            ((2, 2), (2, 0), (0, 2), (0, 0)),
        )
        for i, taps in enumerate(phases):
            a, b = [], []
            for tap in taps:
                if tap is None:
                    a.append(empty)
                    b.append(empty)
                else:
                    lo = (3 * tap[0] + tap[1]) * chan_in
                    a.append(k_a[lo : lo + chan_in, :])
                    b.append(k_b[lo : lo + chan_in, :])
            blocks = (
                a[0],
                a[1],
                jnp.where(low_in, b[0], b[1]),
                a[2],
                a[3],
                jnp.where(low_in, b[2], b[3]),
            )
            for j, block in enumerate(blocks):
                t_one[chan_in * i : chan_in * (i + 1), 128 * j : 128 * j + 128] = block.astype(BF16)
        unpack(1, mid)
        backward(t_two)

    first_row = lat_at * rows
    bottom = lax.axis_size("chip") * core * rows - first_row
    low_cell = (jnp.maximum(-first_row, -ABOVE) + ABOVE) * pitch + 8
    high_cell = (jnp.minimum(bottom, rows + BELOW) + ABOVE) * pitch + 8

    def inside(start, n):
        cell = start + lax.broadcasted_iota(jnp.int32, (n, 128), 0)
        return (cell >= low_cell) & (cell < high_cell)

    def store(start, n, left, right, mask):
        if mask:
            keep = inside(start, n)
            left = jnp.where(keep, left, 0.0)
            right = jnp.where(keep, right, 0.0)
        at = pl.multiple_of(start + GUARD, 8)
        f_a[pl.ds(at, n), :] = left
        f_b[pl.ds(at, n), :] = right

    def windows(target, top, under, f_a=f_a, f_b=f_b):
        wide = -(-(under - top) * pitch // 6 // 16) * 16

        def one(i, _):
            cell = (top + ABOVE) * pitch + i * wide
            q = cell + GUARD
            low = low_lanes(wide)
            b_0, b_1, b_2 = (f_b[pl.ds(q + s, wide), :] for s in (-1, 0, 1))
            b_3 = f_b[pl.ds(q + 1 + pitch, wide), :]
            out = [f_a[pl.ds(q + s, wide), :] for s in (-1, 0, 1)]
            out += [jnp.where(low, b_0, b_1), jnp.where(low, b_2, b_3)]
            at = pl.multiple_of(cell, 16)
            for j, value in enumerate(out):
                target[pl.ds(at, wide), 128 * j : 128 * j + 128] = value.astype(BF16)
            return 0

        lax.fori_loop(0, 6, one, 0)

    def convolve(source, weights, turned, halo, steps, finish):
        start = (ABOVE - halo) * pitch
        total = (rows + 1 + 2 * halo) * pitch + LEFT
        n = -(-total // steps // 16) * 16
        contract = (((1,), (1,)), ((), ())) if turned else (((1,), (0,)), ((), ()))

        def one(i, _):
            p = pl.multiple_of(start + i * n, 16)
            above = source[pl.ds(pl.multiple_of(p - pitch, 16), n), :]
            here = source[pl.ds(p, n), 0:512]
            below = source[pl.ds(pl.multiple_of(p + pitch, 16), n), :]
            value = lax.dot_general(
                jnp.concatenate([above, here, below], axis=1),
                weights[...],
                contract,
                preferred_element_type=F32,
            )
            finish(p, n, value)
            return 0

        lax.fori_loop(0, steps, one, 0)

    def own(ref, lanes, row_step=0, shift=0, offset=0):
        pieces = []
        for r in range(rows):
            at = offset + (ABOVE + r + row_step) * pitch + LEFT + shift
            pieces.append(ref[at : at + cols, lanes])
        return jnp.concatenate(pieces, axis=0)

    ALL = slice(0, 128)

    def turned_deltas():
        left = own(f_a, ALL, offset=GUARD)
        right = own(f_b, ALL, offset=GUARD)
        return jnp.concatenate([left.T, right.T], axis=0).astype(BF16)

    def pack(which, channels, first=0):
        if not whole:
            n = share[which]
            half = n // 3
            low = low_lanes(half)
            for k in range(count):
                at = 2 * half * k
                refs["chunk"][k, first : first + 2 * half, :] = k_a[at : at + 2 * half, :]
                pair = jnp.where(low, k_b[at : at + half, :], k_b[at + half : at + 2 * half, :])
                refs["chunk"][k, first + 2 * half : first + n, :] = pair
            return
        step = 288

        def one(i, _):
            at = i * step
            even_a = k_a[pl.ds(2 * at, step, stride=2), :]
            even_b = k_b[pl.ds(2 * at, step, stride=2), :]
            odd_a = swapped(k_a[pl.ds(2 * at + 1, step, stride=2), :])
            odd_b = k_b[pl.ds(2 * at + 1, step, stride=2), :]
            low = low_lanes(step)
            flat[pl.ds(3 * at, step, stride=3), :] = even_a
            flat[pl.ds(3 * at + 1, step, stride=3), :] = jnp.where(low, even_b, odd_a)
            flat[pl.ds(3 * at + 2, step, stride=3), :] = jnp.where(low, odd_a, odd_b)
            return 0

        lax.fori_loop(0, 9 * channels // 2 // step, one, 0)
        n = share[which]
        for k in range(count):
            refs["chunk"][k, first : first + n, :] = flat[k * n : (k + 1) * n, :]

    def hand_over():
        for k in range(count):
            f, m, c, o = devices.coords(k)
            place, side = 0, 0
            if not whole:
                f, m, side, o = devices.apart(devices.coords(k), mine)
                place = (m * lon + o) * far + f
            terms_ref[side, place] = refs["chunk"][k].astype(BF16)

    def field_grad(which, source, first):
        turned = turned_deltas()
        for a, blocks in enumerate((FRINGE, MIDDLE, LAST)):
            lanes = slice(0, 128 * len(blocks))
            product = lax.dot_general(
                turned,
                own(source, lanes, a - 1),
                (((1,), (0,)), ((), ())),
                preferred_element_type=F32,
            )
            product = product * factor
            for j, block in enumerate(blocks):
                left = product[0:128, 128 * j : 128 * j + 128].T
                right = product[128:256, 128 * j : 128 * j + 128].T
                at = 0
                for tap in block:
                    if tap is None:
                        continue
                    lo, hi = tap_rows(tap, tap[2])
                    k_a[lo:hi, :] = left[at : at + hi - lo]
                    k_b[lo:hi, :] = right[at : at + hi - lo]
                    at += hi - lo
        pack(which, mid, first)

    def forward_pass():
        load_kernels()
        win_one, win_two, slope, spread, c_ref = (
            refs[name] for name in ("win_one", "win_two", "slope", "spread", "c")
        )
        clear()

        def convolve_first():
            halo, steps = 4, 2
            start = (ABOVE - halo) * pitch
            total = (rows + 1 + 2 * halo) * pitch + LEFT
            n = -(-total // steps // 16) * 16

            def one(i, _):
                p = pl.multiple_of(start + i * n, 16)
                above = x_ref[pl.ds(pl.multiple_of(p - pitch, 16), n), 384:768]
                here = x_ref[pl.ds(p, n), :]
                value = lax.dot_general(
                    jnp.concatenate([above, here], axis=1),
                    refs["w_one"][...],
                    (((1,), (0,)), ((), ())),
                    preferred_element_type=F32,
                )
                store(p, n, value[:, :128], value[:, 128:], True)
                return 0

            lax.fori_loop(0, steps, one, 0)

        convolve_first()
        windows(win_one, -4, rows + 6)

        def finish_two(p, n, value):
            s = jax.nn.sigmoid(value)
            active = value * s
            slope[pl.ds(p, n), :] = s + active * (1.0 - s)
            store(p, n, active[:, :128], active[:, 128:], True)

        convolve(win_one, refs["w_two"], False, 3, 2, finish_two)
        windows(win_two, -3, rows + 5)

        def finish_three(p, n, value):
            s = jax.nn.sigmoid(value)
            active = value * s
            delta = c_ref[pl.ds(p, n), :].astype(F32) * (s + active * (1.0 - s))
            store(p, n, delta[:, :128], delta[:, 128:], False)
            spread[pl.ds(p, n), :] = active

        convolve(win_two, refs["w_three"], False, 2, 2, finish_three)
        for r in range(rows):
            at = (ABOVE + r) * pitch + LEFT
            refs["features"][r] = spread[at : at + cols, 0:mid].astype(BF16)
        field_grad(2, win_two, share[1])
        windows(win_delta, -2, rows + 4)

        def finish_delta(p, n, value):
            value = value * slope[pl.ds(p, n), :]
            store(p, n, value[:, :128], value[:, 128:], True)

        convolve(win_delta, refs["t_three"], True, 1, 2, finish_delta)
        field_grad(1, win_one, 0)
        hand_over()

    def backward_pass():
        load_turned()
        windows(win_delta, -1, rows + 3, refs["d_a"], refs["d_b"])

        def finish_back(p, n, value):
            store(p, n, value[:, :128], value[:, 128:], True)

        convolve(win_delta, t_two, True, 0, 2, finish_back)
        turned = turned_deltas()
        for a, (step, lanes) in enumerate(((-1, slice(384, 768)), (0, slice(0, 384)), (0, slice(384, 768)))):
            product = lax.dot_general(
                turned,
                own(x_ref, lanes, step),
                (((1,), (0,)), ((), ())),
                preferred_element_type=F32,
            )
            product = product * factor
            lo = 3 * a * chan_in
            k_a[lo : lo + 3 * chan_in, :] = product[0:128].T
            k_b[lo : lo + 3 * chan_in, :] = product[128:256].T
        pack(0, chan_in)
        hand_over()

        low = low_lanes(rows * cols)

        def four(ref):
            return [own(ref, ALL, r, c, GUARD) for r, c in ((0, 0), (0, 1), (1, 0), (1, 1))]

        a, b = four(f_a), four(f_b)
        around = (a[0], a[1], jnp.where(low, b[0], b[1]), a[2], a[3], jnp.where(low, b[2], b[3]))
        around = jnp.concatenate([value.astype(BF16) for value in around], axis=1)
        for r in range(2):
            wide = 384 * (r + 1)
            product = lax.dot_general(
                around[:, :wide],
                t_one[2 * chan_in * r : 2 * chan_in * (r + 1), :wide],
                (((1,), (1,)), ((), ())),
                preferred_element_type=F32,
            )
            for i in range(rows):
                at = i * cols
                base = (2 * i + r) * 2 * cols
                for c in range(2):
                    spread_in = product[at : at + cols, chan_in * c : chan_in * (c + 1)]
                    refs["image"][pl.ds(base + c, cols, stride=2), :] = spread_in
        for i in range(2 * rows):
            refs["grad_input"][i] = refs["image"][2 * cols * i : 2 * cols * (i + 1), :].astype(BF16)

    if second:
        backward_pass()
    else:
        forward_pass()


VMEM = pl.BlockSpec(memory_space=pltpu.VMEM)
ANY = pl.BlockSpec(memory_space=pl.ANY)


def local(inputs, w_first, w_second, w_third, cotangent):
    devices = Slice()
    rows, cols, mid = cotangent.shape
    chan_in = inputs.shape[2]
    factor = 1.0 / LOSS_CELLS
    far, near, core, lon = devices.sizes
    held = (w_first.shape[0], w_second.shape[0], w_third.shape[0])
    shard = jnp.concatenate([w_first, w_second, w_third]).reshape(-1, 128)
    whole = any(n % 384 for n in held)
    if not whole:
        shard = jnp.pad(shard, ((0, -shard.shape[0] % 16), (0, 0)))
    count = 1 if whole else devices.count

    side_rows, corner_rows = strips(2 * rows, rows)[1], strips(CORNER, CORNER)[1]
    south_rows = 2 * cols * (WEST + BEFORE)
    north_rows = 2 * cols * (EAST + AFTER)
    cost = pl.CostEstimate(flops=0, bytes_accessed=3 * 2**20, transcendentals=0)
    params = pltpu.CompilerParams(vmem_limit_bytes=16 * 2**20)

    def buffers(*sizes):
        return [jax.ShapeDtypeStruct((n, 128), BF16) for n in sizes]

    side, south, north = pl.pallas_call(
        functools.partial(pack_sides, rows, cols),
        out_shape=buffers(side_rows, south_rows, north_rows),
        in_specs=[VMEM] * 2,
        out_specs=[VMEM] * 3,
        scratch_shapes=[pltpu.VMEM((2 * rows * CORNER, 128), F32)],
        compiler_params=params,
        cost_estimate=cost,
    )(inputs, cotangent)
    line = lined(devices, shard)
    south, north = lengthways(south, north)
    side = sideways(side, strips(2 * rows, rows)[0][1][0][0])
    lower, upper = pl.pallas_call(
        functools.partial(pack_corners, rows),
        out_shape=buffers(corner_rows, corner_rows),
        in_specs=[VMEM],
        out_specs=[VMEM] * 2,
        compiler_params=params,
        cost_estimate=cost,
    )(side)
    lower, upper = lengthways(lower, upper)
    line, south, north, side = lax.optimization_barrier((line, south, north, side))
    planes = spread(devices, line)
    size = (rows + ABOVE + BELOW) * (cols + LEFT)
    padded, cot = pl.pallas_call(
        functools.partial(prepare, rows, cols),
        out_shape=(
            jax.ShapeDtypeStruct((size, 6 * chan_in), BF16),
            jax.ShapeDtypeStruct((size, 256), BF16),
        ),
        in_specs=[VMEM] * 7,
        out_specs=(VMEM, VMEM),
        scratch_shapes=[
            pltpu.VMEM(((2 * rows + 40) * (2 * cols + 48), 128), F32),
            pltpu.VMEM((size + 2 * GUARD, 128), F32),
        ],
        compiler_params=pltpu.CompilerParams(vmem_limit_bytes=40 * 2**20),
        cost_estimate=pl.CostEstimate(flops=0, bytes_accessed=12 * 2**20, transcendentals=0),
    )(inputs, cotangent, side, south, north, lower, upper)

    planes[1:], padded, cot = lax.optimization_barrier((planes[1:], padded, cot))
    planes, parts = shared_out(devices, planes)
    if whole:
        chunks = jnp.stack(planes).reshape(devices.count, -1)
        chunks = jnp.take(chunks, jnp.argsort(order(devices, -1)), axis=0)
        pieces = jnp.split(chunks, (held[0], held[0] + held[1]), axis=1)
        chunks = jnp.concatenate([piece.reshape(-1) for piece in pieces])
        planes, parts = [chunks.reshape(1, -1, 128)], [(0, 0, 0)]
    deep = -(-(2 * held[1]) // 2048) * 16, -(-held[0] // 2048) * 16
    if whole:
        deep = 2 * held[1] * devices.count // 128, held[0] * devices.count // 128
    sides = 1 if whole else core
    field_shape = (size + 2 * GUARD, 128)
    shape = (rows, cols, chan_in, mid, factor, whole)
    wide = 128 * len(BLOCKS)
    shared = {
        "flat": ((9 * mid * mid // 128, 128), F32),
        "k_a": ((9 * mid, 128), F32),
        "k_b": ((9 * mid, 128), F32),
        "f_a": (field_shape, F32),
        "f_b": (field_shape, F32),
    }

    def call(second, ins, outs, scratch):
        scratch = {**scratch, **{name: kind for name, kind in shared.items() if name not in outs}}
        names = list(ins) + list(outs) + list(scratch)
        results = pl.pallas_call(
            functools.partial(level, shape, devices, parts, second, names),
            out_shape=[jax.ShapeDtypeStruct(*out) for out in outs.values()],
            in_specs=[VMEM] * len(ins),
            out_specs=[VMEM] * len(outs),
            scratch_shapes=[pltpu.VMEM(*kind) for kind in scratch.values()],
            compiler_params=pltpu.CompilerParams(vmem_limit_bytes=40 * 2**20),
            cost_estimate=pl.CostEstimate(
                flops=2 * 10**9 if second else 5 * 10**9,
                bytes_accessed=12 * 2**20,
                transcendentals=10**6,
            ),
        )(*ins.values())
        return dict(zip(outs, results))

    kernels = {("plane", i): plane for i, plane in enumerate(planes)}
    ins = {"x": padded, "c": cot, **kernels}
    done = call(
        False,
        ins,
        {
            "features": ((rows, cols, mid), BF16),
            "terms": ((sides, count // sides, deep[0], 128), BF16),
            "f_a": (field_shape, F32),
            "f_b": (field_shape, F32),
        },
        {
            "chunk": ((count, deep[0], 128), F32),
            "w_one": ((9 * chan_in, 256), BF16),
            "w_two": ((wide, 256), BF16),
            "w_three": ((wide, 256), BF16),
            "t_three": ((256, wide), BF16),
            "slope": ((size, 256), F32),
            "spread": ((size, 256), F32),
            "win_one": ((size, 640), BF16),
            "win_two": ((size, 640), BF16),
            "win_delta": ((size, 640), BF16),
        },
    )
    features = done["features"]

    def reduced(terms, *sizes):
        if whole:
            cuts = [sum(sizes[:i]) * devices.count for i in range(1, len(sizes))]
            pieces = jnp.split(terms.reshape(-1), cuts)
            terms = [piece.reshape(devices.count, -1) for piece in pieces]
            terms = jnp.take(jnp.concatenate(terms, axis=1), order(devices, 1), axis=0)
            terms = terms.reshape(core, devices.count // core, 1, -1)
        return halved(devices, terms)

    upper = reduced(done["terms"], held[1], held[2])
    upper, f_a, f_b = lax.optimization_barrier((upper, done["f_a"], done["f_b"]))
    upper = planar(devices, upper)
    done = call(
        True,
        {"x": padded, "d_a": f_a, "d_b": f_b, **kernels},
        {
            "grad_input": ((2 * rows, 2 * cols, chan_in), BF16),
            "terms": ((sides, count // sides, deep[1], 128), BF16),
        },
        {
            "chunk": ((count, deep[1], 128), F32),
            "t_one": ((4 * chan_in, 768), BF16),
            "t_two": ((256, wide), BF16),
            "win_delta": ((size, 640), BF16),
            "image": ((4 * rows * cols, 128), F32),
        },
    )
    upper, lower = lax.optimization_barrier((upper, reduced(done["terms"], held[0])))
    lower = planar(devices, lower)
    terms = linear(devices, jnp.concatenate([upper, lower], axis=-1 if whole else -2))
    if whole:
        grad_second, grad_third, grad_first = jnp.split(
            total_of(terms).reshape(-1), (held[1], held[1] + held[2])
        )
    else:
        depth = upper.shape[-2]
        high = [n // 128 for n in (held[1], held[2], held[0])]
        sections = ((0, high[0]), (high[0], high[1]), (depth, high[2]))
        deepest = max(high)
        totals = pl.pallas_call(
            functools.partial(unfold, sections, len(terms)),
            out_shape=[jax.ShapeDtypeStruct((n, 128), F32) for n in high],
            in_specs=[VMEM] * len(terms),
            out_specs=[VMEM] * 3,
            scratch_shapes=[
                pltpu.VMEM(terms[0].shape, F32),
                pltpu.VMEM((deepest, 128), F32),
                pltpu.VMEM((deepest, 128), F32),
            ],
            compiler_params=params,
            cost_estimate=pl.CostEstimate(flops=0, bytes_accessed=2**19, transcendentals=0),
        )(*terms)
        grad_second, grad_third, grad_first = (total.reshape(-1) for total in totals)
    return (features, done["grad_input"], grad_first, grad_second, grad_third)


def solution(mesh):
    lat, lon = mesh.shape["lat"], mesh.shape["lon"]
    core = 2 if lat % 2 == 0 else 1
    chips = jax.sharding.Mesh(mesh.devices.reshape(lat // core, core, lon), BOTH)
    tile = P(LAT, "lon", None)
    flat = P(BOTH)
    return jax.shard_map(
        local,
        mesh=chips,
        in_specs=(tile, flat, flat, flat, tile),
        out_specs=(tile, tile, flat, flat, flat),
        check_vma=False,
    )
```

```python
import functools

import jax
import jax.numpy as jnp
from jax import lax
from jax.experimental import pallas as pl
from jax.experimental.pallas import tpu as pltpu
from jax.sharding import PartitionSpec as P

LOSS_CELLS = 1024
LAT = ("chip", "core")
BOTH = ("chip", "core", "lon")
F32 = jnp.float32
BF16 = jnp.bfloat16


class Slice:
    def __init__(self):
        chip, core, lon = (lax.axis_size(axis) for axis in BOTH)
        near = 2 if chip % 2 == 0 else 1
        self.sizes = (chip // near, near, core, lon)
        self.count = chip * core * lon

    def place(self):
        lat = lax.axis_index("chip") * self.sizes[2] + lax.axis_index("core")
        return lat, self.coords(lat * self.sizes[3] + lax.axis_index("lon"))

    def coords(self, index):
        out = []
        for size in reversed(self.sizes):
            if isinstance(index, int):
                out.append(index % size)
                index = index // size
            else:
                out.append(lax.rem(index, size))
                index = lax.div(index, size)
        return tuple(reversed(out))

    def index(self, coords):
        total = 0
        for at, size in zip(coords, self.sizes):
            total = total * size + at
        return total

    def moved(self, coords, steps, sign=1):
        out = []
        for at, by, size in zip(coords, steps, self.sizes):
            if size & (size - 1) == 0:
                out.append(at ^ by)
            else:
                to = at + sign * by + size
                out.append(to % size if isinstance(to, int) else lax.rem(to, size))
        return tuple(out)

    def apart(self, coords, origin):
        out = []
        for to, at, size in zip(coords, origin, self.sizes):
            out.append(at ^ to if size & (size - 1) == 0 else lax.rem(to - at + size, size))
        return tuple(out)

    def send(self, value, steps):
        pairs = []
        for source in range(self.count):
            pairs.append((source, self.index(self.moved(self.coords(source), steps))))
        return lax.ppermute(value, BOTH, pairs)


def lined(devices, shard):
    far = devices.sizes[0]
    return jnp.stack([shard] + [devices.send(shard, (f, 0, 0, 0)) for f in range(1, far)])


def spread(devices, line):
    far, near, core, lon = devices.sizes
    planes = []
    for n in range(near):
        for o in range(lon):
            planes.append(line if n == o == 0 else devices.send(line, (0, n, 0, o)))
    return planes


def shared_out(devices, planes):
    far, near, core, lon = devices.sizes
    out, parts = [], []
    for c in range(core):
        for n in range(near):
            for o in range(lon):
                plane = planes[n * lon + o]
                out.append(devices.send(plane, (0, 0, c, 0)) if c else plane)
                parts.append((c, n, o))
    return out, parts


def halved(devices, chunks):
    half = chunks[0].astype(F32)
    for c in range(1, chunks.shape[0]):
        half = half + devices.send(chunks[c], (0, 0, c, 0)).astype(F32)
    return half.astype(BF16)


def order(devices, sign):
    far, near, core, lon = devices.sizes
    mine = devices.place()[1]
    places = []
    for c in range(core):
        for n in range(near):
            for o in range(lon):
                for f in range(far):
                    places.append(devices.index(devices.moved(mine, (f, n, c, o), sign)))
    return jnp.stack(places)


def total_of(terms):
    total = terms[0].astype(F32)
    for term in terms[1:]:
        total = total + term.astype(F32)
    return total


def planar(devices, half):
    far, near, core, lon = devices.sizes
    half = half.reshape(near * lon, far, *half.shape[1:])
    terms = []
    for n in range(near):
        for o in range(lon):
            part = half[n * lon + o]
            terms.append(part if n == o == 0 else devices.send(part, (0, n, 0, o)))
    return total_of(terms).astype(BF16)


def linear(devices, line):
    far = devices.sizes[0]
    return [line[0]] + [devices.send(line[f], (f, 0, 0, 0)) for f in range(1, far)]


WEST, EAST = 9, 10
BEFORE, AFTER = 2, 3
CORNER = 16


def strips(inputs_high, cots_high):
    side, at = [], 0
    for inputs, cots in ((WEST, BEFORE), (EAST, AFTER)):
        columns = [at + inputs_high * j for j in range(inputs)]
        at += inputs_high * inputs
        parts = [[at + cots_high * (cots * part + j) for j in range(cots)] for part in range(2)]
        at += 2 * cots_high * cots
        side.append((columns, parts))
    return side, at


def halves(value):
    return value[..., :128], jnp.concatenate([value[..., 128:], value[..., 128:]], axis=-1)


def pack_sides(rows, cols, x_ref, c_ref, side_ref, south_ref, north_ref, strip):
    west, east = strips(2 * rows, rows)[0]

    def columns(value, wanted, places):
        high = value.shape[0]
        strip[: high * CORNER, :] = value.astype(F32).reshape(high * CORNER, 128)
        for j, place in zip(wanted, places):
            side_ref[place : place + high, :] = strip[pl.ds(j, high, stride=CORNER), :].astype(BF16)

    columns(x_ref[:, 2 * cols - CORNER :, :], range(CORNER - WEST, CORNER), west[0])
    columns(x_ref[:, :CORNER, :], range(EAST), east[0])
    parts = halves(c_ref[...])
    for part in range(2):
        columns(parts[part][:, cols - CORNER :], range(CORNER - BEFORE, CORNER), west[1][part])
        columns(parts[part][:, :CORNER], range(AFTER), east[1][part])
    for ref, inputs, cots, x_row, c_row in (
        (south_ref, WEST, BEFORE, 2 * rows - WEST, rows - BEFORE),
        (north_ref, EAST, AFTER, 0, 0),
    ):
        for i in range(inputs):
            ref[2 * cols * i : 2 * cols * (i + 1), :] = x_ref[x_row + i]
        at = 2 * cols * inputs
        for part in range(2):
            for i in range(cots):
                ref[at : at + cols, :] = parts[part][c_row + i]
                at += cols


def pack_corners(rows, side_ref, lower_ref, upper_ref):
    for side, corner in zip(strips(2 * rows, rows)[0], strips(CORNER, CORNER)[0]):
        strip = [(2 * rows, *pair) for pair in zip(side[0], corner[0])]
        for part in range(2):
            strip += [(rows, *pair) for pair in zip(side[1][part], corner[1][part])]
        for high, place, to in strip:
            end = place + high
            lower_ref[to : to + CORNER, :] = side_ref[end - CORNER : end, :]
            upper_ref[to : to + CORNER, :] = side_ref[place : place + CORNER, :]


def sideways(packed, cut):
    count = lax.axis_size("lon")
    east = [(i, (i + 1) % count) for i in range(count)]
    west = [(i, (i - 1) % count) for i in range(count)]
    if count == 2:
        return lax.ppermute(packed, "lon", east)
    before = lax.ppermute(packed[:cut], "lon", east)
    after = lax.ppermute(packed[cut:], "lon", west)
    return jnp.concatenate([before, after], axis=0)


def lengthways(south, north):
    count = lax.axis_size("chip") * lax.axis_size("core")
    down = [(i, i + 1) for i in range(count - 1)]
    up = [(i + 1, i) for i in range(count - 1)]
    return lax.ppermute(south, LAT, down), lax.ppermute(north, LAT, up)


LEFT = 16
ABOVE = 5
BELOW = 7
GUARD = 8
HALF = 64

FRINGE = (((0, 0, 0),), ((0, 1, 0),), ((0, 2, 0),), ((0, 0, 1), (0, 1, 1)), ((0, 2, 1), (1, 2, 1)))
MIDDLE = (((1, 0, 0),), ((1, 1, 0),), ((1, 2, 0),), ((1, 0, 1), (1, 1, 1)))
LAST = (((2, 0, 0),), ((2, 1, 0),), ((2, 2, 0),), ((2, 0, 1), (2, 1, 1)), ((2, 2, 1), None))
BLOCKS = FRINGE + MIDDLE + LAST


def low_lanes(rows):
    return lax.broadcasted_iota(jnp.int32, (rows, 128), 1) < HALF


def swapped(value):
    return pltpu.roll(value, HALF, 1)


def prepare(
    rows, cols, x_ref, c_ref, side_ref, south_ref, north_ref, lower_ref, upper_ref,
    windows_ref, cot_ref, wide, cots,
):
    pitch = cols + LEFT
    height = rows + ABOVE + BELOW
    size = height * pitch
    span = 2 * cols + 48
    base_row, base_col = 20, 24
    wide[...] = jnp.zeros_like(wide)
    cots[...] = jnp.zeros_like(cots)
    side = strips(2 * rows, rows)[0]
    corners = strips(CORNER, CORNER)[0]
    columns = [*range(-WEST, 0), *range(2 * cols, 2 * cols + EAST)]

    def at(i, j):
        return (i + base_row) * span + base_col + j

    def own(i, _):
        wide[pl.ds(pl.multiple_of(at(i, 0), 8), 2 * cols), :] = x_ref[i].astype(F32)
        return 0

    lax.fori_loop(0, 2 * rows, own, 0, unroll=8)
    for j, place in zip(columns, side[0][0] + side[1][0]):
        strip = side_ref[place : place + 2 * rows, :].astype(F32)
        wide[pl.ds(at(0, j), 2 * rows, stride=span), :] = strip
    for ref, corner_ref, inputs, top, first in (
        (south_ref, lower_ref, WEST, -WEST, -CORNER),
        (north_ref, upper_ref, EAST, 2 * rows, 2 * rows),
    ):
        for i in range(inputs):
            edge = ref[2 * cols * i : 2 * cols * (i + 1), :].astype(F32)
            wide[at(top + i, 0) : at(top + i, 0) + 2 * cols, :] = edge
        for place, j in zip(corners[0][0] + corners[1][0], columns):
            corner = corner_ref[place : place + CORNER, :].astype(F32)
            wide[pl.ds(at(first, j), CORNER, stride=span), :] = corner

    def window(k, _):
        for parity in range(2):
            row = 2 * (k - ABOVE) + parity + base_row
            for tap in range(3):
                base = row * span + base_col - 1 + tap
                mid = wide[pl.ds(base, cols, stride=2), :]
                before = wide[pl.ds(base - 16, 8, stride=2), :]
                after = wide[pl.ds(base - 2 * span + 2 * cols, 8, stride=2), :]
                lane = (3 * parity + tap) * 128
                cells = jnp.concatenate([after, before, mid], axis=0).astype(BF16)
                windows_ref[pl.ds(pl.multiple_of(k * pitch, 16), pitch), lane : lane + 128] = cells
        return 0

    lax.fori_loop(0, height, window, 0, unroll=11)

    def cell(i, j):
        return GUARD + (i + ABOVE) * pitch + LEFT + j

    columns = [*range(-BEFORE, 0), *range(cols, cols + AFTER)]
    parts = halves(c_ref[...])
    for part in range(2):
        for i in range(rows):
            cots[cell(i, 0) : cell(i, cols), :] = parts[part][i].astype(F32)
        for j, place in zip(columns, side[0][1][part] + side[1][1][part]):
            strip = side_ref[place : place + rows, :].astype(F32)
            cots[pl.ds(cell(0, j), rows, stride=pitch), :] = strip
        for ref, corner_ref, inputs, count, above in (
            (south_ref, lower_ref, WEST, BEFORE, True),
            (north_ref, upper_ref, EAST, AFTER, False),
        ):
            first = -count if above else rows
            for i in range(count):
                place = 2 * cols * inputs + cols * (count * part + i)
                to = cell(first + i, 0)
                cots[to : to + cols, :] = ref[place : place + cols, :].astype(F32)
            for place, j in zip(corners[0][1][part] + corners[1][1][part], columns):
                corner = corner_ref[place : place + CORNER, :].astype(F32)
                corner = corner[CORNER - 8 :] if above else corner[:8]
                for i in range(count):
                    line = 8 - count + i if above else i
                    cots[cell(first + i, j) : cell(first + i, j) + 1, :] = corner[line : line + 1]
        cot_ref[:, 128 * part : 128 * part + 128] = cots[GUARD : GUARD + size, :].astype(BF16)


def unfold(sections, count, *refs):
    terms, outs = refs[:count], refs[count : count + len(sections)]
    total, k_a, k_b = refs[count + len(sections) :]
    value = terms[0][...].astype(F32)
    for term in terms[1:]:
        value = value + term[...].astype(F32)
    total[...] = value
    for (first, n), out in zip(sections, outs):
        half = n // 3
        low = low_lanes(half)
        pair = total[first + 2 * half : first + n, :]
        turned = swapped(pair)
        k_a[0 : 2 * half, :] = total[first : first + 2 * half, :]
        k_b[0:half, :] = jnp.where(low, pair, turned)
        k_b[half : 2 * half, :] = jnp.where(low, turned, pair)
        even_a = k_a[pl.ds(0, half, stride=2), :]
        even_b = k_b[pl.ds(0, half, stride=2), :]
        odd_a = swapped(k_a[pl.ds(1, half, stride=2), :])
        odd_b = k_b[pl.ds(1, half, stride=2), :]
        out[pl.ds(0, half, stride=3), :] = even_a
        out[pl.ds(1, half, stride=3), :] = jnp.where(low, even_b, odd_a)
        out[pl.ds(2, half, stride=3), :] = jnp.where(low, odd_a, odd_b)


def level(shape, devices, parts, second, names, *refs):
    rows, cols, chan_in, mid, factor, whole = shape
    refs = dict(zip(names, refs))
    x_ref, terms_ref = refs["x"], refs["terms"]
    flat, k_a, k_b, f_a, f_b = (refs[name] for name in ("flat", "k_a", "k_b", "f_a", "f_b"))
    win_delta = refs["win_delta"]
    if second:
        t_one, t_two = refs["t_one"], refs["t_two"]
    pitch = cols + LEFT
    height = rows + ABOVE + BELOW
    size = height * pitch
    far, near, core, lon = devices.sizes
    count = 1 if whole else devices.count
    share = [9 * c * mid // 128 // count for c in (chan_in, mid, mid)]
    begin = [0, share[0], share[0] + share[1]]
    lat_at, mine = devices.place()

    def clear():
        head, tail = GUARD + pitch, GUARD + (ABOVE + rows + 5) * pitch
        for field in (f_a, f_b):
            field[0:head, :] = jnp.zeros((head, 128), F32)
            field[tail:, :] = jnp.zeros((field.shape[0] - tail, 128), F32)

    def unpack(which, channels):
        n = share[which]
        for i, (c, m, o) in enumerate(parts):
            plane = refs["plane", i]
            for f in range(plane.shape[0]):
                owner = 0 if whole else devices.index(devices.moved(mine, (f, m, c, o), -1))
                lo = begin[which] // 16 * 16
                hi = -(-(begin[which] + n) // 16) * 16
                value = plane[f, lo:hi, :].astype(F32)
                flat[pl.ds(owner * n, n), :] = value[begin[which] - lo : begin[which] - lo + n]
        pairs = 9 * channels // 2
        step = 288

        def one(i, _):
            at = i * step
            first = flat[pl.ds(3 * at, step, stride=3), :]
            second = flat[pl.ds(3 * at + 1, step, stride=3), :]
            third = flat[pl.ds(3 * at + 2, step, stride=3), :]
            low = low_lanes(step)
            second_r, third_r = swapped(second), swapped(third)
            k_a[pl.ds(2 * at, step, stride=2), :] = first
            k_b[pl.ds(2 * at, step, stride=2), :] = jnp.where(low, second, second_r)
            k_a[pl.ds(2 * at + 1, step, stride=2), :] = jnp.where(low, second_r, third_r)
            k_b[pl.ds(2 * at + 1, step, stride=2), :] = jnp.where(low, third_r, third)
            return 0

        lax.fori_loop(0, pairs // step, one, 0, unroll=True)

    def tap_rows(tap, part):
        start = (3 * tap[0] + tap[1]) * mid + 128 * part
        return start, start + (HALF if part else 128)

    def forward(target):
        at = 0
        for block in BLOCKS:
            for tap in block:
                if tap is None:
                    target[at : at + HALF, :] = jnp.zeros((HALF, 256), BF16)
                    at += HALF
                    continue
                lo, hi = tap_rows(tap, tap[2])
                target[at : at + hi - lo, 0:128] = k_a[lo:hi, :].astype(BF16)
                target[at : at + hi - lo, 128:256] = k_b[lo:hi, :].astype(BF16)
                at += hi - lo

    def backward(target):
        low = low_lanes(mid)
        for i, block in enumerate(BLOCKS):
            values = []
            for tap in block:
                if tap is None:
                    values.append(jnp.zeros((mid, 128), F32))
                    continue
                lo = (3 * (2 - tap[0]) + 2 - tap[1]) * mid
                source = k_b if tap[2] else k_a
                values.append(source[lo : lo + mid, :])
            value = values[0] if len(values) == 1 else jnp.where(low, values[0], values[1])
            value = value.astype(BF16)
            target[0:mid, 128 * i : 128 * i + 128] = value
            target[mid:256, 128 * i : 128 * i + 128] = value[128:mid]

    def load_kernels():
        unpack(0, chan_in)
        refs["w_one"][:, 0:128] = k_a[0 : 9 * chan_in, :].astype(BF16)
        refs["w_one"][:, 128:256] = k_b[0 : 9 * chan_in, :].astype(BF16)
        unpack(1, mid)
        forward(refs["w_two"])
        unpack(2, mid)
        forward(refs["w_three"])
        backward(refs["t_three"])

    def load_turned():
        unpack(0, chan_in)
        empty = jnp.zeros((chan_in, 128), F32)
        low_in = low_lanes(chan_in)
        phases = (
            ((1, 1), None, None, None),
            ((1, 2), (1, 0), None, None),
            ((2, 1), None, (0, 1), None),
            ((2, 2), (2, 0), (0, 2), (0, 0)),
        )
        for i, taps in enumerate(phases):
            a, b = [], []
            for tap in taps:
                if tap is None:
                    a.append(empty)
                    b.append(empty)
                else:
                    lo = (3 * tap[0] + tap[1]) * chan_in
                    a.append(k_a[lo : lo + chan_in, :])
                    b.append(k_b[lo : lo + chan_in, :])
            blocks = (
                a[0],
                a[1],
                jnp.where(low_in, b[0], b[1]),
                a[2],
                a[3],
                jnp.where(low_in, b[2], b[3]),
            )
            for j, block in enumerate(blocks):
                t_one[chan_in * i : chan_in * (i + 1), 128 * j : 128 * j + 128] = block.astype(BF16)
        unpack(1, mid)
        backward(t_two)

    first_row = lat_at * rows
    bottom = lax.axis_size("chip") * core * rows - first_row
    low_cell = (jnp.maximum(-first_row, -ABOVE) + ABOVE) * pitch + 8
    high_cell = (jnp.minimum(bottom, rows + BELOW) + ABOVE) * pitch + 8

    def inside(start, n):
        cell = start + lax.broadcasted_iota(jnp.int32, (n, 128), 0)
        return (cell >= low_cell) & (cell < high_cell)

    def store(start, n, left, right, mask):
        if mask:
            keep = inside(start, n)
            left = jnp.where(keep, left, 0.0)
            right = jnp.where(keep, right, 0.0)
        at = pl.multiple_of(start + GUARD, 8)
        f_a[pl.ds(at, n), :] = left
        f_b[pl.ds(at, n), :] = right

    def windows(target, top, under, f_a=f_a, f_b=f_b):
        wide = -(-(under - top) * pitch // 6 // 16) * 16

        def one(i, _):
            cell = (top + ABOVE) * pitch + i * wide
            q = cell + GUARD
            low = low_lanes(wide)
            b_0, b_1, b_2 = (f_b[pl.ds(q + s, wide), :] for s in (-1, 0, 1))
            b_3 = f_b[pl.ds(q + 1 + pitch, wide), :]
            out = [f_a[pl.ds(q + s, wide), :] for s in (-1, 0, 1)]
            out += [jnp.where(low, b_0, b_1), jnp.where(low, b_2, b_3)]
            at = pl.multiple_of(cell, 16)
            for j, value in enumerate(out):
                target[pl.ds(at, wide), 128 * j : 128 * j + 128] = value.astype(BF16)
            return 0

        lax.fori_loop(0, 6, one, 0)

    def convolve(source, weights, turned, halo, steps, finish):
        start = (ABOVE - halo) * pitch
        total = (rows + 1 + 2 * halo) * pitch + LEFT
        n = -(-total // steps // 16) * 16
        contract = (((1,), (1,)), ((), ())) if turned else (((1,), (0,)), ((), ()))

        def one(i, _):
            p = pl.multiple_of(start + i * n, 16)
            above = source[pl.ds(pl.multiple_of(p - pitch, 16), n), :]
            here = source[pl.ds(p, n), 0:512]
            below = source[pl.ds(pl.multiple_of(p + pitch, 16), n), :]
            value = lax.dot_general(
                jnp.concatenate([above, here, below], axis=1),
                weights[...],
                contract,
                preferred_element_type=F32,
            )
            finish(p, n, value)
            return 0

        lax.fori_loop(0, steps, one, 0)

    def own(ref, lanes, row_step=0, shift=0, offset=0):
        pieces = []
        for r in range(rows):
            at = offset + (ABOVE + r + row_step) * pitch + LEFT + shift
            pieces.append(ref[at : at + cols, lanes])
        return jnp.concatenate(pieces, axis=0)

    ALL = slice(0, 128)

    def turned_deltas():
        left = own(f_a, ALL, offset=GUARD)
        right = own(f_b, ALL, offset=GUARD)
        return jnp.concatenate([left.T, right.T], axis=0).astype(BF16)

    def pack(which, channels, first=0):
        if not whole:
            n = share[which]
            half = n // 3
            low = low_lanes(half)
            for k in range(count):
                at = 2 * half * k
                refs["chunk"][k, first : first + 2 * half, :] = k_a[at : at + 2 * half, :]
                pair = jnp.where(low, k_b[at : at + half, :], k_b[at + half : at + 2 * half, :])
                refs["chunk"][k, first + 2 * half : first + n, :] = pair
            return
        step = 288

        def one(i, _):
            at = i * step
            even_a = k_a[pl.ds(2 * at, step, stride=2), :]
            even_b = k_b[pl.ds(2 * at, step, stride=2), :]
            odd_a = swapped(k_a[pl.ds(2 * at + 1, step, stride=2), :])
            odd_b = k_b[pl.ds(2 * at + 1, step, stride=2), :]
            low = low_lanes(step)
            flat[pl.ds(3 * at, step, stride=3), :] = even_a
            flat[pl.ds(3 * at + 1, step, stride=3), :] = jnp.where(low, even_b, odd_a)
            flat[pl.ds(3 * at + 2, step, stride=3), :] = jnp.where(low, odd_a, odd_b)
            return 0

        lax.fori_loop(0, 9 * channels // 2 // step, one, 0)
        n = share[which]
        for k in range(count):
            refs["chunk"][k, first : first + n, :] = flat[k * n : (k + 1) * n, :]

    def hand_over():
        for k in range(count):
            f, m, c, o = devices.coords(k)
            place, side = 0, 0
            if not whole:
                f, m, side, o = devices.apart(devices.coords(k), mine)
                place = (m * lon + o) * far + f
            terms_ref[side, place] = refs["chunk"][k].astype(BF16)

    def field_grad(which, source, first):
        turned = turned_deltas()
        for a, blocks in enumerate((FRINGE, MIDDLE, LAST)):
            lanes = slice(0, 128 * len(blocks))
            product = lax.dot_general(
                turned,
                own(source, lanes, a - 1),
                (((1,), (0,)), ((), ())),
                preferred_element_type=F32,
            )
            product = product * factor
            for j, block in enumerate(blocks):
                left = product[0:128, 128 * j : 128 * j + 128].T
                right = product[128:256, 128 * j : 128 * j + 128].T
                at = 0
                for tap in block:
                    if tap is None:
                        continue
                    lo, hi = tap_rows(tap, tap[2])
                    k_a[lo:hi, :] = left[at : at + hi - lo]
                    k_b[lo:hi, :] = right[at : at + hi - lo]
                    at += hi - lo
        pack(which, mid, first)

    def forward_pass():
        load_kernels()
        win_one, win_two, slope, spread, c_ref = (
            refs[name] for name in ("win_one", "win_two", "slope", "spread", "c")
        )
        clear()

        def convolve_first():
            halo, steps = 4, 2
            start = (ABOVE - halo) * pitch
            total = (rows + 1 + 2 * halo) * pitch + LEFT
            n = -(-total // steps // 16) * 16

            def one(i, _):
                p = pl.multiple_of(start + i * n, 16)
                above = x_ref[pl.ds(pl.multiple_of(p - pitch, 16), n), 384:768]
                here = x_ref[pl.ds(p, n), :]
                value = lax.dot_general(
                    jnp.concatenate([above, here], axis=1),
                    refs["w_one"][...],
                    (((1,), (0,)), ((), ())),
                    preferred_element_type=F32,
                )
                store(p, n, value[:, :128], value[:, 128:], True)
                return 0

            lax.fori_loop(0, steps, one, 0)

        convolve_first()
        windows(win_one, -4, rows + 6)

        def finish_two(p, n, value):
            s = jax.nn.sigmoid(value)
            active = value * s
            slope[pl.ds(p, n), :] = s + active * (1.0 - s)
            store(p, n, active[:, :128], active[:, 128:], True)

        convolve(win_one, refs["w_two"], False, 3, 2, finish_two)
        windows(win_two, -3, rows + 5)

        def finish_three(p, n, value):
            s = jax.nn.sigmoid(value)
            active = value * s
            delta = c_ref[pl.ds(p, n), :].astype(F32) * (s + active * (1.0 - s))
            store(p, n, delta[:, :128], delta[:, 128:], False)
            spread[pl.ds(p, n), :] = active

        convolve(win_two, refs["w_three"], False, 2, 2, finish_three)
        for r in range(rows):
            at = (ABOVE + r) * pitch + LEFT
            refs["features"][r] = spread[at : at + cols, 0:mid].astype(BF16)
        field_grad(2, win_two, share[1])
        windows(win_delta, -2, rows + 4)

        def finish_delta(p, n, value):
            value = value * slope[pl.ds(p, n), :]
            store(p, n, value[:, :128], value[:, 128:], True)

        convolve(win_delta, refs["t_three"], True, 1, 2, finish_delta)
        field_grad(1, win_one, 0)
        hand_over()

    def backward_pass():
        load_turned()
        windows(win_delta, -1, rows + 3, refs["d_a"], refs["d_b"])

        def finish_back(p, n, value):
            store(p, n, value[:, :128], value[:, 128:], True)

        convolve(win_delta, t_two, True, 0, 2, finish_back)
        turned = turned_deltas()
        for a, (step, lanes) in enumerate(((-1, slice(384, 768)), (0, slice(0, 384)), (0, slice(384, 768)))):
            product = lax.dot_general(
                turned,
                own(x_ref, lanes, step),
                (((1,), (0,)), ((), ())),
                preferred_element_type=F32,
            )
            product = product * factor
            lo = 3 * a * chan_in
            k_a[lo : lo + 3 * chan_in, :] = product[0:128].T
            k_b[lo : lo + 3 * chan_in, :] = product[128:256].T
        pack(0, chan_in)
        hand_over()

        low = low_lanes(rows * cols)

        def four(ref):
            return [own(ref, ALL, r, c, GUARD) for r, c in ((0, 0), (0, 1), (1, 0), (1, 1))]

        a, b = four(f_a), four(f_b)
        around = (a[0], a[1], jnp.where(low, b[0], b[1]), a[2], a[3], jnp.where(low, b[2], b[3]))
        around = jnp.concatenate([value.astype(BF16) for value in around], axis=1)
        for r in range(2):
            wide = 384 * (r + 1)
            product = lax.dot_general(
                around[:, :wide],
                t_one[2 * chan_in * r : 2 * chan_in * (r + 1), :wide],
                (((1,), (1,)), ((), ())),
                preferred_element_type=F32,
            )
            for i in range(rows):
                at = i * cols
                base = (2 * i + r) * 2 * cols
                for c in range(2):
                    spread_in = product[at : at + cols, chan_in * c : chan_in * (c + 1)]
                    refs["image"][pl.ds(base + c, cols, stride=2), :] = spread_in
        for i in range(2 * rows):
            refs["grad_input"][i] = refs["image"][2 * cols * i : 2 * cols * (i + 1), :].astype(BF16)

    if second:
        backward_pass()
    else:
        forward_pass()


VMEM = pl.BlockSpec(memory_space=pltpu.VMEM)
ANY = pl.BlockSpec(memory_space=pl.ANY)


def local(inputs, w_first, w_second, w_third, cotangent):
    devices = Slice()
    rows, cols, mid = cotangent.shape
    chan_in = inputs.shape[2]
    factor = 1.0 / LOSS_CELLS
    far, near, core, lon = devices.sizes
    held = (w_first.shape[0], w_second.shape[0], w_third.shape[0])
    shard = jnp.concatenate([w_first, w_second, w_third]).reshape(-1, 128)
    whole = any(n % 384 for n in held)
    if not whole:
        shard = jnp.pad(shard, ((0, -shard.shape[0] % 16), (0, 0)))
    count = 1 if whole else devices.count

    side_rows, corner_rows = strips(2 * rows, rows)[1], strips(CORNER, CORNER)[1]
    south_rows = 2 * cols * (WEST + BEFORE)
    north_rows = 2 * cols * (EAST + AFTER)
    cost = pl.CostEstimate(flops=0, bytes_accessed=3 * 2**20, transcendentals=0)
    params = pltpu.CompilerParams(vmem_limit_bytes=16 * 2**20)

    def buffers(*sizes):
        return [jax.ShapeDtypeStruct((n, 128), BF16) for n in sizes]

    side, south, north = pl.pallas_call(
        functools.partial(pack_sides, rows, cols),
        out_shape=buffers(side_rows, south_rows, north_rows),
        in_specs=[VMEM] * 2,
        out_specs=[VMEM] * 3,
        scratch_shapes=[pltpu.VMEM((2 * rows * CORNER, 128), F32)],
        compiler_params=params,
        cost_estimate=cost,
    )(inputs, cotangent)
    line = lined(devices, shard)
    south, north = lengthways(south, north)
    side = sideways(side, strips(2 * rows, rows)[0][1][0][0])
    lower, upper = pl.pallas_call(
        functools.partial(pack_corners, rows),
        out_shape=buffers(corner_rows, corner_rows),
        in_specs=[VMEM],
        out_specs=[VMEM] * 2,
        compiler_params=params,
        cost_estimate=cost,
    )(side)
    lower, upper = lengthways(lower, upper)
    line, south, north, side = lax.optimization_barrier((line, south, north, side))
    planes = spread(devices, line)
    size = (rows + ABOVE + BELOW) * (cols + LEFT)
    padded, cot = pl.pallas_call(
        functools.partial(prepare, rows, cols),
        out_shape=(
            jax.ShapeDtypeStruct((size, 6 * chan_in), BF16),
            jax.ShapeDtypeStruct((size, 256), BF16),
        ),
        in_specs=[VMEM] * 7,
        out_specs=(VMEM, VMEM),
        scratch_shapes=[
            pltpu.VMEM(((2 * rows + 40) * (2 * cols + 48), 128), F32),
            pltpu.VMEM((size + 2 * GUARD, 128), F32),
        ],
        compiler_params=pltpu.CompilerParams(vmem_limit_bytes=40 * 2**20),
        cost_estimate=pl.CostEstimate(flops=0, bytes_accessed=12 * 2**20, transcendentals=0),
    )(inputs, cotangent, side, south, north, lower, upper)

    planes[1:], padded, cot = lax.optimization_barrier((planes[1:], padded, cot))
    planes, parts = shared_out(devices, planes)
    if whole:
        chunks = jnp.stack(planes).reshape(devices.count, -1)
        chunks = jnp.take(chunks, jnp.argsort(order(devices, -1)), axis=0)
        pieces = jnp.split(chunks, (held[0], held[0] + held[1]), axis=1)
        chunks = jnp.concatenate([piece.reshape(-1) for piece in pieces])
        planes, parts = [chunks.reshape(1, -1, 128)], [(0, 0, 0)]
    deep = -(-(2 * held[1]) // 2048) * 16, -(-held[0] // 2048) * 16
    if whole:
        deep = 2 * held[1] * devices.count // 128, held[0] * devices.count // 128
    sides = 1 if whole else core
    field_shape = (size + 2 * GUARD, 128)
    shape = (rows, cols, chan_in, mid, factor, whole)
    wide = 128 * len(BLOCKS)
    shared = {
        "flat": ((9 * mid * mid // 128, 128), F32),
        "k_a": ((9 * mid, 128), F32),
        "k_b": ((9 * mid, 128), F32),
        "f_a": (field_shape, F32),
        "f_b": (field_shape, F32),
    }

    def call(second, ins, outs, scratch):
        scratch = {**scratch, **{name: kind for name, kind in shared.items() if name not in outs}}
        names = list(ins) + list(outs) + list(scratch)
        results = pl.pallas_call(
            functools.partial(level, shape, devices, parts, second, names),
            out_shape=[jax.ShapeDtypeStruct(*out) for out in outs.values()],
            in_specs=[VMEM] * len(ins),
            out_specs=[VMEM] * len(outs),
            scratch_shapes=[pltpu.VMEM(*kind) for kind in scratch.values()],
            compiler_params=pltpu.CompilerParams(vmem_limit_bytes=40 * 2**20),
            cost_estimate=pl.CostEstimate(
                flops=2 * 10**9 if second else 5 * 10**9,
                bytes_accessed=12 * 2**20,
                transcendentals=10**6,
            ),
        )(*ins.values())
        return dict(zip(outs, results))

    kernels = {("plane", i): plane for i, plane in enumerate(planes)}
    ins = {"x": padded, "c": cot, **kernels}
    done = call(
        False,
        ins,
        {
            "features": ((rows, cols, mid), BF16),
            "terms": ((sides, count // sides, deep[0], 128), BF16),
            "f_a": (field_shape, F32),
            "f_b": (field_shape, F32),
        },
        {
            "chunk": ((count, deep[0], 128), F32),
            "w_one": ((9 * chan_in, 256), BF16),
            "w_two": ((wide, 256), BF16),
            "w_three": ((wide, 256), BF16),
            "t_three": ((256, wide), BF16),
            "slope": ((size, 256), F32),
            "spread": ((size, 256), F32),
            "win_one": ((size, 640), BF16),
            "win_two": ((size, 640), BF16),
            "win_delta": ((size, 640), BF16),
        },
    )
    features = done["features"]

    def reduced(terms, *sizes):
        if whole:
            cuts = [sum(sizes[:i]) * devices.count for i in range(1, len(sizes))]
            pieces = jnp.split(terms.reshape(-1), cuts)
            terms = [piece.reshape(devices.count, -1) for piece in pieces]
            terms = jnp.take(jnp.concatenate(terms, axis=1), order(devices, 1), axis=0)
            terms = terms.reshape(core, devices.count // core, 1, -1)
        return halved(devices, terms)

    upper = reduced(done["terms"], held[1], held[2])
    upper, f_a, f_b = lax.optimization_barrier((upper, done["f_a"], done["f_b"]))
    upper = planar(devices, upper)
    done = call(
        True,
        {"x": padded, "d_a": f_a, "d_b": f_b, **kernels},
        {
            "grad_input": ((2 * rows, 2 * cols, chan_in), BF16),
            "terms": ((sides, count // sides, deep[1], 128), BF16),
        },
        {
            "chunk": ((count, deep[1], 128), F32),
            "t_one": ((4 * chan_in, 768), BF16),
            "t_two": ((256, wide), BF16),
            "win_delta": ((size, 640), BF16),
            "image": ((4 * rows * cols, 128), F32),
        },
    )
    upper, lower = lax.optimization_barrier((upper, reduced(done["terms"], held[0])))
    lower = planar(devices, lower)
    terms = linear(devices, jnp.concatenate([upper, lower], axis=-1 if whole else -2))
    if whole:
        grad_second, grad_third, grad_first = jnp.split(
            total_of(terms).reshape(-1), (held[1], held[1] + held[2])
        )
    else:
        depth = upper.shape[-2]
        high = [n // 128 for n in (held[1], held[2], held[0])]
        sections = ((0, high[0]), (high[0], high[1]), (depth, high[2]))
        deepest = max(high)
        totals = pl.pallas_call(
            functools.partial(unfold, sections, len(terms)),
            out_shape=[jax.ShapeDtypeStruct((n, 128), F32) for n in high],
            in_specs=[VMEM] * len(terms),
            out_specs=[VMEM] * 3,
            scratch_shapes=[
                pltpu.VMEM(terms[0].shape, F32),
                pltpu.VMEM((deepest, 128), F32),
                pltpu.VMEM((deepest, 128), F32),
            ],
            compiler_params=params,
            cost_estimate=pl.CostEstimate(flops=0, bytes_accessed=2**19, transcendentals=0),
        )(*terms)
        grad_second, grad_third, grad_first = (total.reshape(-1) for total in totals)
    return (features, done["grad_input"], grad_first, grad_second, grad_third)


def solution(mesh):
    lat, lon = mesh.shape["lat"], mesh.shape["lon"]
    core = 2 if lat % 2 == 0 else 1
    chips = jax.sharding.Mesh(mesh.devices.reshape(lat // core, core, lon), BOTH)
    tile = P(LAT, "lon", None)
    flat = P(BOTH)
    return jax.shard_map(
        local,
        mesh=chips,
        in_specs=(tile, flat, flat, flat, tile),
        out_specs=(tile, tile, flat, flat, flat),
        check_vma=False,
    )
```

```python
import functools

import jax
import jax.numpy as jnp
from jax import lax
from jax.experimental import pallas as pl
from jax.experimental.pallas import tpu as pltpu
from jax.sharding import PartitionSpec as P

LOSS_CELLS = 1024
LAT = ("chip", "core")
BOTH = ("chip", "core", "lon")
F32 = jnp.float32
BF16 = jnp.bfloat16


class Slice:
    def __init__(self):
        chip, core, lon = (lax.axis_size(axis) for axis in BOTH)
        near = 2 if chip % 2 == 0 else 1
        self.sizes = (chip // near, near, core, lon)
        self.count = chip * core * lon

    def place(self):
        lat = lax.axis_index("chip") * self.sizes[2] + lax.axis_index("core")
        return lat, self.coords(lat * self.sizes[3] + lax.axis_index("lon"))

    def coords(self, index):
        out = []
        for size in reversed(self.sizes):
            if isinstance(index, int):
                out.append(index % size)
                index = index // size
            else:
                out.append(lax.rem(index, size))
                index = lax.div(index, size)
        return tuple(reversed(out))

    def index(self, coords):
        total = 0
        for at, size in zip(coords, self.sizes):
            total = total * size + at
        return total

    def moved(self, coords, steps, sign=1):
        out = []
        for at, by, size in zip(coords, steps, self.sizes):
            if size & (size - 1) == 0:
                out.append(at ^ by)
            else:
                to = at + sign * by + size
                out.append(to % size if isinstance(to, int) else lax.rem(to, size))
        return tuple(out)

    def apart(self, coords, origin):
        out = []
        for to, at, size in zip(coords, origin, self.sizes):
            out.append(at ^ to if size & (size - 1) == 0 else lax.rem(to - at + size, size))
        return tuple(out)

    def send(self, value, steps):
        pairs = []
        for source in range(self.count):
            pairs.append((source, self.index(self.moved(self.coords(source), steps))))
        return lax.ppermute(value, BOTH, pairs)


def lined(devices, shard):
    far = devices.sizes[0]
    return jnp.stack([shard] + [devices.send(shard, (f, 0, 0, 0)) for f in range(1, far)])


def spread(devices, line):
    far, near, core, lon = devices.sizes
    planes = []
    for n in range(near):
        for o in range(lon):
            planes.append(line if n == o == 0 else devices.send(line, (0, n, 0, o)))
    return planes


def shared_out(devices, planes):
    far, near, core, lon = devices.sizes
    out, parts = [], []
    for c in range(core):
        for n in range(near):
            for o in range(lon):
                plane = planes[n * lon + o]
                out.append(devices.send(plane, (0, 0, c, 0)) if c else plane)
                parts.append((c, n, o))
    return out, parts


def halved(devices, chunks):
    half = chunks[0].astype(F32)
    for c in range(1, chunks.shape[0]):
        half = half + devices.send(chunks[c], (0, 0, c, 0)).astype(F32)
    return half.astype(BF16)


def order(devices, sign):
    far, near, core, lon = devices.sizes
    mine = devices.place()[1]
    places = []
    for c in range(core):
        for n in range(near):
            for o in range(lon):
                for f in range(far):
                    places.append(devices.index(devices.moved(mine, (f, n, c, o), sign)))
    return jnp.stack(places)


def total_of(terms):
    total = terms[0].astype(F32)
    for term in terms[1:]:
        total = total + term.astype(F32)
    return total


def planar(devices, half):
    far, near, core, lon = devices.sizes
    half = half.reshape(near * lon, far, *half.shape[1:])
    terms = []
    for n in range(near):
        for o in range(lon):
            part = half[n * lon + o]
            terms.append(part if n == o == 0 else devices.send(part, (0, n, 0, o)))
    return total_of(terms).astype(BF16)


def linear(devices, line):
    far = devices.sizes[0]
    return [line[0]] + [devices.send(line[f], (f, 0, 0, 0)) for f in range(1, far)]


WEST, EAST = 9, 10
BEFORE, AFTER = 2, 3
CORNER = 16


def strips(inputs_high, cots_high):
    side, at = [], 0
    for inputs, cots in ((WEST, BEFORE), (EAST, AFTER)):
        columns = [at + inputs_high * j for j in range(inputs)]
        at += inputs_high * inputs
        parts = [[at + cots_high * (cots * part + j) for j in range(cots)] for part in range(2)]
        at += 2 * cots_high * cots
        side.append((columns, parts))
    return side, at


def halves(value):
    return value[..., :128], jnp.concatenate([value[..., 128:], value[..., 128:]], axis=-1)


def pack_sides(rows, cols, x_ref, c_ref, side_ref, south_ref, north_ref, strip):
    west, east = strips(2 * rows, rows)[0]

    def columns(value, wanted, places):
        high = value.shape[0]
        strip[: high * CORNER, :] = value.astype(F32).reshape(high * CORNER, 128)
        for j, place in zip(wanted, places):
            side_ref[place : place + high, :] = strip[pl.ds(j, high, stride=CORNER), :].astype(BF16)

    columns(x_ref[:, 2 * cols - CORNER :, :], range(CORNER - WEST, CORNER), west[0])
    columns(x_ref[:, :CORNER, :], range(EAST), east[0])
    parts = halves(c_ref[...])
    for part in range(2):
        columns(parts[part][:, cols - CORNER :], range(CORNER - BEFORE, CORNER), west[1][part])
        columns(parts[part][:, :CORNER], range(AFTER), east[1][part])
    for ref, inputs, cots, x_row, c_row in (
        (south_ref, WEST, BEFORE, 2 * rows - WEST, rows - BEFORE),
        (north_ref, EAST, AFTER, 0, 0),
    ):
        for i in range(inputs):
            ref[2 * cols * i : 2 * cols * (i + 1), :] = x_ref[x_row + i]
        at = 2 * cols * inputs
        for part in range(2):
            for i in range(cots):
                ref[at : at + cols, :] = parts[part][c_row + i]
                at += cols


def pack_corners(rows, side_ref, lower_ref, upper_ref):
    for side, corner in zip(strips(2 * rows, rows)[0], strips(CORNER, CORNER)[0]):
        strip = [(2 * rows, *pair) for pair in zip(side[0], corner[0])]
        for part in range(2):
            strip += [(rows, *pair) for pair in zip(side[1][part], corner[1][part])]
        for high, place, to in strip:
            end = place + high
            lower_ref[to : to + CORNER, :] = side_ref[end - CORNER : end, :]
            upper_ref[to : to + CORNER, :] = side_ref[place : place + CORNER, :]


def sideways(packed, cut):
    count = lax.axis_size("lon")
    east = [(i, (i + 1) % count) for i in range(count)]
    west = [(i, (i - 1) % count) for i in range(count)]
    if count == 2:
        return lax.ppermute(packed, "lon", east)
    before = lax.ppermute(packed[:cut], "lon", east)
    after = lax.ppermute(packed[cut:], "lon", west)
    return jnp.concatenate([before, after], axis=0)


def lengthways(south, north):
    count = lax.axis_size("chip") * lax.axis_size("core")
    down = [(i, i + 1) for i in range(count - 1)]
    up = [(i + 1, i) for i in range(count - 1)]
    return lax.ppermute(south, LAT, down), lax.ppermute(north, LAT, up)


LEFT = 16
ABOVE = 5
BELOW = 7
GUARD = 8
HALF = 64

FRINGE = (((0, 0, 0),), ((0, 1, 0),), ((0, 2, 0),), ((0, 0, 1), (0, 1, 1)), ((0, 2, 1), (1, 2, 1)))
MIDDLE = (((1, 0, 0),), ((1, 1, 0),), ((1, 2, 0),), ((1, 0, 1), (1, 1, 1)))
LAST = (((2, 0, 0),), ((2, 1, 0),), ((2, 2, 0),), ((2, 0, 1), (2, 1, 1)), ((2, 2, 1), None))
BLOCKS = FRINGE + MIDDLE + LAST


def low_lanes(rows):
    return lax.broadcasted_iota(jnp.int32, (rows, 128), 1) < HALF


def swapped(value):
    return pltpu.roll(value, HALF, 1)


def prepare(
    rows, cols, x_ref, c_ref, side_ref, south_ref, north_ref, lower_ref, upper_ref,
    windows_ref, cot_ref, wide, cots,
):
    pitch = cols + LEFT
    height = rows + ABOVE + BELOW
    size = height * pitch
    span = 2 * cols + 48
    base_row, base_col = 20, 24
    wide[...] = jnp.zeros_like(wide)
    cots[...] = jnp.zeros_like(cots)
    side = strips(2 * rows, rows)[0]
    corners = strips(CORNER, CORNER)[0]
    columns = [*range(-WEST, 0), *range(2 * cols, 2 * cols + EAST)]

    def at(i, j):
        return (i + base_row) * span + base_col + j

    def own(i, _):
        wide[pl.ds(pl.multiple_of(at(i, 0), 8), 2 * cols), :] = x_ref[i].astype(F32)
        return 0

    lax.fori_loop(0, 2 * rows, own, 0, unroll=8)
    for j, place in zip(columns, side[0][0] + side[1][0]):
        strip = side_ref[place : place + 2 * rows, :].astype(F32)
        wide[pl.ds(at(0, j), 2 * rows, stride=span), :] = strip
    for ref, corner_ref, inputs, top, first in (
        (south_ref, lower_ref, WEST, -WEST, -CORNER),
        (north_ref, upper_ref, EAST, 2 * rows, 2 * rows),
    ):
        for i in range(inputs):
            edge = ref[2 * cols * i : 2 * cols * (i + 1), :].astype(F32)
            wide[at(top + i, 0) : at(top + i, 0) + 2 * cols, :] = edge
        for place, j in zip(corners[0][0] + corners[1][0], columns):
            corner = corner_ref[place : place + CORNER, :].astype(F32)
            wide[pl.ds(at(first, j), CORNER, stride=span), :] = corner

    def window(k, _):
        for parity in range(2):
            row = 2 * (k - ABOVE) + parity + base_row
            for tap in range(3):
                base = row * span + base_col - 1 + tap
                mid = wide[pl.ds(base, cols, stride=2), :]
                before = wide[pl.ds(base - 16, 8, stride=2), :]
                after = wide[pl.ds(base - 2 * span + 2 * cols, 8, stride=2), :]
                lane = (3 * parity + tap) * 128
                cells = jnp.concatenate([after, before, mid], axis=0).astype(BF16)
                windows_ref[pl.ds(pl.multiple_of(k * pitch, 16), pitch), lane : lane + 128] = cells
        return 0

    lax.fori_loop(0, height, window, 0, unroll=11)

    def cell(i, j):
        return GUARD + (i + ABOVE) * pitch + LEFT + j

    columns = [*range(-BEFORE, 0), *range(cols, cols + AFTER)]
    parts = halves(c_ref[...])
    for part in range(2):
        for i in range(rows):
            cots[cell(i, 0) : cell(i, cols), :] = parts[part][i].astype(F32)
        for j, place in zip(columns, side[0][1][part] + side[1][1][part]):
            strip = side_ref[place : place + rows, :].astype(F32)
            cots[pl.ds(cell(0, j), rows, stride=pitch), :] = strip
        for ref, corner_ref, inputs, count, above in (
            (south_ref, lower_ref, WEST, BEFORE, True),
            (north_ref, upper_ref, EAST, AFTER, False),
        ):
            first = -count if above else rows
            for i in range(count):
                place = 2 * cols * inputs + cols * (count * part + i)
                to = cell(first + i, 0)
                cots[to : to + cols, :] = ref[place : place + cols, :].astype(F32)
            for place, j in zip(corners[0][1][part] + corners[1][1][part], columns):
                corner = corner_ref[place : place + CORNER, :].astype(F32)
                corner = corner[CORNER - 8 :] if above else corner[:8]
                for i in range(count):
                    line = 8 - count + i if above else i
                    cots[cell(first + i, j) : cell(first + i, j) + 1, :] = corner[line : line + 1]
        cot_ref[:, 128 * part : 128 * part + 128] = cots[GUARD : GUARD + size, :].astype(BF16)


def unfold(sections, count, *refs):
    terms, outs = refs[:count], refs[count : count + len(sections)]
    total, k_a, k_b = refs[count + len(sections) :]
    value = terms[0][...].astype(F32)
    for term in terms[1:]:
        value = value + term[...].astype(F32)
    total[...] = value
    for (first, n), out in zip(sections, outs):
        half = n // 3
        low = low_lanes(half)
        pair = total[first + 2 * half : first + n, :]
        turned = swapped(pair)
        k_a[0 : 2 * half, :] = total[first : first + 2 * half, :]
        k_b[0:half, :] = jnp.where(low, pair, turned)
        k_b[half : 2 * half, :] = jnp.where(low, turned, pair)
        even_a = k_a[pl.ds(0, half, stride=2), :]
        even_b = k_b[pl.ds(0, half, stride=2), :]
        odd_a = swapped(k_a[pl.ds(1, half, stride=2), :])
        odd_b = k_b[pl.ds(1, half, stride=2), :]
        out[pl.ds(0, half, stride=3), :] = even_a
        out[pl.ds(1, half, stride=3), :] = jnp.where(low, even_b, odd_a)
        out[pl.ds(2, half, stride=3), :] = jnp.where(low, odd_a, odd_b)


def level(shape, devices, parts, second, names, *refs):
    rows, cols, chan_in, mid, factor, whole = shape
    refs = dict(zip(names, refs))
    x_ref, terms_ref = refs["x"], refs["terms"]
    flat, k_a, k_b, f_a, f_b = (refs[name] for name in ("flat", "k_a", "k_b", "f_a", "f_b"))
    win_delta = refs["win_delta"]
    if second:
        t_one, t_two = refs["t_one"], refs["t_two"]
    pitch = cols + LEFT
    height = rows + ABOVE + BELOW
    size = height * pitch
    far, near, core, lon = devices.sizes
    count = 1 if whole else devices.count
    share = [9 * c * mid // 128 // count for c in (chan_in, mid, mid)]
    begin = [0, share[0], share[0] + share[1]]
    lat_at, mine = devices.place()

    def clear():
        head, tail = GUARD + pitch, GUARD + (ABOVE + rows + 5) * pitch
        for field in (f_a, f_b):
            field[0:head, :] = jnp.zeros((head, 128), F32)
            field[tail:, :] = jnp.zeros((field.shape[0] - tail, 128), F32)

    def unpack(which, channels):
        n = share[which]
        for i, (c, m, o) in enumerate(parts):
            plane = refs["plane", i]
            for f in range(plane.shape[0]):
                owner = 0 if whole else devices.index(devices.moved(mine, (f, m, c, o), -1))
                lo = begin[which] // 16 * 16
                hi = -(-(begin[which] + n) // 16) * 16
                value = plane[f, lo:hi, :].astype(F32)
                flat[pl.ds(owner * n, n), :] = value[begin[which] - lo : begin[which] - lo + n]
        pairs = 9 * channels // 2
        step = 288

        def one(i, _):
            at = i * step
            first = flat[pl.ds(3 * at, step, stride=3), :]
            second = flat[pl.ds(3 * at + 1, step, stride=3), :]
            third = flat[pl.ds(3 * at + 2, step, stride=3), :]
            low = low_lanes(step)
            second_r, third_r = swapped(second), swapped(third)
            k_a[pl.ds(2 * at, step, stride=2), :] = first
            k_b[pl.ds(2 * at, step, stride=2), :] = jnp.where(low, second, second_r)
            k_a[pl.ds(2 * at + 1, step, stride=2), :] = jnp.where(low, second_r, third_r)
            k_b[pl.ds(2 * at + 1, step, stride=2), :] = jnp.where(low, third_r, third)
            return 0

        lax.fori_loop(0, pairs // step, one, 0, unroll=True)

    def tap_rows(tap, part):
        start = (3 * tap[0] + tap[1]) * mid + 128 * part
        return start, start + (HALF if part else 128)

    def forward(target):
        at = 0
        for block in BLOCKS:
            for tap in block:
                if tap is None:
                    target[at : at + HALF, :] = jnp.zeros((HALF, 256), BF16)
                    at += HALF
                    continue
                lo, hi = tap_rows(tap, tap[2])
                target[at : at + hi - lo, 0:128] = k_a[lo:hi, :].astype(BF16)
                target[at : at + hi - lo, 128:256] = k_b[lo:hi, :].astype(BF16)
                at += hi - lo

    def backward(target):
        low = low_lanes(mid)
        for i, block in enumerate(BLOCKS):
            values = []
            for tap in block:
                if tap is None:
                    values.append(jnp.zeros((mid, 128), F32))
                    continue
                lo = (3 * (2 - tap[0]) + 2 - tap[1]) * mid
                source = k_b if tap[2] else k_a
                values.append(source[lo : lo + mid, :])
            value = values[0] if len(values) == 1 else jnp.where(low, values[0], values[1])
            value = value.astype(BF16)
            target[0:mid, 128 * i : 128 * i + 128] = value
            target[mid:256, 128 * i : 128 * i + 128] = value[128:mid]

    def load_kernels():
        unpack(0, chan_in)
        refs["w_one"][:, 0:128] = k_a[0 : 9 * chan_in, :].astype(BF16)
        refs["w_one"][:, 128:256] = k_b[0 : 9 * chan_in, :].astype(BF16)
        unpack(1, mid)
        forward(refs["w_two"])
        unpack(2, mid)
        forward(refs["w_three"])
        backward(refs["t_three"])

    def load_turned():
        unpack(0, chan_in)
        empty = jnp.zeros((chan_in, 128), F32)
        low_in = low_lanes(chan_in)
        phases = (
            ((1, 1), None, None, None),
            ((1, 2), (1, 0), None, None),
            ((2, 1), None, (0, 1), None),
            ((2, 2), (2, 0), (0, 2), (0, 0)),
        )
        for i, taps in enumerate(phases):
            a, b = [], []
            for tap in taps:
                if tap is None:
                    a.append(empty)
                    b.append(empty)
                else:
                    lo = (3 * tap[0] + tap[1]) * chan_in
                    a.append(k_a[lo : lo + chan_in, :])
                    b.append(k_b[lo : lo + chan_in, :])
            blocks = (
                a[0],
                a[1],
                jnp.where(low_in, b[0], b[1]),
                a[2],
                a[3],
                jnp.where(low_in, b[2], b[3]),
            )
            for j, block in enumerate(blocks):
                t_one[chan_in * i : chan_in * (i + 1), 128 * j : 128 * j + 128] = block.astype(BF16)
        unpack(1, mid)
        backward(t_two)

    first_row = lat_at * rows
    bottom = lax.axis_size("chip") * core * rows - first_row
    low_cell = (jnp.maximum(-first_row, -ABOVE) + ABOVE) * pitch + 8
    high_cell = (jnp.minimum(bottom, rows + BELOW) + ABOVE) * pitch + 8

    def inside(start, n):
        cell = start + lax.broadcasted_iota(jnp.int32, (n, 128), 0)
        return (cell >= low_cell) & (cell < high_cell)

    def store(start, n, left, right, mask):
        if mask:
            keep = inside(start, n)
            left = jnp.where(keep, left, 0.0)
            right = jnp.where(keep, right, 0.0)
        at = pl.multiple_of(start + GUARD, 8)
        f_a[pl.ds(at, n), :] = left
        f_b[pl.ds(at, n), :] = right

    def windows(target, top, under, f_a=f_a, f_b=f_b):
        wide = -(-(under - top) * pitch // 6 // 16) * 16

        def one(i, _):
            cell = (top + ABOVE) * pitch + i * wide
            q = cell + GUARD
            low = low_lanes(wide)
            b_0, b_1, b_2 = (f_b[pl.ds(q + s, wide), :] for s in (-1, 0, 1))
            b_3 = f_b[pl.ds(q + 1 + pitch, wide), :]
            out = [f_a[pl.ds(q + s, wide), :] for s in (-1, 0, 1)]
            out += [jnp.where(low, b_0, b_1), jnp.where(low, b_2, b_3)]
            at = pl.multiple_of(cell, 16)
            for j, value in enumerate(out):
                target[pl.ds(at, wide), 128 * j : 128 * j + 128] = value.astype(BF16)
            return 0

        lax.fori_loop(0, 6, one, 0, unroll=2)

    def convolve(source, weights, turned, halo, steps, finish):
        start = (ABOVE - halo) * pitch
        total = (rows + 1 + 2 * halo) * pitch + LEFT
        n = -(-total // steps // 16) * 16
        contract = (((1,), (1,)), ((), ())) if turned else (((1,), (0,)), ((), ()))

        def one(i, _):
            p = pl.multiple_of(start + i * n, 16)
            above = source[pl.ds(pl.multiple_of(p - pitch, 16), n), :]
            here = source[pl.ds(p, n), 0:512]
            below = source[pl.ds(pl.multiple_of(p + pitch, 16), n), :]
            value = lax.dot_general(
                jnp.concatenate([above, here, below], axis=1),
                weights[...],
                contract,
                preferred_element_type=F32,
            )
            finish(p, n, value)
            return 0

        lax.fori_loop(0, steps, one, 0)

    def own(ref, lanes, row_step=0, shift=0, offset=0):
        pieces = []
        for r in range(rows):
            at = offset + (ABOVE + r + row_step) * pitch + LEFT + shift
            pieces.append(ref[at : at + cols, lanes])
        return jnp.concatenate(pieces, axis=0)

    ALL = slice(0, 128)

    def turned_deltas():
        left = own(f_a, ALL, offset=GUARD)
        right = own(f_b, ALL, offset=GUARD)
        return jnp.concatenate([left.T, right.T], axis=0).astype(BF16)

    def pack(which, channels, first=0):
        if not whole:
            n = share[which]
            half = n // 3
            low = low_lanes(half)
            for k in range(count):
                at = 2 * half * k
                refs["chunk"][k, first : first + 2 * half, :] = k_a[at : at + 2 * half, :]
                pair = jnp.where(low, k_b[at : at + half, :], k_b[at + half : at + 2 * half, :])
                refs["chunk"][k, first + 2 * half : first + n, :] = pair
            return
        step = 288

        def one(i, _):
            at = i * step
            even_a = k_a[pl.ds(2 * at, step, stride=2), :]
            even_b = k_b[pl.ds(2 * at, step, stride=2), :]
            odd_a = swapped(k_a[pl.ds(2 * at + 1, step, stride=2), :])
            odd_b = k_b[pl.ds(2 * at + 1, step, stride=2), :]
            low = low_lanes(step)
            flat[pl.ds(3 * at, step, stride=3), :] = even_a
            flat[pl.ds(3 * at + 1, step, stride=3), :] = jnp.where(low, even_b, odd_a)
            flat[pl.ds(3 * at + 2, step, stride=3), :] = jnp.where(low, odd_a, odd_b)
            return 0

        lax.fori_loop(0, 9 * channels // 2 // step, one, 0)
        n = share[which]
        for k in range(count):
            refs["chunk"][k, first : first + n, :] = flat[k * n : (k + 1) * n, :]

    def hand_over():
        for k in range(count):
            f, m, c, o = devices.coords(k)
            place, side = 0, 0
            if not whole:
                f, m, side, o = devices.apart(devices.coords(k), mine)
                place = (m * lon + o) * far + f
            terms_ref[side, place] = refs["chunk"][k].astype(BF16)

    def field_grad(which, source, first):
        turned = turned_deltas()
        for a, blocks in enumerate((FRINGE, MIDDLE, LAST)):
            lanes = slice(0, 128 * len(blocks))
            product = lax.dot_general(
                turned,
                own(source, lanes, a - 1),
                (((1,), (0,)), ((), ())),
                preferred_element_type=F32,
            )
            product = product * factor
            for j, block in enumerate(blocks):
                left = product[0:128, 128 * j : 128 * j + 128].T
                right = product[128:256, 128 * j : 128 * j + 128].T
                at = 0
                for tap in block:
                    if tap is None:
                        continue
                    lo, hi = tap_rows(tap, tap[2])
                    k_a[lo:hi, :] = left[at : at + hi - lo]
                    k_b[lo:hi, :] = right[at : at + hi - lo]
                    at += hi - lo
        pack(which, mid, first)

    def forward_pass():
        load_kernels()
        win_one, win_two, slope, spread, c_ref = (
            refs[name] for name in ("win_one", "win_two", "slope", "spread", "c")
        )
        clear()

        def convolve_first():
            halo, steps = 4, 2
            start = (ABOVE - halo) * pitch
            total = (rows + 1 + 2 * halo) * pitch + LEFT
            n = -(-total // steps // 16) * 16

            def one(i, _):
                p = pl.multiple_of(start + i * n, 16)
                above = x_ref[pl.ds(pl.multiple_of(p - pitch, 16), n), 384:768]
                here = x_ref[pl.ds(p, n), :]
                value = lax.dot_general(
                    jnp.concatenate([above, here], axis=1),
                    refs["w_one"][...],
                    (((1,), (0,)), ((), ())),
                    preferred_element_type=F32,
                )
                store(p, n, value[:, :128], value[:, 128:], True)
                return 0

            lax.fori_loop(0, steps, one, 0)

        convolve_first()
        windows(win_one, -4, rows + 6)

        def finish_two(p, n, value):
            s = jax.nn.sigmoid(value)
            active = value * s
            slope[pl.ds(p, n), :] = s + active * (1.0 - s)
            store(p, n, active[:, :128], active[:, 128:], True)

        convolve(win_one, refs["w_two"], False, 3, 2, finish_two)
        windows(win_two, -3, rows + 5)

        def finish_three(p, n, value):
            s = jax.nn.sigmoid(value)
            active = value * s
            delta = c_ref[pl.ds(p, n), :].astype(F32) * (s + active * (1.0 - s))
            store(p, n, delta[:, :128], delta[:, 128:], False)
            spread[pl.ds(p, n), :] = active

        convolve(win_two, refs["w_three"], False, 2, 2, finish_three)
        for r in range(rows):
            at = (ABOVE + r) * pitch + LEFT
            refs["features"][r] = spread[at : at + cols, 0:mid].astype(BF16)
        field_grad(2, win_two, share[1])
        windows(win_delta, -2, rows + 4)

        def finish_delta(p, n, value):
            value = value * slope[pl.ds(p, n), :]
            store(p, n, value[:, :128], value[:, 128:], True)

        convolve(win_delta, refs["t_three"], True, 1, 2, finish_delta)
        field_grad(1, win_one, 0)
        hand_over()

    def backward_pass():
        load_turned()
        windows(win_delta, -1, rows + 3, refs["d_a"], refs["d_b"])

        def finish_back(p, n, value):
            store(p, n, value[:, :128], value[:, 128:], True)

        convolve(win_delta, t_two, True, 0, 2, finish_back)
        turned = turned_deltas()
        for a, (step, lanes) in enumerate(((-1, slice(384, 768)), (0, slice(0, 384)), (0, slice(384, 768)))):
            product = lax.dot_general(
                turned,
                own(x_ref, lanes, step),
                (((1,), (0,)), ((), ())),
                preferred_element_type=F32,
            )
            product = product * factor
            lo = 3 * a * chan_in
            k_a[lo : lo + 3 * chan_in, :] = product[0:128].T
            k_b[lo : lo + 3 * chan_in, :] = product[128:256].T
        pack(0, chan_in)
        hand_over()

        low = low_lanes(rows * cols)

        def four(ref):
            return [own(ref, ALL, r, c, GUARD) for r, c in ((0, 0), (0, 1), (1, 0), (1, 1))]

        a, b = four(f_a), four(f_b)
        around = (a[0], a[1], jnp.where(low, b[0], b[1]), a[2], a[3], jnp.where(low, b[2], b[3]))
        around = jnp.concatenate([value.astype(BF16) for value in around], axis=1)
        for r in range(2):
            wide = 384 * (r + 1)
            product = lax.dot_general(
                around[:, :wide],
                t_one[2 * chan_in * r : 2 * chan_in * (r + 1), :wide],
                (((1,), (1,)), ((), ())),
                preferred_element_type=F32,
            )
            for i in range(rows):
                at = i * cols
                base = (2 * i + r) * 2 * cols
                for c in range(2):
                    spread_in = product[at : at + cols, chan_in * c : chan_in * (c + 1)]
                    refs["image"][pl.ds(base + c, cols, stride=2), :] = spread_in
        for i in range(2 * rows):
            refs["grad_input"][i] = refs["image"][2 * cols * i : 2 * cols * (i + 1), :].astype(BF16)

    if second:
        backward_pass()
    else:
        forward_pass()


VMEM = pl.BlockSpec(memory_space=pltpu.VMEM)
ANY = pl.BlockSpec(memory_space=pl.ANY)


def local(inputs, w_first, w_second, w_third, cotangent):
    devices = Slice()
    rows, cols, mid = cotangent.shape
    chan_in = inputs.shape[2]
    factor = 1.0 / LOSS_CELLS
    far, near, core, lon = devices.sizes
    held = (w_first.shape[0], w_second.shape[0], w_third.shape[0])
    shard = jnp.concatenate([w_first, w_second, w_third]).reshape(-1, 128)
    whole = any(n % 384 for n in held)
    if not whole:
        shard = jnp.pad(shard, ((0, -shard.shape[0] % 16), (0, 0)))
    count = 1 if whole else devices.count

    side_rows, corner_rows = strips(2 * rows, rows)[1], strips(CORNER, CORNER)[1]
    south_rows = 2 * cols * (WEST + BEFORE)
    north_rows = 2 * cols * (EAST + AFTER)
    cost = pl.CostEstimate(flops=0, bytes_accessed=3 * 2**20, transcendentals=0)
    params = pltpu.CompilerParams(vmem_limit_bytes=16 * 2**20)

    def buffers(*sizes):
        return [jax.ShapeDtypeStruct((n, 128), BF16) for n in sizes]

    side, south, north = pl.pallas_call(
        functools.partial(pack_sides, rows, cols),
        out_shape=buffers(side_rows, south_rows, north_rows),
        in_specs=[VMEM] * 2,
        out_specs=[VMEM] * 3,
        scratch_shapes=[pltpu.VMEM((2 * rows * CORNER, 128), F32)],
        compiler_params=params,
        cost_estimate=cost,
    )(inputs, cotangent)
    line = lined(devices, shard)
    south, north = lengthways(south, north)
    side = sideways(side, strips(2 * rows, rows)[0][1][0][0])
    lower, upper = pl.pallas_call(
        functools.partial(pack_corners, rows),
        out_shape=buffers(corner_rows, corner_rows),
        in_specs=[VMEM],
        out_specs=[VMEM] * 2,
        compiler_params=params,
        cost_estimate=cost,
    )(side)
    lower, upper = lengthways(lower, upper)
    line, south, north, side = lax.optimization_barrier((line, south, north, side))
    planes = spread(devices, line)
    size = (rows + ABOVE + BELOW) * (cols + LEFT)
    padded, cot = pl.pallas_call(
        functools.partial(prepare, rows, cols),
        out_shape=(
            jax.ShapeDtypeStruct((size, 6 * chan_in), BF16),
            jax.ShapeDtypeStruct((size, 256), BF16),
        ),
        in_specs=[VMEM] * 7,
        out_specs=(VMEM, VMEM),
        scratch_shapes=[
            pltpu.VMEM(((2 * rows + 40) * (2 * cols + 48), 128), F32),
            pltpu.VMEM((size + 2 * GUARD, 128), F32),
        ],
        compiler_params=pltpu.CompilerParams(vmem_limit_bytes=40 * 2**20),
        cost_estimate=pl.CostEstimate(flops=0, bytes_accessed=12 * 2**20, transcendentals=0),
    )(inputs, cotangent, side, south, north, lower, upper)

    planes[1:], padded, cot = lax.optimization_barrier((planes[1:], padded, cot))
    planes, parts = shared_out(devices, planes)
    if whole:
        chunks = jnp.stack(planes).reshape(devices.count, -1)
        chunks = jnp.take(chunks, jnp.argsort(order(devices, -1)), axis=0)
        pieces = jnp.split(chunks, (held[0], held[0] + held[1]), axis=1)
        chunks = jnp.concatenate([piece.reshape(-1) for piece in pieces])
        planes, parts = [chunks.reshape(1, -1, 128)], [(0, 0, 0)]
    deep = -(-(2 * held[1]) // 2048) * 16, -(-held[0] // 2048) * 16
    if whole:
        deep = 2 * held[1] * devices.count // 128, held[0] * devices.count // 128
    sides = 1 if whole else core
    field_shape = (size + 2 * GUARD, 128)
    shape = (rows, cols, chan_in, mid, factor, whole)
    wide = 128 * len(BLOCKS)
    shared = {
        "flat": ((9 * mid * mid // 128, 128), F32),
        "k_a": ((9 * mid, 128), F32),
        "k_b": ((9 * mid, 128), F32),
        "f_a": (field_shape, F32),
        "f_b": (field_shape, F32),
    }

    def call(second, ins, outs, scratch):
        scratch = {**scratch, **{name: kind for name, kind in shared.items() if name not in outs}}
        names = list(ins) + list(outs) + list(scratch)
        results = pl.pallas_call(
            functools.partial(level, shape, devices, parts, second, names),
            out_shape=[jax.ShapeDtypeStruct(*out) for out in outs.values()],
            in_specs=[VMEM] * len(ins),
            out_specs=[VMEM] * len(outs),
            scratch_shapes=[pltpu.VMEM(*kind) for kind in scratch.values()],
            compiler_params=pltpu.CompilerParams(vmem_limit_bytes=40 * 2**20),
            cost_estimate=pl.CostEstimate(
                flops=2 * 10**9 if second else 5 * 10**9,
                bytes_accessed=12 * 2**20,
                transcendentals=10**6,
            ),
        )(*ins.values())
        return dict(zip(outs, results))

    kernels = {("plane", i): plane for i, plane in enumerate(planes)}
    ins = {"x": padded, "c": cot, **kernels}
    done = call(
        False,
        ins,
        {
            "features": ((rows, cols, mid), BF16),
            "terms": ((sides, count // sides, deep[0], 128), BF16),
            "f_a": (field_shape, F32),
            "f_b": (field_shape, F32),
        },
        {
            "chunk": ((count, deep[0], 128), F32),
            "w_one": ((9 * chan_in, 256), BF16),
            "w_two": ((wide, 256), BF16),
            "w_three": ((wide, 256), BF16),
            "t_three": ((256, wide), BF16),
            "slope": ((size, 256), F32),
            "spread": ((size, 256), F32),
            "win_one": ((size, 640), BF16),
            "win_two": ((size, 640), BF16),
            "win_delta": ((size, 640), BF16),
        },
    )
    features = done["features"]

    def reduced(terms, *sizes):
        if whole:
            cuts = [sum(sizes[:i]) * devices.count for i in range(1, len(sizes))]
            pieces = jnp.split(terms.reshape(-1), cuts)
            terms = [piece.reshape(devices.count, -1) for piece in pieces]
            terms = jnp.take(jnp.concatenate(terms, axis=1), order(devices, 1), axis=0)
            terms = terms.reshape(core, devices.count // core, 1, -1)
        return halved(devices, terms)

    upper = reduced(done["terms"], held[1], held[2])
    upper, f_a, f_b = lax.optimization_barrier((upper, done["f_a"], done["f_b"]))
    upper = planar(devices, upper)
    done = call(
        True,
        {"x": padded, "d_a": f_a, "d_b": f_b, **kernels},
        {
            "grad_input": ((2 * rows, 2 * cols, chan_in), BF16),
            "terms": ((sides, count // sides, deep[1], 128), BF16),
        },
        {
            "chunk": ((count, deep[1], 128), F32),
            "t_one": ((4 * chan_in, 768), BF16),
            "t_two": ((256, wide), BF16),
            "win_delta": ((size, 640), BF16),
            "image": ((4 * rows * cols, 128), F32),
        },
    )
    upper, lower = lax.optimization_barrier((upper, reduced(done["terms"], held[0])))
    lower = planar(devices, lower)
    terms = linear(devices, jnp.concatenate([upper, lower], axis=-1 if whole else -2))
    if whole:
        grad_second, grad_third, grad_first = jnp.split(
            total_of(terms).reshape(-1), (held[1], held[1] + held[2])
        )
    else:
        depth = upper.shape[-2]
        high = [n // 128 for n in (held[1], held[2], held[0])]
        sections = ((0, high[0]), (high[0], high[1]), (depth, high[2]))
        deepest = max(high)
        totals = pl.pallas_call(
            functools.partial(unfold, sections, len(terms)),
            out_shape=[jax.ShapeDtypeStruct((n, 128), F32) for n in high],
            in_specs=[VMEM] * len(terms),
            out_specs=[VMEM] * 3,
            scratch_shapes=[
                pltpu.VMEM(terms[0].shape, F32),
                pltpu.VMEM((deepest, 128), F32),
                pltpu.VMEM((deepest, 128), F32),
            ],
            compiler_params=params,
            cost_estimate=pl.CostEstimate(flops=0, bytes_accessed=2**19, transcendentals=0),
        )(*terms)
        grad_second, grad_third, grad_first = (total.reshape(-1) for total in totals)
    return (features, done["grad_input"], grad_first, grad_second, grad_third)


def solution(mesh):
    lat, lon = mesh.shape["lat"], mesh.shape["lon"]
    core = 2 if lat % 2 == 0 else 1
    chips = jax.sharding.Mesh(mesh.devices.reshape(lat // core, core, lon), BOTH)
    tile = P(LAT, "lon", None)
    flat = P(BOTH)
    return jax.shard_map(
        local,
        mesh=chips,
        in_specs=(tile, flat, flat, flat, tile),
        out_specs=(tile, tile, flat, flat, flat),
        check_vma=False,
    )
```
